256 devices in a mesh: gx: 16 (over x, y), gy: 16 (over z, core).
Axes of the slice: x: 4, y: 4, z: 8, core: 2. Of those that a mesh axis runs over, the one named last changes fastest.
Arguments:
- level_set: float32 [512, 1024, 128], P('gx', 'gy'), may hold values from -6 to 6
- stress_jump: float32 [512, 1024, 128], P('gx', 'gy'), may hold values from -6 to 6
- materials: int32 [512, 1024, 128], P('gx', 'gy'), may hold values from 0 to 2
Outputs:
- new_level: float32 [512, 1024, 128], P('gx', 'gy')
- normal_speed: float32 [512, 1024, 128], P('gx', 'gy')
The draws below stay inside these ranges and needn't reach their ends.
Inputs may be any that keep to these rules, and one draw needn't show every extreme that they name: `materials`: 0 marks magnet, 1 iron, 2 air.
All inputs are finite; a program needn't handle non-finite values. Where the reference program divides by a largest or mean magnitude, that divisor is 1e-20 or more.
Results may differ from the reference program's by a relative error of at most 0.0003.
Values sent between devices are 32-bit elements; how exact they have to be, the bound alone decides.
No kernel may reach another device: no remote copies, remote signals or barrier semaphores. Data moves between devices by JAX's collectives and lax.ppermute only.
A program may use at most 64 MiB of HBM per device.

```python
import jax
import jax.numpy as jnp
from jax import lax

SWEEPS = 4
REINIT = 2
NX = 512
NY = 1024
NZ = 128


def plant(drawn, own_key, least, largest):
    index_at = [jax.random.randint(jax.random.fold_in(own_key, axis), (), 0, length) for axis, length in enumerate(drawn.shape)]
    main_axis = drawn.shape.index(max(drawn.shape))
    neighbour = index_at[:main_axis] + [(index_at[main_axis] + 1) % drawn.shape[main_axis]] + index_at[main_axis + 1:]
    return drawn.at[tuple(index_at)].set(least).at[tuple(neighbour)].set(largest)


def block_levels(rng, dims, cuts, low, largest):
    def one(position, blocks):
        steps = jax.random.uniform(jax.random.fold_in(jax.random.fold_in(rng, 6), position), (blocks,), jnp.float32, low / len(cuts), largest / len(cuts))
        return jnp.repeat(jnp.exp(steps), dims[position] // blocks).reshape((-1,) + (1,) * (len(dims) - position - 1))

    loudness = one(*cuts[0])
    for cut in cuts[1:]:
        loudness = loudness * one(*cut)
    return loudness


def noise(key, dims, deviation, limit, cuts=(), dtype=jnp.bfloat16):
    entries = deviation * jax.random.normal(key, dims, jnp.float32)
    if cuts:
        entries = entries * block_levels(key, dims, cuts, -0.22, 0.18)
    return jnp.clip(entries, -limit, limit).astype(dtype)


def setup_inputs(seed: int = 0) -> dict:
    arg_keys = jax.random.split(jax.random.key(seed), 4)
    return {
        "level_set": noise(arg_keys[0], (NX, NY, NZ), 1.0, 6.0, ((0, 16), (1, 16)), jnp.float32),
        "stress_jump": noise(arg_keys[1], (NX, NY, NZ), 1.0, 6.0, ((0, 16), (1, 16)), jnp.float32),
        "materials": plant(jax.random.randint(arg_keys[2], (NX, NY, NZ), 0, 3), jax.random.fold_in(arg_keys[2], 1), 0, 2).astype(jnp.int32),
    }


screening = 0.1
spectral_mid = screening + 6.0
spectral_half = 6.0
courant = 0.25
pseudo_step = 0.25
weno_floor = 1e-06

def material_weight(materials):
    return jnp.where(materials == 0, 1.0, jnp.where(materials == 1, 0.6, 0.0)).astype(jnp.float32)

def periodic_pad(field, along, margin):
    extent = field.shape[along]
    leading = lax.slice_in_dim(field, extent - margin, extent, axis=along)
    trailing = lax.slice_in_dim(field, 0, margin, axis=along)
    return jnp.concatenate([leading, field, trailing], axis=along)

def square_of(value):
    return value * value

def weno_side(stencil_a, stencil_b, stencil_c, stencil_d, stencil_e):
    smooth_a = 13.0 / 12.0 * square_of(stencil_a - 2.0 * stencil_b + stencil_c) + 0.25 * square_of(stencil_a - 4.0 * stencil_b + 3.0 * stencil_c)
    smooth_b = 13.0 / 12.0 * square_of(stencil_b - 2.0 * stencil_c + stencil_d) + 0.25 * square_of(stencil_b - stencil_d)
    smooth_c = 13.0 / 12.0 * square_of(stencil_c - 2.0 * stencil_d + stencil_e) + 0.25 * square_of(3.0 * stencil_c - 4.0 * stencil_d + stencil_e)
    weight_a = 0.1 / square_of(weno_floor + smooth_a)
    weight_b = 0.6 / square_of(weno_floor + smooth_b)
    weight_c = 0.3 / square_of(weno_floor + smooth_c)
    weight_sum = weight_a + weight_b + weight_c
    combined = weight_a * (stencil_a / 3.0 - 7.0 * stencil_b / 6.0 + 11.0 * stencil_c / 6.0)
    combined = combined + weight_b * (-stencil_b / 6.0 + 5.0 * stencil_c / 6.0 + stencil_d / 3.0)
    combined = combined + weight_c * (stencil_c / 3.0 + 5.0 * stencil_d / 6.0 - stencil_e / 6.0)
    return combined / weight_sum

def weno_pair(padded, along, extent):
    length = padded.shape[along]
    differences = lax.slice_in_dim(padded, 1, length, axis=along) - lax.slice_in_dim(padded, 0, length - 1, axis=along)
    pieces = [lax.slice_in_dim(differences, k, k + extent, axis=along) for k in range(6)]
    left_side = weno_side(pieces[0], pieces[1], pieces[2], pieces[3], pieces[4])
    right_side = weno_side(pieces[5], pieces[4], pieces[3], pieces[2], pieces[1])
    return (left_side, right_side)

def godunov_square(left_side, right_side, positive):
    upper = jnp.maximum(square_of(jnp.maximum(left_side, 0.0)), square_of(jnp.minimum(right_side, 0.0)))
    lower = jnp.maximum(square_of(jnp.minimum(left_side, 0.0)), square_of(jnp.maximum(right_side, 0.0)))
    return jnp.where(positive, upper, lower)

def apply_periodic(field):
    beside = jnp.roll(field, -1, 0) + jnp.roll(field, 1, 0)
    beside = beside + jnp.roll(field, -1, 1) + jnp.roll(field, 1, 1)
    beside = beside + jnp.roll(field, 1, 2) + jnp.roll(field, -1, 2)
    return spectral_mid * field - beside

def advect_rate(level, velocity):
    positive = velocity > 0
    total = jnp.zeros_like(level)
    for along in range(3):
        left_side, right_side = weno_pair(periodic_pad(level, along, 3), along, level.shape[along])
        total = total + godunov_square(left_side, right_side, positive)
    return -velocity * jnp.sqrt(total)

def reinit_sweep(level, sign_field):
    positive = sign_field > 0
    total = jnp.zeros_like(level)
    for along in range(3):
        left_side = level - jnp.roll(level, 1, along)
        right_side = jnp.roll(level, -1, along) - level
        total = total + godunov_square(left_side, right_side, positive)
    return level - pseudo_step * sign_field * (jnp.sqrt(total) - 1.0)

def reference(level_set, stress_jump, materials):
    source = material_weight(materials) * stress_jump
    iterate = jnp.zeros_like(source)
    residue = source
    search = source / spectral_mid
    ratio_now = spectral_half / spectral_mid
    for k in range(SWEEPS):
        applied = apply_periodic(search)
        iterate = iterate + search
        residue = residue - applied
        ratio_next = 1.0 / (2.0 * spectral_mid / spectral_half - ratio_now)
        search = ratio_next * ratio_now * search + 2.0 * ratio_next / spectral_half * residue
        ratio_now = ratio_next
    normal_speed = iterate + search
    peak_speed = jnp.max(jnp.abs(normal_speed))
    time_step = courant / (peak_speed + 1e-06)
    section_one = level_set + time_step * advect_rate(level_set, normal_speed)
    advected = 0.5 * level_set + 0.5 * (section_one + time_step * advect_rate(section_one, normal_speed))
    sign_field = advected / jnp.sqrt(advected * advected + 1.0)
    new_level = advected
    for k in range(REINIT):
        new_level = reinit_sweep(new_level, sign_field)
    return (new_level, normal_speed)
```

```python
import jax
import jax.numpy as jnp
import numpy as np
from jax import lax
from jax.experimental import pallas as pl
from jax.experimental.pallas import tpu as pltpu
from jax.sharding import PartitionSpec as P

SWEEPS = 4
REINIT = 2

screening = 0.1
spectral_mid = screening + 6.0
spectral_half = 6.0
courant = 0.25
pseudo_step = 0.25
weno_floor = 1e-06

OWN = 16
ROWS = 96
SRC = 9
LEV = 8
SPD = 5


def velocity_polynomial():
    times = np.array([0.0, 1.0])
    add = np.polynomial.polynomial.polyadd
    mul = np.polynomial.polynomial.polymul
    operator = add([spectral_mid], -times)
    ratio_now = spectral_half / spectral_mid
    iterate, residue, search = np.array([0.0]), np.array([1.0]), np.array([1.0 / spectral_mid])
    for _ in range(SWEEPS):
        applied = mul(operator, search)
        iterate = add(iterate, search)
        residue = add(residue, -applied)
        ratio_next = 1.0 / (2.0 * spectral_mid / spectral_half - ratio_now)
        search = add(ratio_next * ratio_now * search, 2.0 * ratio_next / spectral_half * residue)
        ratio_now = ratio_next
    return [float(c) for c in add(iterate, search)]


def along_lanes(value, k):
    return pltpu.roll(value, (-k) % value.shape[1], axis=1)


def inverse(x):
    r = pl.reciprocal(x, approx=True)
    return r * (2.0 - x * r)


def smooth_terms(second, second_next, third, scaled, scaled_next):
    twice = third + third
    middle = (third * twice + (1.5 * weno_floor)) + scaled * second_next
    return middle + scaled_next * twice, middle, middle - scaled * twice


def side_ratios(u1, u2, u3, jump_near, jump_far):
    p12 = jnp.square(u1 * u2)
    p13 = jnp.square(u1 * u3)
    p23 = jnp.square(u2 * u3)
    a = p12 * jump_near
    b = p23 * jump_far
    both = a + b
    both = both + both
    base = 3.0 * p13 + 0.5 * (p12 + p23)
    return (both + a) * inverse(base + p12), (both + b) * inverse(base + p23)


def weno_line(f, count):
    values, first, second, third, scaled, terms, jump, ratios = ({} for _ in range(8))

    def need(table, j, make):
        if j not in table:
            table[j] = make(j)
        return table[j]

    def val(j):
        return need(values, j, f)

    def d1(j):
        return need(first, j, lambda k: val(k + 1) - val(k))

    def d2(j):
        return need(second, j, lambda k: d1(k) - d1(k - 1))

    def d3(j):
        return need(third, j, lambda k: d2(k + 1) - d2(k))

    def sc(j):
        return need(scaled, j, lambda k: 1.5 * d2(k))

    def u(j):
        return need(terms, j, lambda k: smooth_terms(d2(k), d2(k + 1), d3(k), sc(k), sc(k + 1)))

    def g(j):
        return need(jump, j, lambda k: d3(k + 1) - d3(k))

    def r(c):
        return need(
            ratios, c, lambda k: side_ratios(u(k - 2)[0], u(k - 1)[1], u(k)[2], g(k - 1), g(k - 2))
        )

    for i in range(count):
        wide = 6.0 * (d1(i) + d1(i - 1))
        left = (wide - (d3(i - 1) + d3(i - 1))) - r(i)[0]
        right = ((d3(i) + d3(i)) - wide) - r(i + 1)[1]
        yield i, left, right


def weno_lanes(f):
    ahead = along_lanes(f, 1) - f
    behind = along_lanes(ahead, -1)
    second = ahead - behind
    second_next = along_lanes(second, 1)
    third = second_next - second
    u1, u2, u3 = smooth_terms(second, second_next, third, 1.5 * second, 1.5 * second_next)
    third_back = along_lanes(third, -1)
    near = third - third_back
    far = along_lanes(near, -1)
    ratio_left, ratio_right = side_ratios(
        along_lanes(u1, -2), along_lanes(u2, -1), u3, near, far
    )
    wide = 6.0 * (ahead + behind)
    left = (wide - (third_back + third_back)) - ratio_left
    right = ((third + third) - wide) - along_lanes(ratio_right, 1)
    return left, right


def upwind_square(left, right, sign):
    return jnp.square(jnp.maximum(jnp.maximum(sign * left, sign * right), 0.0))


def sign_of(value):
    return jnp.where(value > 0, 1.0, -1.0)


def strided(ref, x, start, step):
    return ref[x, pl.ds(start, 8, stride=step), :]


def weno_rates(field, fx, speed, sx, acc, planes, start, step, emit):
    def along_x(t, _):
        row = start + t

        def f(j):
            return strided(field, fx + j, row, step)

        for i, left, right in weno_line(f, planes):
            sign = sign_of(strided(speed, sx + i, row, step))
            acc[i, t] = upwind_square(left, right, sign)
        return _

    lax.fori_loop(0, step, along_x, 0)

    def along_yz(x, _):
        lines = {}

        def f(j):
            if j not in lines:
                lines[j] = strided(field, fx + x, start + j, step)
            return lines[j]

        for t, left, right in weno_line(f, step):
            velocity = strided(speed, sx + x, start + t, step)
            sign = sign_of(velocity)
            total = acc[x, t] + upwind_square(left, right, sign)
            left, right = weno_lanes(f(t))
            total = total + upwind_square(left, right, sign)
            emit(x, t, velocity * (jnp.sqrt(total) * (-1.0 / 12.0)))
        return _

    lax.fori_loop(0, planes, along_yz, 0)


def reinit_sweep(field, fx, origin, ox, planes, start, step, emit):
    def body(x, _):
        lines = {}

        def f(j):
            if j not in lines:
                lines[j] = strided(field, fx + x, start + j, step)
            return lines[j]

        for t in range(step):
            row = start + t
            centre = f(t)
            base = strided(origin, ox + x, row, step)
            sign_field = base / jnp.sqrt(base * base + 1.0)
            sign = sign_of(sign_field)
            total = upwind_square(
                centre - strided(field, fx + x - 1, row, step),
                centre - strided(field, fx + x + 1, row, step),
                sign,
            )
            total = total + upwind_square(centre - f(t - 1), centre - f(t + 1), sign)
            total = total + upwind_square(
                centre - along_lanes(centre, -1), centre - along_lanes(centre, 1), sign
            )
            emit(x, t, centre - pseudo_step * sign_field * (jnp.sqrt(total) - 1.0))
        return _

    lax.fori_loop(0, planes, body, 0)


def pack_x(level, stress, materials, source, low, high):
    nx, ny, _ = level.shape

    def weigh(x, _):
        label = materials[x]
        weight = jnp.where(label == 0, 1.0, jnp.where(label == 1, 0.6, 0.0)).astype(jnp.float32)
        source[x] = weight * stress[x]
        return _

    lax.fori_loop(0, nx, weigh, 0)
    for k in range(SRC):
        low[pl.ds(k * ny, ny), :] = source[k]
        high[pl.ds(k * ny, ny), :] = source[nx - SRC + k]
    for k in range(LEV):
        low[pl.ds((SRC + k) * ny, ny), :] = level[k]
        high[pl.ds((SRC + k) * ny, ny), :] = level[nx - LEV + k]


def pack_y(level, source, before, after, low, high):
    nx, ny, _ = level.shape
    wide = nx + 2 * SRC
    tall = nx + 2 * LEV
    extra = tall * 8 + wide * 8

    def put_level(k, piece_low, piece_high):
        low[pl.ds(k * 8, 8), :] = piece_low
        high[pl.ds(k * 8, 8), :] = piece_high

    def put_source(k, piece_low, row_low, piece_high, row_high):
        low[pl.ds((tall + k) * 8, 8), :] = piece_low
        high[pl.ds((tall + k) * 8, 8), :] = piece_high
        low[pl.ds(extra + k, 1), :] = row_low
        high[pl.ds(extra + k, 1), :] = row_high

    for k in range(nx):
        put_level(LEV + k, level[k, 0:8], level[k, ny - 8 : ny])
        put_source(
            SRC + k,
            source[k, 0:8],
            source[k, 8:9],
            source[k, ny - 8 : ny],
            source[k, ny - 9 : ny - 8],
        )
    for ref, at in ((before, 0), (after, 1)):
        for k in range(SRC):
            b = k * ny
            put_source(
                k + at * (SRC + nx),
                ref[b : b + 8],
                ref[b + 8 : b + 9],
                ref[b + ny - 8 : b + ny],
                ref[b + ny - 9 : b + ny - 8],
            )
        for k in range(LEV):
            b = (SRC + k) * ny
            put_level(k + at * (LEV + nx), ref[b : b + 8], ref[b + ny - 8 : b + ny])
    low[pl.ds(extra + wide, 8 - wide % 8), :] = jnp.zeros((8 - wide % 8, 128), jnp.float32)
    high[pl.ds(extra + wide, 8 - wide % 8), :] = jnp.zeros((8 - wide % 8, 128), jnp.float32)


def extend(level, source, before, after, below, above, level_out, source_out):
    nx, ny, _ = level.shape
    wide = nx + 2 * SRC
    tall = nx + 2 * LEV
    extra = tall * 8 + wide * 8
    top = OWN + ny
    for k in range(nx):
        level_out[LEV + k, OWN:top] = level[k]
        source_out[SRC + k, OWN:top] = source[k]
    for ref, at in ((before, 0), (after, 1)):
        for k in range(SRC):
            source_out[k + at * (SRC + nx), OWN:top] = ref[k * ny : (k + 1) * ny]
        for k in range(LEV):
            b = (SRC + k) * ny
            level_out[k + at * (LEV + nx), OWN:top] = ref[b : b + ny]
    for k in range(tall):
        level_out[k, OWN - 8 : OWN] = below[k * 8 : k * 8 + 8]
        level_out[k, top : top + 8] = above[k * 8 : k * 8 + 8]
    for k in range(wide):
        b = (tall + k) * 8
        source_out[k, OWN - 8 : OWN] = below[b : b + 8]
        source_out[k, top : top + 8] = above[b : b + 8]
        source_out[k, OWN - 9 : OWN - 8] = below[extra + k : extra + k + 1]
        source_out[k, top + 8 : top + 9] = above[extra + k : extra + k + 1]


def velocity(
    level, source, before, after, below, above, level_out, speed, own_speed, peaks, src, one, two
):
    extend(level, source, before, after, below, above, level_out, src)
    nx, ny, _ = level.shape
    wide = nx + 2 * SRC
    coefficients = velocity_polynomial()
    step = (ny + 2 * (SRC - 1)) // 8
    start = OWN - (SRC - 1)

    def sweep(old, new, shift, lo, hi, last, constant):
        def body(x, _):
            lines = {}

            def f(j):
                if j not in lines:
                    lines[j] = strided(old, x, start + j, step)
                return lines[j]

            for t in range(step):
                centre = f(t)
                beside = strided(old, x - 1, start + t, step) + strided(old, x + 1, start + t, step)
                beside = beside + (f(t - 1) + f(t + 1))
                beside = beside + (along_lanes(centre, 1) + along_lanes(centre, -1))
                if last is not None:
                    beside = last * beside
                own = centre if old is src else strided(src, x, start + t, step)
                new[x - shift, pl.ds(start + t, 8, stride=step), :] = beside + constant * own
            return _

        lax.fori_loop(lo, hi, body, 0)

    sweep(src, one, 0, 1, wide - 1, coefficients[4], coefficients[3])
    sweep(one, two, 0, 2, wide - 2, None, coefficients[2])
    sweep(two, one, 0, 3, wide - 3, None, coefficients[1])
    sweep(one, speed, SRC - SPD, 4, wide - 4, None, coefficients[0])

    def largest(x, carry):
        mine = speed[SPD + x, OWN : OWN + ny]
        own_speed[x] = mine
        return jnp.maximum(carry, jnp.abs(mine))

    top = lax.fori_loop(0, nx, largest, jnp.zeros((ny, 128), jnp.float32))
    peaks[...] = jnp.broadcast_to(jnp.max(top), peaks.shape)


def first_stage(level, speed, rate, acc):
    planes = rate.shape[0]
    step = 10
    start = OWN - SPD

    def emit(x, t, value):
        rate[x, pl.ds(start + t, 8, stride=step), :] = value

    weno_rates(level, LEV - SPD, speed, 0, acc, planes, start, step, emit)


def second_stage(level, speed, rate, peaks, new_level, stage, advected, swept, acc):
    nx, ny, _ = new_level.shape
    peak = jnp.max(peaks[...], axis=0, keepdims=True)
    time_step = courant / (peak + 1e-06)
    step_row = jnp.broadcast_to(time_step, (8, 128))
    step_rows = jnp.broadcast_to(time_step, (ROWS - 8, 128))

    def advance(x, _):
        stage[x, 8:ROWS] = level[x + LEV - SPD, 8:ROWS] + step_rows * rate[x, 8:ROWS]
        return _

    lax.fori_loop(0, stage.shape[0], advance, 0)

    start, step = OWN - 2, 9

    def emit(x, t, value):
        row = start + t
        after = strided(stage, x + SPD - 2, row, step) + step_row * value
        before = strided(level, x + LEV - 2, row, step)
        advected[x, pl.ds(row, 8, stride=step), :] = 0.5 * before + 0.5 * after

    weno_rates(stage, SPD - 2, speed, SPD - 2, acc, nx + 4, start, step, emit)

    def emit_one(x, t, value):
        swept[x, pl.ds(OWN - 1 + t, 8, stride=9), :] = value

    reinit_sweep(advected, 1, advected, 1, nx + 2, OWN - 1, 9, emit_one)

    def emit_two(x, t, value):
        new_level[x, pl.ds(t, 8, stride=ny // 8), :] = value

    reinit_sweep(swept, 1, advected, 2, nx, OWN, ny // 8, emit_two)


VM = pl.BlockSpec(memory_space=pltpu.VMEM)


def call(kernel, outs, scratch, args):
    return pl.pallas_call(
        kernel,
        out_shape=[jax.ShapeDtypeStruct(s, jnp.float32) for s in outs],
        in_specs=[VM] * len(args),
        out_specs=[VM] * len(outs),
        scratch_shapes=[pltpu.VMEM(s, jnp.float32) for s in scratch],
        compiler_params=pltpu.CompilerParams(vmem_limit_bytes=40 * 1024 * 1024),
    )(*args)


def local(level_set, stress_jump, materials):
    nx, ny, nz = level_set.shape
    wide, tall, mid = nx + 2 * SRC, nx + 2 * LEV, nx + 2 * SPD
    size_x, size_y = lax.axis_size("gx"), lax.axis_size("gy")

    def shift(value, axis, size, by):
        return lax.ppermute(value, axis, [(i, (i + by) % size) for i in range(size)])

    message = ((SRC + LEV) * ny, nz)
    source, low, high = call(
        pack_x, [(nx, ny, nz), message, message], [], (level_set, stress_jump, materials)
    )
    after = shift(low, "gx", size_x, -1)
    before = shift(high, "gx", size_x, 1)
    message = (tall * 8 + wide * 8 + (wide + 7) // 8 * 8, nz)
    low, high = call(pack_y, [message, message], [], (level_set, source, before, after))
    above = shift(low, "gy", size_y, -1)
    below = shift(high, "gy", size_y, 1)
    devices = size_x * size_y
    level, speed, normal_speed, peaks = call(
        velocity,
        [(tall, ROWS, nz), (mid, ROWS, nz), (nx, ny, nz), (devices, nz)],
        [(wide, ROWS, nz)] * 3,
        (level_set, source, before, after, below, above),
    )
    peaks = lax.all_to_all(peaks.reshape(devices, 1, nz), ("gx", "gy"), 0, 0)
    peaks = peaks.reshape(devices, nz)
    (rate,) = call(first_stage, [(mid, ROWS, nz)], [(mid, 10, 8, nz)], (level, speed))
    (new_level,) = call(
        second_stage,
        [(nx, ny, nz)],
        [(mid, ROWS, nz), (nx + 4, ROWS, nz), (nx + 2, ROWS, nz), (nx + 4, 9, 8, nz)],
        (level, speed, rate, peaks),
    )
    return (new_level, normal_speed)


def solution(mesh):
    in_specs = (P("gx", "gy", None), P("gx", "gy", None), P("gx", "gy", None))
    out_specs = (P("gx", "gy", None), P("gx", "gy", None))
    return jax.shard_map(local, mesh=mesh, in_specs=in_specs, out_specs=out_specs, check_vma=False)
```

```python
import jax
import jax.numpy as jnp
import numpy as np
from jax import lax
from jax.experimental import pallas as pl
from jax.experimental.pallas import tpu as pltpu
from jax.sharding import PartitionSpec as P

SWEEPS = 4
REINIT = 2

screening = 0.1
spectral_mid = screening + 6.0
spectral_half = 6.0
courant = 0.25
pseudo_step = 0.25
weno_floor = 1e-06

OWN = 16
ROWS = 96
SRC = 9
LEV = 8
SPD = 5


def velocity_polynomial():
    times = np.array([0.0, 1.0])
    add = np.polynomial.polynomial.polyadd
    mul = np.polynomial.polynomial.polymul
    operator = add([spectral_mid], -times)
    ratio_now = spectral_half / spectral_mid
    iterate, residue, search = np.array([0.0]), np.array([1.0]), np.array([1.0 / spectral_mid])
    for _ in range(SWEEPS):
        applied = mul(operator, search)
        iterate = add(iterate, search)
        residue = add(residue, -applied)
        ratio_next = 1.0 / (2.0 * spectral_mid / spectral_half - ratio_now)
        search = add(ratio_next * ratio_now * search, 2.0 * ratio_next / spectral_half * residue)
        ratio_now = ratio_next
    return [float(c) for c in add(iterate, search)]


def along_lanes(value, k):
    return pltpu.roll(value, (-k) % value.shape[1], axis=1)


def inverse(x):
    return pl.reciprocal(x, approx=True)


def root(x):
    return x * lax.rsqrt(jnp.maximum(x, 1.2e-38))


def smooth_terms(second, second_next, third, scaled, scaled_next):
    twice = third + third
    middle = (third * twice + (1.5 * weno_floor)) + scaled * second_next
    return middle + scaled_next * twice, middle, middle - scaled * twice


def side_ratios(u1, u2, u3, jump_near, jump_far):
    p12 = jnp.square(u1 * u2)
    p13 = jnp.square(u1 * u3)
    p23 = jnp.square(u2 * u3)
    a = p12 * jump_near
    b = p23 * jump_far
    both = a + b
    both = both + both
    base = 3.0 * p13 + 0.5 * (p12 + p23)
    return (both + a) * inverse(base + p12), (both + b) * inverse(base + p23)


def weno_line(f, count):
    values, first, second, third, scaled, terms, jump, ratios = ({} for _ in range(8))

    def need(table, j, make):
        if j not in table:
            table[j] = make(j)
        return table[j]

    def val(j):
        return need(values, j, f)

    def d1(j):
        return need(first, j, lambda k: val(k + 1) - val(k))

    def d2(j):
        return need(second, j, lambda k: d1(k) - d1(k - 1))

    def d3(j):
        return need(third, j, lambda k: d2(k + 1) - d2(k))

    def sc(j):
        return need(scaled, j, lambda k: 1.5 * d2(k))

    def u(j):
        return need(terms, j, lambda k: smooth_terms(d2(k), d2(k + 1), d3(k), sc(k), sc(k + 1)))

    def g(j):
        return need(jump, j, lambda k: d3(k + 1) - d3(k))

    def r(c):
        return need(
            ratios, c, lambda k: side_ratios(u(k - 2)[0], u(k - 1)[1], u(k)[2], g(k - 1), g(k - 2))
        )

    for i in range(count):
        wide = 6.0 * (d1(i) + d1(i - 1))
        left = (wide - (d3(i - 1) + d3(i - 1))) - r(i)[0]
        right = ((d3(i) + d3(i)) - wide) - r(i + 1)[1]
        yield i, left, right


def weno_lanes(f):
    shifted = {k: along_lanes(f, k) if k else f for k in range(-3, 4)}
    ((_, left, right),) = weno_line(lambda j: shifted[j], 1)
    return left, right


def upwind_square(left, right, sign):
    return jnp.square(jnp.maximum(jnp.maximum(sign * left, sign * right), 0.0))


def sign_of(value):
    return jnp.where(value > 0, 1.0, -1.0)


def strided(ref, x, start, step):
    return ref[x, pl.ds(start, 8, stride=step), :]


def weno_rates(field, fx, speed, sx, acc, planes, start, step, emit):
    def along_x(t, _):
        row = start + t

        def f(j):
            return strided(field, fx + j, row, step)

        for i, left, right in weno_line(f, planes):
            sign = sign_of(strided(speed, sx + i, row, step))
            acc[i, t] = upwind_square(left, right, sign)
        return _

    lax.fori_loop(0, step, along_x, 0)

    def along_yz(x, _):
        lines = {}

        def f(j):
            if j not in lines:
                lines[j] = strided(field, fx + x, start + j, step)
            return lines[j]

        for t, left, right in weno_line(f, step):
            velocity = strided(speed, sx + x, start + t, step)
            sign = sign_of(velocity)
            total = acc[x, t] + upwind_square(left, right, sign)
            left, right = weno_lanes(f(t))
            total = total + upwind_square(left, right, sign)
            emit(x, t, velocity * (root(total) * (-1.0 / 12.0)))
        return _

    lax.fori_loop(0, planes, along_yz, 0, unroll=2)


def reinit_sweep(field, fx, origin, ox, planes, start, step, emit):
    def body(x, _):
        lines = {}

        def f(j):
            if j not in lines:
                lines[j] = strided(field, fx + x, start + j, step)
            return lines[j]

        for t in range(step):
            row = start + t
            centre = f(t)
            base = strided(origin, ox + x, row, step)
            sign_field = base * lax.rsqrt(base * base + 1.0)
            sign = sign_of(sign_field)
            total = upwind_square(
                centre - strided(field, fx + x - 1, row, step),
                centre - strided(field, fx + x + 1, row, step),
                sign,
            )
            total = total + upwind_square(centre - f(t - 1), centre - f(t + 1), sign)
            total = total + upwind_square(
                centre - along_lanes(centre, -1), centre - along_lanes(centre, 1), sign
            )
            emit(x, t, centre - pseudo_step * sign_field * (root(total) - 1.0))
        return _

    lax.fori_loop(0, planes, body, 0, unroll=2)


def pack_x(level, stress, materials, source, low, high):
    nx, ny, _ = level.shape

    def weigh(x, _):
        label = materials[x]
        weight = jnp.where(label == 0, 1.0, jnp.where(label == 1, 0.6, 0.0)).astype(jnp.float32)
        source[x] = weight * stress[x]
        return _

    lax.fori_loop(0, nx, weigh, 0)
    for k in range(SRC):
        low[pl.ds(k * ny, ny), :] = source[k]
        high[pl.ds(k * ny, ny), :] = source[nx - SRC + k]
    for k in range(LEV):
        low[pl.ds((SRC + k) * ny, ny), :] = level[k]
        high[pl.ds((SRC + k) * ny, ny), :] = level[nx - LEV + k]


def pack_y(level, source, before, after, low, high):
    nx, ny, _ = level.shape
    wide = nx + 2 * SRC
    tall = nx + 2 * LEV
    extra = tall * 8 + wide * 8

    def put_level(k, piece_low, piece_high):
        low[pl.ds(k * 8, 8), :] = piece_low
        high[pl.ds(k * 8, 8), :] = piece_high

    def put_source(k, piece_low, row_low, piece_high, row_high):
        low[pl.ds((tall + k) * 8, 8), :] = piece_low
        high[pl.ds((tall + k) * 8, 8), :] = piece_high
        low[pl.ds(extra + k, 1), :] = row_low
        high[pl.ds(extra + k, 1), :] = row_high

    for k in range(nx):
        put_level(LEV + k, level[k, 0:8], level[k, ny - 8 : ny])
        put_source(
            SRC + k,
            source[k, 0:8],
            source[k, 8:9],
            source[k, ny - 8 : ny],
            source[k, ny - 9 : ny - 8],
        )
    for ref, at in ((before, 0), (after, 1)):
        for k in range(SRC):
            b = k * ny
            put_source(
                k + at * (SRC + nx),
                ref[b : b + 8],
                ref[b + 8 : b + 9],
                ref[b + ny - 8 : b + ny],
                ref[b + ny - 9 : b + ny - 8],
            )
        for k in range(LEV):
            b = (SRC + k) * ny
            put_level(k + at * (LEV + nx), ref[b : b + 8], ref[b + ny - 8 : b + ny])
    low[pl.ds(extra + wide, 8 - wide % 8), :] = jnp.zeros((8 - wide % 8, 128), jnp.float32)
    high[pl.ds(extra + wide, 8 - wide % 8), :] = jnp.zeros((8 - wide % 8, 128), jnp.float32)


def extend(level, source, before, after, below, above, level_out, source_out):
    nx, ny, _ = level.shape
    wide = nx + 2 * SRC
    tall = nx + 2 * LEV
    extra = tall * 8 + wide * 8
    top = OWN + ny
    for k in range(nx):
        level_out[LEV + k, OWN:top] = level[k]
        source_out[SRC + k, OWN:top] = source[k]
    for ref, at in ((before, 0), (after, 1)):
        for k in range(SRC):
            source_out[k + at * (SRC + nx), OWN:top] = ref[k * ny : (k + 1) * ny]
        for k in range(LEV):
            b = (SRC + k) * ny
            level_out[k + at * (LEV + nx), OWN:top] = ref[b : b + ny]
    for k in range(tall):
        level_out[k, OWN - 8 : OWN] = below[k * 8 : k * 8 + 8]
        level_out[k, top : top + 8] = above[k * 8 : k * 8 + 8]
    for k in range(wide):
        b = (tall + k) * 8
        source_out[k, OWN - 8 : OWN] = below[b : b + 8]
        source_out[k, top : top + 8] = above[b : b + 8]
        source_out[k, OWN - 9 : OWN - 8] = below[extra + k : extra + k + 1]
        source_out[k, top + 8 : top + 9] = above[extra + k : extra + k + 1]


def velocity(
    level, source, before, after, below, above, level_out, speed, own_speed, peaks, src, one, two
):
    extend(level, source, before, after, below, above, level_out, src)
    nx, ny, _ = level.shape
    wide = nx + 2 * SRC
    coefficients = velocity_polynomial()
    step = (ny + 2 * (SRC - 1)) // 8
    start = OWN - (SRC - 1)

    def sweep(old, new, shift, lo, hi, last, constant):
        def body(x, _):
            lines = {}

            def f(j):
                if j not in lines:
                    lines[j] = strided(old, x, start + j, step)
                return lines[j]

            for t in range(step):
                centre = f(t)
                beside = strided(old, x - 1, start + t, step) + strided(old, x + 1, start + t, step)
                beside = beside + (f(t - 1) + f(t + 1))
                beside = beside + (along_lanes(centre, 1) + along_lanes(centre, -1))
                if last is not None:
                    beside = last * beside
                own = centre if old is src else strided(src, x, start + t, step)
                new[x - shift, pl.ds(start + t, 8, stride=step), :] = beside + constant * own
            return _

        lax.fori_loop(lo, hi, body, 0, unroll=4)

    sweep(src, one, 0, 1, wide - 1, coefficients[4], coefficients[3])
    sweep(one, two, 0, 2, wide - 2, None, coefficients[2])
    sweep(two, one, 0, 3, wide - 3, None, coefficients[1])
    sweep(one, speed, SRC - SPD, 4, wide - 4, None, coefficients[0])

    def largest(x, carry):
        mine = speed[SPD + x, OWN : OWN + ny]
        own_speed[x] = mine
        return jnp.maximum(carry, jnp.abs(mine))

    top = lax.fori_loop(0, nx, largest, jnp.zeros((ny, 128), jnp.float32))
    peaks[...] = jnp.broadcast_to(jnp.max(top), peaks.shape)


def first_stage(level, speed, rate, acc):
    planes = rate.shape[0]
    step = 10
    start = OWN - SPD

    def emit(x, t, value):
        rate[x, pl.ds(start + t, 8, stride=step), :] = value

    weno_rates(level, LEV - SPD, speed, 0, acc, planes, start, step, emit)


def second_stage(level, speed, rate, peaks, new_level, stage, advected, swept, acc):
    nx, ny, _ = new_level.shape
    peak = jnp.max(peaks[...], axis=0, keepdims=True)
    time_step = courant / (peak + 1e-06)
    step_row = jnp.broadcast_to(time_step, (8, 128))
    step_rows = jnp.broadcast_to(time_step, (ROWS - 8, 128))

    def advance(x, _):
        stage[x, 8:ROWS] = level[x + LEV - SPD, 8:ROWS] + step_rows * rate[x, 8:ROWS]
        return _

    lax.fori_loop(0, stage.shape[0], advance, 0)

    start, step = OWN - 2, 9

    def emit(x, t, value):
        row = start + t
        after = strided(stage, x + SPD - 2, row, step) + step_row * value
        before = strided(level, x + LEV - 2, row, step)
        advected[x, pl.ds(row, 8, stride=step), :] = 0.5 * before + 0.5 * after

    weno_rates(stage, SPD - 2, speed, SPD - 2, acc, nx + 4, start, step, emit)

    def emit_one(x, t, value):
        swept[x, pl.ds(OWN - 1 + t, 8, stride=9), :] = value

    reinit_sweep(advected, 1, advected, 1, nx + 2, OWN - 1, 9, emit_one)

    def emit_two(x, t, value):
        new_level[x, pl.ds(t, 8, stride=ny // 8), :] = value

    reinit_sweep(swept, 1, advected, 2, nx, OWN, ny // 8, emit_two)


VM = pl.BlockSpec(memory_space=pltpu.VMEM)


def call(kernel, outs, scratch, args, megabytes=18):
    return pl.pallas_call(
        kernel,
        out_shape=[jax.ShapeDtypeStruct(s, jnp.float32) for s in outs],
        in_specs=[VM] * len(args),
        out_specs=[VM] * len(outs),
        scratch_shapes=[pltpu.VMEM(s, jnp.float32) for s in scratch],
        compiler_params=pltpu.CompilerParams(vmem_limit_bytes=megabytes * 1024 * 1024),
    )(*args)


def local(level_set, stress_jump, materials):
    nx, ny, nz = level_set.shape
    wide, tall, mid = nx + 2 * SRC, nx + 2 * LEV, nx + 2 * SPD
    size_x, size_y = lax.axis_size("gx"), lax.axis_size("gy")

    def shift(value, axis, size, by):
        return lax.ppermute(value, axis, [(i, (i + by) % size) for i in range(size)])

    message = ((SRC + LEV) * ny, nz)
    source, low, high = call(
        pack_x, [(nx, ny, nz), message, message], [], (level_set, stress_jump, materials)
    )
    after = shift(low, "gx", size_x, -1)
    before = shift(high, "gx", size_x, 1)
    message = (tall * 8 + wide * 8 + (wide + 7) // 8 * 8, nz)
    low, high = call(pack_y, [message, message], [], (level_set, source, before, after))
    above = shift(low, "gy", size_y, -1)
    below = shift(high, "gy", size_y, 1)
    devices = size_x * size_y
    level, speed, normal_speed, peaks = call(
        velocity,
        [(tall, ROWS, nz), (mid, ROWS, nz), (nx, ny, nz), (devices, nz)],
        [(wide, ROWS, nz)] * 3,
        (level_set, source, before, after, below, above),
        megabytes=24,
    )
    peaks = lax.all_to_all(peaks.reshape(devices, 1, nz), ("gx", "gy"), 0, 0)
    peaks = peaks.reshape(devices, nz)
    (rate,) = call(first_stage, [(mid, ROWS, nz)], [(mid, 10, 8, nz)], (level, speed))
    (new_level,) = call(
        second_stage,
        [(nx, ny, nz)],
        [(mid, ROWS, nz), (nx + 4, ROWS, nz), (nx + 2, ROWS, nz), (nx + 4, 9, 8, nz)],
        (level, speed, rate, peaks),
    )
    return (new_level, normal_speed)


def solution(mesh):
    in_specs = (P("gx", "gy", None), P("gx", "gy", None), P("gx", "gy", None))
    out_specs = (P("gx", "gy", None), P("gx", "gy", None))
    return jax.shard_map(local, mesh=mesh, in_specs=in_specs, out_specs=out_specs, check_vma=False)
```

```python
import jax
import jax.numpy as jnp
import numpy as np
from jax import lax
from jax.experimental import pallas as pl
from jax.experimental.pallas import tpu as pltpu
from jax.sharding import PartitionSpec as P

SWEEPS = 4
REINIT = 2

screening = 0.1
spectral_mid = screening + 6.0
spectral_half = 6.0
courant = 0.25
pseudo_step = 0.25
weno_floor = 1e-06

OWN = 16
ROWS = 96
SRC = 9
LEV = 8
SPD = 5


def velocity_polynomial():
    times = np.array([0.0, 1.0])
    add = np.polynomial.polynomial.polyadd
    mul = np.polynomial.polynomial.polymul
    operator = add([spectral_mid], -times)
    ratio_now = spectral_half / spectral_mid
    iterate, residue, search = np.array([0.0]), np.array([1.0]), np.array([1.0 / spectral_mid])
    for _ in range(SWEEPS):
        applied = mul(operator, search)
        iterate = add(iterate, search)
        residue = add(residue, -applied)
        ratio_next = 1.0 / (2.0 * spectral_mid / spectral_half - ratio_now)
        search = add(ratio_next * ratio_now * search, 2.0 * ratio_next / spectral_half * residue)
        ratio_now = ratio_next
    return [float(c) for c in add(iterate, search)]


def along_lanes(value, k):
    return pltpu.roll(value, (-k) % value.shape[1], axis=1)


def inverse(x):
    return pl.reciprocal(x, approx=True)


def root(x):
    return x * lax.rsqrt(jnp.maximum(x, 1.2e-38))


def smooth_terms(second, second_next, third, scaled, scaled_next):
    twice = third + third
    middle = (third * twice + (1.5 * weno_floor)) + scaled * second_next
    return middle + scaled_next * twice, middle, middle - scaled * twice


def side_ratios(u1, u2, u3, jump_near, jump_far):
    p12 = jnp.square(u1 * u2)
    p13 = jnp.square(u1 * u3)
    p23 = jnp.square(u2 * u3)
    a = p12 * jump_near
    b = p23 * jump_far
    both = a + b
    both = both + both
    base = 3.0 * p13 + 0.5 * (p12 + p23)
    return (both + a) * inverse(base + p12), (both + b) * inverse(base + p23)


def weno_line(f, count):
    values, first, second, third, scaled, terms, jump, ratios = ({} for _ in range(8))

    def need(table, j, make):
        if j not in table:
            table[j] = make(j)
        return table[j]

    def val(j):
        return need(values, j, f)

    def d1(j):
        return need(first, j, lambda k: val(k + 1) - val(k))

    def d2(j):
        return need(second, j, lambda k: d1(k) - d1(k - 1))

    def d3(j):
        return need(third, j, lambda k: d2(k + 1) - d2(k))

    def sc(j):
        return need(scaled, j, lambda k: 1.5 * d2(k))

    def u(j):
        return need(terms, j, lambda k: smooth_terms(d2(k), d2(k + 1), d3(k), sc(k), sc(k + 1)))

    def g(j):
        return need(jump, j, lambda k: d3(k + 1) - d3(k))

    def r(c):
        return need(
            ratios, c, lambda k: side_ratios(u(k - 2)[0], u(k - 1)[1], u(k)[2], g(k - 1), g(k - 2))
        )

    for i in range(count):
        wide = 6.0 * (d1(i) + d1(i - 1))
        left = (wide - (d3(i - 1) + d3(i - 1))) - r(i)[0]
        right = ((d3(i) + d3(i)) - wide) - r(i + 1)[1]
        yield i, left, right


def weno_lanes(f):
    shifted = {k: along_lanes(f, k) if k else f for k in range(-3, 4)}
    ((_, left, right),) = weno_line(lambda j: shifted[j], 1)
    return left, right


def upwind_square(left, right, sign):
    return jnp.square(jnp.maximum(jnp.maximum(sign * left, sign * right), 0.0))


def sign_of(value):
    return jnp.where(value > 0, 1.0, -1.0)


def strided(ref, x, start, step):
    return ref[x, pl.ds(start, 8, stride=step), :]


def weno_rates(field, fx, speed, sx, acc, planes, start, step, emit):
    def along_x(t, _):
        row = start + t

        def f(j):
            return strided(field, fx + j, row, step)

        for i, left, right in weno_line(f, planes):
            sign = sign_of(strided(speed, sx + i, row, step))
            acc[i, t] = upwind_square(left, right, sign)
        return _

    lax.fori_loop(0, step, along_x, 0)

    def along_yz(x, _):
        lines = {}

        def f(j):
            if j not in lines:
                lines[j] = strided(field, fx + x, start + j, step)
            return lines[j]

        for t, left, right in weno_line(f, step):
            velocity = strided(speed, sx + x, start + t, step)
            sign = sign_of(velocity)
            total = acc[x, t] + upwind_square(left, right, sign)
            left, right = weno_lanes(f(t))
            total = total + upwind_square(left, right, sign)
            emit(x, t, velocity * (root(total) * (-1.0 / 12.0)))
        return _

    lax.fori_loop(0, planes, along_yz, 0, unroll=2)


def reinit_sweep(field, fx, origin, ox, planes, start, step, emit):
    def body(x, _):
        lines = {}

        def f(j):
            if j not in lines:
                lines[j] = strided(field, fx + x, start + j, step)
            return lines[j]

        for t in range(step):
            row = start + t
            centre = f(t)
            base = strided(origin, ox + x, row, step)
            sign_field = base * lax.rsqrt(base * base + 1.0)
            sign = sign_of(sign_field)
            total = upwind_square(
                centre - strided(field, fx + x - 1, row, step),
                centre - strided(field, fx + x + 1, row, step),
                sign,
            )
            total = total + upwind_square(centre - f(t - 1), centre - f(t + 1), sign)
            total = total + upwind_square(
                centre - along_lanes(centre, -1), centre - along_lanes(centre, 1), sign
            )
            emit(x, t, centre - pseudo_step * sign_field * (root(total) - 1.0))
        return _

    lax.fori_loop(0, planes, body, 0, unroll=2)


def copies(pairs, sems):
    started = [pltpu.make_async_copy(s, d, sems.at[k]) for k, (s, d) in enumerate(pairs)]
    for copy in started:
        copy.start()
    return started


def weigh(stress, materials):
    weight = jnp.where(materials == 0, 1.0, jnp.where(materials == 1, 0.6, 0.0))
    return weight.astype(jnp.float32) * stress


def pack_source(source, before, after, low, high):
    nx, ny, _ = source.shape
    wide = nx + 2 * SRC
    rest = wide * 8
    planes = [before[k] for k in range(SRC)] + [source[k] for k in range(nx)]
    planes = planes + [after[k] for k in range(SRC)]
    for k, plane in enumerate(planes):
        low[k * 8 : k * 8 + 8] = plane[0:8]
        high[k * 8 : k * 8 + 8] = plane[ny - 8 : ny]
        low[rest + k : rest + k + 1] = plane[8:9]
        high[rest + k : rest + k + 1] = plane[ny - 9 : ny - 8]
    tail = low.shape[0] - rest - wide
    low[rest + wide :] = jnp.zeros((tail, 128), jnp.float32)
    high[rest + wide :] = jnp.zeros((tail, 128), jnp.float32)


def pack_level(level, before, after, order, low, high):
    nx, ny, _ = level.shape
    for k in range(nx + 2 * LEV):
        ref, j = (level, k - LEV)
        if k < LEV:
            ref, j = (before, k)
        elif k >= LEV + nx:
            ref, j = (after, k - LEV - nx)
        low[k] = ref[j, 0:8]
        high[k] = ref[j, ny - 8 : ny]


def velocity(
    source, before, after, below_any, above_any, order, speed_hbm, own_speed, peaks,
    src, one, two, speed, below, above, sems,
):
    nx, ny, _ = source.shape
    wide = nx + 2 * SRC
    top = OWN + ny
    rest = wide * 8
    arrivals = copies(
        [
            (below_any, below),
            (above_any, above),
            (source, src.at[pl.ds(SRC, nx), pl.ds(OWN, ny)]),
            (before, src.at[pl.ds(0, SRC), pl.ds(OWN, ny)]),
            (after, src.at[pl.ds(SRC + nx, SRC), pl.ds(OWN, ny)]),
        ],
        sems,
    )
    for arrival in arrivals[:2]:
        arrival.wait()
    for k in range(wide):
        src[k, OWN - 8 : OWN] = below[k * 8 : k * 8 + 8]
        src[k, top : top + 8] = above[k * 8 : k * 8 + 8]
        src[k, OWN - 9 : OWN - 8] = below[rest + k : rest + k + 1]
        src[k, top + 8 : top + 9] = above[rest + k : rest + k + 1]
    for arrival in arrivals[2:]:
        arrival.wait()
    coefficients = velocity_polynomial()
    step = (ny + 2 * (SRC - 1)) // 8
    start = OWN - (SRC - 1)

    def sweep(old, new, shift, lo, hi, last, constant):
        def body(x, _):
            lines = {}

            def f(j):
                if j not in lines:
                    lines[j] = strided(old, x, start + j, step)
                return lines[j]

            for t in range(step):
                centre = f(t)
                beside = strided(old, x - 1, start + t, step) + strided(old, x + 1, start + t, step)
                beside = beside + (f(t - 1) + f(t + 1))
                beside = beside + (along_lanes(centre, 1) + along_lanes(centre, -1))
                if last is not None:
                    beside = last * beside
                own = centre if old is src else strided(src, x, start + t, step)
                new[x - shift, pl.ds(start + t, 8, stride=step), :] = beside + constant * own
            return _

        lax.fori_loop(lo, hi, body, 0, unroll=4)

    sweep(src, one, 0, 1, wide - 1, coefficients[4], coefficients[3])
    sweep(one, two, 0, 2, wide - 2, None, coefficients[2])
    sweep(two, one, 0, 3, wide - 3, None, coefficients[1])
    sweep(one, speed, SRC - SPD, 4, wide - 4, None, coefficients[0])
    out = pltpu.make_async_copy(speed, speed_hbm, sems.at[0])
    out.start()

    def largest(x, carry):
        mine = speed[SPD + x, OWN : OWN + ny]
        own_speed[x] = mine
        return jnp.maximum(carry, jnp.abs(mine))

    top = lax.fori_loop(0, nx, largest, jnp.zeros((ny, 128), jnp.float32))
    peaks[...] = jnp.broadcast_to(jnp.max(top), peaks.shape)
    out.wait()


def evolve(
    own_level, before, after, below, above, speed_hbm, peaks, new_level,
    level, speed, rate, stage, advected, swept, acc, sems,
):
    nx, ny, _ = new_level.shape
    tall = nx + 2 * LEV
    rows = pl.ds(OWN, ny)
    arrivals = copies(
        [
            (own_level, level.at[pl.ds(LEV, nx), rows]),
            (before, level.at[pl.ds(0, LEV), rows]),
            (after, level.at[pl.ds(LEV + nx, LEV), rows]),
            (below, level.at[pl.ds(0, tall), pl.ds(OWN - 8, 8)]),
            (above, level.at[pl.ds(0, tall), pl.ds(OWN + ny, 8)]),
            (speed_hbm, speed),
        ],
        sems,
    )
    for arrival in arrivals:
        arrival.wait()

    def emit_rate(x, t, value):
        rate[x, pl.ds(OWN - SPD + t, 8, stride=10), :] = value

    weno_rates(level, LEV - SPD, speed, 0, acc, nx + 2 * SPD, OWN - SPD, 10, emit_rate)

    peak = jnp.max(peaks[...], axis=0, keepdims=True)
    time_step = courant / (peak + 1e-06)
    step_row = jnp.broadcast_to(time_step, (8, 128))
    step_rows = jnp.broadcast_to(time_step, (ROWS - 8, 128))

    def advance(x, _):
        stage[x, 8:ROWS] = level[x + LEV - SPD, 8:ROWS] + step_rows * rate[x, 8:ROWS]
        return _

    lax.fori_loop(0, stage.shape[0], advance, 0)

    start, step = OWN - 2, 9

    def emit(x, t, value):
        row = start + t
        after = strided(stage, x + SPD - 2, row, step) + step_row * value
        before = strided(level, x + LEV - 2, row, step)
        advected[x, pl.ds(row, 8, stride=step), :] = 0.5 * before + 0.5 * after

    weno_rates(stage, SPD - 2, speed, SPD - 2, acc, nx + 4, start, step, emit)

    def emit_one(x, t, value):
        swept[x, pl.ds(OWN - 1 + t, 8, stride=9), :] = value

    reinit_sweep(advected, 1, advected, 1, nx + 2, OWN - 1, 9, emit_one)

    def emit_two(x, t, value):
        new_level[x, pl.ds(t, 8, stride=ny // 8), :] = value

    reinit_sweep(swept, 1, advected, 2, nx, OWN, ny // 8, emit_two)


BIG = 56
VM = pl.BlockSpec(memory_space=pltpu.VMEM)
HBM = pl.BlockSpec(memory_space=pltpu.HBM)
ANY = pl.BlockSpec(memory_space=pl.ANY)


def call(kernel, outs, scratch, args, megabytes, copied=0):
    ins = [a if isinstance(a, tuple) else (a, VM) for a in args]
    outs = [o if isinstance(o[0], tuple) else (o, VM) for o in outs]
    scratch = [s if isinstance(s[0], tuple) else (s, jnp.float32) for s in scratch]
    scratch_shapes = [pltpu.VMEM(shape, dtype) for shape, dtype in scratch]
    if copied:
        scratch_shapes.append(pltpu.SemaphoreType.DMA((copied,)))
    return pl.pallas_call(
        kernel,
        out_shape=[jax.ShapeDtypeStruct(shape, jnp.float32) for shape, _ in outs],
        in_specs=[place for _, place in ins],
        out_specs=[place for _, place in outs],
        scratch_shapes=scratch_shapes,
        compiler_params=pltpu.CompilerParams(vmem_limit_bytes=megabytes * 1024 * 1024),
    )(*[array for array, _ in ins])


def local(level_set, stress_jump, materials):
    tile = level_set.shape
    nx, ny, nz = tile
    wide, tall, mid = nx + 2 * SRC, nx + 2 * LEV, nx + 2 * SPD
    size_x, size_y = lax.axis_size("gx"), lax.axis_size("gy")
    devices = size_x * size_y

    def shift(value, axis, size, by):
        return lax.ppermute(value, axis, [(i, (i + by) % size) for i in range(size)])

    low = weigh(stress_jump[:SRC], materials[:SRC])
    high = weigh(stress_jump[nx - SRC :], materials[nx - SRC :])
    source_after = shift(low, "gx", size_x, -1)
    source_before = shift(high, "gx", size_x, 1)
    source = weigh(stress_jump, materials)
    level_low, level_high, _, _ = lax.optimization_barrier(
        (level_set[:LEV], level_set[nx - LEV :], low, high)
    )
    level_after = shift(level_low, "gx", size_x, -1)
    level_before = shift(level_high, "gx", size_x, 1)
    message = rows_message = (wide * 8 + (wide + 7) // 8 * 8, nz)
    low, high = call(
        pack_source, [message, message], [], (source, source_before, source_after), 8
    )
    source_above = shift(low, "gy", size_y, -1)
    source_below = shift(high, "gy", size_y, 1)
    message = (tall, 8, nz)
    low, high = call(
        pack_level,
        [message, message],
        [],
        (level_set, level_before, level_after, (low, ANY)),
        8,
    )
    level_above = shift(low, "gy", size_y, -1)
    level_below = shift(high, "gy", size_y, 1)
    speed, normal_speed, peaks = call(
        velocity,
        [((mid, ROWS, nz), HBM), tile, (devices, nz)],
        [(wide, ROWS, nz)] * 3 + [(mid, ROWS, nz), rows_message, rows_message],
        [(a, ANY) for a in (source, source_before, source_after, source_below, source_above, low)],
        BIG,
        copied=5,
    )
    peaks, level_above, level_below = lax.optimization_barrier((peaks, level_above, level_below))
    peaks = lax.all_to_all(peaks.reshape(devices, 1, nz), ("gx", "gy"), 0, 0)
    (new_level,) = call(
        evolve,
        [tile],
        [
            (tall, ROWS, nz),
            (mid, ROWS, nz),
            (mid, ROWS, nz),
            (mid, ROWS, nz),
            (nx + 4, ROWS, nz),
            (nx + 2, ROWS, nz),
            (mid, 10, 8, nz),
        ],
        [
            (a, ANY)
            for a in (level_set, level_before, level_after, level_below, level_above, speed)
        ]
        + [peaks.reshape(devices, nz)],
        BIG,
        copied=6,
    )
    return (new_level, normal_speed)


def solution(mesh):
    in_specs = (P("gx", "gy", None), P("gx", "gy", None), P("gx", "gy", None))
    out_specs = (P("gx", "gy", None), P("gx", "gy", None))
    return jax.shard_map(local, mesh=mesh, in_specs=in_specs, out_specs=out_specs, check_vma=False)
```

```python
import jax
import jax.numpy as jnp
import numpy as np
from jax import lax
from jax.experimental import pallas as pl
from jax.experimental.pallas import tpu as pltpu
from jax.sharding import PartitionSpec as P

SWEEPS = 4
REINIT = 2

screening = 0.1
spectral_mid = screening + 6.0
spectral_half = 6.0
courant = 0.25
pseudo_step = 0.25
weno_floor = 1e-06

OWN = 16
ROWS = 96
SRC = 9
LEV = 8
SPD = 5


def velocity_polynomial():
    times = np.array([0.0, 1.0])
    add = np.polynomial.polynomial.polyadd
    mul = np.polynomial.polynomial.polymul
    operator = add([spectral_mid], -times)
    ratio_now = spectral_half / spectral_mid
    iterate, residue, search = np.array([0.0]), np.array([1.0]), np.array([1.0 / spectral_mid])
    for _ in range(SWEEPS):
        applied = mul(operator, search)
        iterate = add(iterate, search)
        residue = add(residue, -applied)
        ratio_next = 1.0 / (2.0 * spectral_mid / spectral_half - ratio_now)
        search = add(ratio_next * ratio_now * search, 2.0 * ratio_next / spectral_half * residue)
        ratio_now = ratio_next
    return [float(c) for c in add(iterate, search)]


def along_lanes(value, k):
    return pltpu.roll(value, (-k) % value.shape[1], axis=1)


def inverse(x):
    return pl.reciprocal(x, approx=True)


def root(x):
    return x * lax.rsqrt(jnp.maximum(x, 1.2e-38))


def smooth_terms(second, second_next, third, scaled, scaled_next):
    twice = third + third
    middle = (third * twice + (1.5 * weno_floor)) + scaled * second_next
    return middle + scaled_next * twice, middle, middle - scaled * twice


def side_ratios(u1, u2, u3, jump_near, jump_far):
    p12 = jnp.square(u1 * u2)
    p13 = jnp.square(u1 * u3)
    p23 = jnp.square(u2 * u3)
    a = p12 * jump_near
    b = p23 * jump_far
    both = a + b
    both = both + both
    base = 3.0 * p13 + 0.5 * (p12 + p23)
    return (both + a) * inverse(base + p12), (both + b) * inverse(base + p23)


def weno_line(f, count):
    values, first, second, third, scaled, terms, jump, ratios = ({} for _ in range(8))

    def need(table, j, make):
        if j not in table:
            table[j] = make(j)
        return table[j]

    def val(j):
        return need(values, j, f)

    def d1(j):
        return need(first, j, lambda k: val(k + 1) - val(k))

    def d2(j):
        return need(second, j, lambda k: d1(k) - d1(k - 1))

    def d3(j):
        return need(third, j, lambda k: d2(k + 1) - d2(k))

    def sc(j):
        return need(scaled, j, lambda k: 1.5 * d2(k))

    def u(j):
        return need(terms, j, lambda k: smooth_terms(d2(k), d2(k + 1), d3(k), sc(k), sc(k + 1)))

    def g(j):
        return need(jump, j, lambda k: d3(k + 1) - d3(k))

    def r(c):
        return need(
            ratios, c, lambda k: side_ratios(u(k - 2)[0], u(k - 1)[1], u(k)[2], g(k - 1), g(k - 2))
        )

    for i in range(count):
        wide = 6.0 * (d1(i) + d1(i - 1))
        left = (wide - (d3(i - 1) + d3(i - 1))) - r(i)[0]
        right = ((d3(i) + d3(i)) - wide) - r(i + 1)[1]
        yield i, left, right


def weno_lanes(f):
    shifted = {k: along_lanes(f, k) if k else f for k in range(-3, 4)}
    ((_, left, right),) = weno_line(lambda j: shifted[j], 1)
    return left, right


def upwind_square(left, right, sign):
    return jnp.square(jnp.maximum(jnp.maximum(sign * left, sign * right), 0.0))


def sign_of(value):
    return jnp.where(value > 0, 1.0, -1.0)


def strided(ref, x, start, step):
    return ref[x, pl.ds(start, 8, stride=step), :]


def weno_rates(field, fx, speed, sx, acc, planes, start, step, emit):
    def along_x(t, _):
        row = start + t

        def f(j):
            return strided(field, fx + j, row, step)

        for i, left, right in weno_line(f, planes):
            sign = sign_of(strided(speed, sx + i, row, step))
            acc[i, t] = upwind_square(left, right, sign)
        return _

    lax.fori_loop(0, step, along_x, 0)

    def along_yz(x, _):
        lines = {}

        def f(j):
            if j not in lines:
                lines[j] = strided(field, fx + x, start + j, step)
            return lines[j]

        for t, left, right in weno_line(f, step):
            velocity = strided(speed, sx + x, start + t, step)
            sign = sign_of(velocity)
            total = acc[x, t] + upwind_square(left, right, sign)
            left, right = weno_lanes(f(t))
            total = total + upwind_square(left, right, sign)
            emit(x, t, velocity * (root(total) * (-1.0 / 12.0)))
        return _

    lax.fori_loop(0, planes, along_yz, 0, unroll=2)


def reinit_sweep(field, fx, origin, ox, planes, start, step, emit):
    def body(x, _):
        lines = {}

        def f(j):
            if j not in lines:
                lines[j] = strided(field, fx + x, start + j, step)
            return lines[j]

        for t in range(step):
            row = start + t
            centre = f(t)
            base = strided(origin, ox + x, row, step)
            sign_field = base * lax.rsqrt(base * base + 1.0)
            sign = sign_of(sign_field)
            total = upwind_square(
                centre - strided(field, fx + x - 1, row, step),
                centre - strided(field, fx + x + 1, row, step),
                sign,
            )
            total = total + upwind_square(centre - f(t - 1), centre - f(t + 1), sign)
            total = total + upwind_square(
                centre - along_lanes(centre, -1), centre - along_lanes(centre, 1), sign
            )
            emit(x, t, centre - pseudo_step * sign_field * (root(total) - 1.0))
        return _

    lax.fori_loop(0, planes, body, 0, unroll=2)


def weigh(stress, materials):
    weight = jnp.where(materials == 0, 1.0, jnp.where(materials == 1, 0.6, 0.0))
    return weight.astype(jnp.float32) * stress


def pack_source(source, before, after, low, high):
    nx, ny, _ = source.shape
    wide = nx + 2 * SRC
    rest = wide * 8
    planes = [before[k] for k in range(SRC)] + [source[k] for k in range(nx)]
    planes = planes + [after[k] for k in range(SRC)]
    for k, plane in enumerate(planes):
        low[k * 8 : k * 8 + 8] = plane[0:8]
        high[k * 8 : k * 8 + 8] = plane[ny - 8 : ny]
        low[rest + k : rest + k + 1] = plane[8:9]
        high[rest + k : rest + k + 1] = plane[ny - 9 : ny - 8]
    tail = low.shape[0] - rest - wide
    low[rest + wide :] = jnp.zeros((tail, 128), jnp.float32)
    high[rest + wide :] = jnp.zeros((tail, 128), jnp.float32)


def pack_level(level, before, after, order, low, high):
    nx, ny, _ = level.shape
    for k in range(nx + 2 * LEV):
        ref, j = (level, k - LEV)
        if k < LEV:
            ref, j = (before, k)
        elif k >= LEV + nx:
            ref, j = (after, k - LEV - nx)
        low[k] = ref[j, 0:8]
        high[k] = ref[j, ny - 8 : ny]


def velocity(
    source, before, after, below, above, order, speed, own_speed, peaks, src, one, two
):
    nx, ny, _ = source.shape
    wide = nx + 2 * SRC
    top = OWN + ny
    rest = wide * 8
    for k in range(nx):
        src[SRC + k, OWN:top] = source[k]
    for k in range(SRC):
        src[k, OWN:top] = before[k]
        src[SRC + nx + k, OWN:top] = after[k]
    for k in range(wide):
        src[k, OWN - 8 : OWN] = below[k * 8 : k * 8 + 8]
        src[k, top : top + 8] = above[k * 8 : k * 8 + 8]
        src[k, OWN - 9 : OWN - 8] = below[rest + k : rest + k + 1]
        src[k, top + 8 : top + 9] = above[rest + k : rest + k + 1]
    coefficients = velocity_polynomial()
    step = (ny + 2 * (SRC - 1)) // 8
    start = OWN - (SRC - 1)

    def sweep(old, new, shift, lo, hi, last, constant):
        def body(x, _):
            lines = {}

            def f(j):
                if j not in lines:
                    lines[j] = strided(old, x, start + j, step)
                return lines[j]

            for t in range(step):
                centre = f(t)
                beside = strided(old, x - 1, start + t, step) + strided(old, x + 1, start + t, step)
                beside = beside + (f(t - 1) + f(t + 1))
                beside = beside + (along_lanes(centre, 1) + along_lanes(centre, -1))
                if last is not None:
                    beside = last * beside
                own = centre if old is src else strided(src, x, start + t, step)
                new[x - shift, pl.ds(start + t, 8, stride=step), :] = beside + constant * own
            return _

        lax.fori_loop(lo, hi, body, 0, unroll=4)

    sweep(src, one, 0, 1, wide - 1, coefficients[4], coefficients[3])
    sweep(one, two, 0, 2, wide - 2, None, coefficients[2])
    sweep(two, one, 0, 3, wide - 3, None, coefficients[1])
    sweep(one, speed, SRC - SPD, 4, wide - 4, None, coefficients[0])

    def largest(x, carry):
        mine = speed[SPD + x, OWN : OWN + ny]
        own_speed[x] = mine
        return jnp.maximum(carry, jnp.abs(mine))

    top = lax.fori_loop(0, nx, largest, jnp.zeros((ny, 128), jnp.float32))
    peaks[...] = jnp.broadcast_to(jnp.max(top), peaks.shape)


def evolve(
    own_level, before, after, below, above, speed, peaks, new_level,
    level, rate, stage, advected, swept, acc,
):
    nx, ny, _ = new_level.shape
    tall = nx + 2 * LEV
    top = OWN + ny
    for k in range(nx):
        level[LEV + k, OWN:top] = own_level[k]
    for k in range(LEV):
        level[k, OWN:top] = before[k]
        level[LEV + nx + k, OWN:top] = after[k]
    for k in range(tall):
        level[k, OWN - 8 : OWN] = below[k]
        level[k, top : top + 8] = above[k]

    def emit_rate(x, t, value):
        rate[x, pl.ds(OWN - SPD + t, 8, stride=10), :] = value

    weno_rates(level, LEV - SPD, speed, 0, acc, nx + 2 * SPD, OWN - SPD, 10, emit_rate)

    peak = jnp.max(peaks[...], axis=0, keepdims=True)
    time_step = courant / (peak + 1e-06)
    step_row = jnp.broadcast_to(time_step, (8, 128))
    step_rows = jnp.broadcast_to(time_step, (ROWS - 8, 128))

    def advance(x, _):
        stage[x, 8:ROWS] = level[x + LEV - SPD, 8:ROWS] + step_rows * rate[x, 8:ROWS]
        return _

    lax.fori_loop(0, stage.shape[0], advance, 0)

    start, step = OWN - 2, 9

    def emit(x, t, value):
        row = start + t
        after = strided(stage, x + SPD - 2, row, step) + step_row * value
        before = strided(level, x + LEV - 2, row, step)
        advected[x, pl.ds(row, 8, stride=step), :] = 0.5 * before + 0.5 * after

    weno_rates(stage, SPD - 2, speed, SPD - 2, acc, nx + 4, start, step, emit)

    def emit_one(x, t, value):
        swept[x, pl.ds(OWN - 1 + t, 8, stride=9), :] = value

    reinit_sweep(advected, 1, advected, 1, nx + 2, OWN - 1, 9, emit_one)

    def emit_two(x, t, value):
        new_level[x, pl.ds(t, 8, stride=ny // 8), :] = value

    reinit_sweep(swept, 1, advected, 2, nx, OWN, ny // 8, emit_two)


BIG = 32
VM = pl.BlockSpec(memory_space=pltpu.VMEM)
ANY = pl.BlockSpec(memory_space=pl.ANY)


def call(kernel, outs, scratch, args, megabytes):
    ins = [a if isinstance(a, tuple) else (a, VM) for a in args]
    return pl.pallas_call(
        kernel,
        out_shape=[jax.ShapeDtypeStruct(shape, jnp.float32) for shape in outs],
        in_specs=[place for _, place in ins],
        out_specs=[VM] * len(outs),
        scratch_shapes=[pltpu.VMEM(shape, jnp.float32) for shape in scratch],
        compiler_params=pltpu.CompilerParams(vmem_limit_bytes=megabytes * 1024 * 1024),
    )(*[array for array, _ in ins])


def local(level_set, stress_jump, materials):
    tile = level_set.shape
    nx, ny, nz = tile
    wide, tall, mid = nx + 2 * SRC, nx + 2 * LEV, nx + 2 * SPD
    size_x, size_y = lax.axis_size("gx"), lax.axis_size("gy")
    devices = size_x * size_y

    def shift(value, axis, size, by):
        return lax.ppermute(value, axis, [(i, (i + by) % size) for i in range(size)])

    low = weigh(stress_jump[:SRC], materials[:SRC])
    high = weigh(stress_jump[nx - SRC :], materials[nx - SRC :])
    source_after = shift(low, "gx", size_x, -1)
    source_before = shift(high, "gx", size_x, 1)
    source = weigh(stress_jump, materials)
    level_low, level_high, _, _ = lax.optimization_barrier(
        (level_set[:LEV], level_set[nx - LEV :], low, high)
    )
    level_after = shift(level_low, "gx", size_x, -1)
    level_before = shift(level_high, "gx", size_x, 1)
    message = (wide * 8 + (wide + 7) // 8 * 8, nz)
    low, high = call(
        pack_source, [message, message], [], (source, source_before, source_after), 8
    )
    source_above = shift(low, "gy", size_y, -1)
    source_below = shift(high, "gy", size_y, 1)
    message = (tall, 8, nz)
    low, high = call(
        pack_level,
        [message, message],
        [],
        (level_set, level_before, level_after, (low, ANY)),
        8,
    )
    level_above = shift(low, "gy", size_y, -1)
    level_below = shift(high, "gy", size_y, 1)
    speed, normal_speed, peaks = call(
        velocity,
        [(mid, ROWS, nz), tile, (devices, nz)],
        [(wide, ROWS, nz)] * 3,
        (source, source_before, source_after, source_below, source_above, (low, ANY)),
        BIG,
    )
    peaks, level_above, level_below = lax.optimization_barrier((peaks, level_above, level_below))
    peaks = lax.all_to_all(peaks.reshape(devices, 1, nz), ("gx", "gy"), 0, 0)
    (new_level,) = call(
        evolve,
        [tile],
        [
            (tall, ROWS, nz),
            (mid, ROWS, nz),
            (mid, ROWS, nz),
            (nx + 4, ROWS, nz),
            (nx + 2, ROWS, nz),
            (mid, 10, 8, nz),
        ],
        (
            level_set,
            level_before,
            level_after,
            level_below,
            level_above,
            speed,
            peaks.reshape(devices, nz),
        ),
        BIG,
    )
    return (new_level, normal_speed)


def solution(mesh):
    in_specs = (P("gx", "gy", None), P("gx", "gy", None), P("gx", "gy", None))
    out_specs = (P("gx", "gy", None), P("gx", "gy", None))
    return jax.shard_map(local, mesh=mesh, in_specs=in_specs, out_specs=out_specs, check_vma=False)
```

```python
import jax
import jax.numpy as jnp
import numpy as np
from jax import lax
from jax.experimental import pallas as pl
from jax.experimental.pallas import tpu as pltpu
from jax.sharding import Mesh, PartitionSpec as P

SWEEPS = 4
REINIT = 2

screening = 0.1
spectral_mid = screening + 6.0
spectral_half = 6.0
courant = 0.25
pseudo_step = 0.25
weno_floor = 1e-06

OWN = 16
ROWS = 96
SRC = 9
LEV = 8
SPD = 5


def velocity_polynomial():
    times = np.array([0.0, 1.0])
    add = np.polynomial.polynomial.polyadd
    mul = np.polynomial.polynomial.polymul
    operator = add([spectral_mid], -times)
    ratio_now = spectral_half / spectral_mid
    iterate, residue, search = np.array([0.0]), np.array([1.0]), np.array([1.0 / spectral_mid])
    for _ in range(SWEEPS):
        applied = mul(operator, search)
        iterate = add(iterate, search)
        residue = add(residue, -applied)
        ratio_next = 1.0 / (2.0 * spectral_mid / spectral_half - ratio_now)
        search = add(ratio_next * ratio_now * search, 2.0 * ratio_next / spectral_half * residue)
        ratio_now = ratio_next
    return [float(c) for c in add(iterate, search)]


def along_lanes(value, k):
    return pltpu.roll(value, (-k) % value.shape[1], axis=1)


def inverse(x):
    return pl.reciprocal(x, approx=True)


def root(x):
    return x * lax.rsqrt(jnp.maximum(x, 1.2e-38))


def smooth_terms(second, second_next, third, scaled, scaled_next):
    twice = third + third
    middle = (third * twice + (1.5 * weno_floor)) + scaled * second_next
    return middle + scaled_next * twice, middle, middle - scaled * twice


def side_ratios(u1, u2, u3, jump_near, jump_far):
    p12 = jnp.square(u1 * u2)
    p13 = jnp.square(u1 * u3)
    p23 = jnp.square(u2 * u3)
    a = p12 * jump_near
    b = p23 * jump_far
    both = a + b
    both = both + both
    base = 3.0 * p13 + 0.5 * (p12 + p23)
    return (both + a) * inverse(base + p12), (both + b) * inverse(base + p23)


def weno_line(f, count):
    values, first, second, third, scaled, terms, jump, ratios = ({} for _ in range(8))

    def need(table, j, make):
        if j not in table:
            table[j] = make(j)
        return table[j]

    def val(j):
        return need(values, j, f)

    def d1(j):
        return need(first, j, lambda k: val(k + 1) - val(k))

    def d2(j):
        return need(second, j, lambda k: d1(k) - d1(k - 1))

    def d3(j):
        return need(third, j, lambda k: d2(k + 1) - d2(k))

    def sc(j):
        return need(scaled, j, lambda k: 1.5 * d2(k))

    def u(j):
        return need(terms, j, lambda k: smooth_terms(d2(k), d2(k + 1), d3(k), sc(k), sc(k + 1)))

    def g(j):
        return need(jump, j, lambda k: d3(k + 1) - d3(k))

    def r(c):
        return need(
            ratios, c, lambda k: side_ratios(u(k - 2)[0], u(k - 1)[1], u(k)[2], g(k - 1), g(k - 2))
        )

    for i in range(count):
        wide = 6.0 * (d1(i) + d1(i - 1))
        left = (wide - (d3(i - 1) + d3(i - 1))) - r(i)[0]
        right = ((d3(i) + d3(i)) - wide) - r(i + 1)[1]
        yield i, left, right


def weno_lanes(f):
    shifted = {k: along_lanes(f, k) if k else f for k in range(-3, 4)}
    ((_, left, right),) = weno_line(lambda j: shifted[j], 1)
    return left, right


def upwind_square(left, right, sign):
    return jnp.square(jnp.maximum(jnp.maximum(sign * left, sign * right), 0.0))


def sign_of(value):
    return jnp.where(value > 0, 1.0, -1.0)


def strided(ref, x, start, step):
    return ref[x, pl.ds(start, 8, stride=step), :]


def weno_rates(field, fx, speed, sx, acc, planes, start, step, emit):
    def along_x(t, _):
        row = start + t

        def f(j):
            return strided(field, fx + j, row, step)

        for i, left, right in weno_line(f, planes):
            sign = sign_of(strided(speed, sx + i, row, step))
            acc[i, t] = upwind_square(left, right, sign)
        return _

    lax.fori_loop(0, step, along_x, 0)

    def along_yz(x, _):
        lines = {}

        def f(j):
            if j not in lines:
                lines[j] = strided(field, fx + x, start + j, step)
            return lines[j]

        for t, left, right in weno_line(f, step):
            velocity = strided(speed, sx + x, start + t, step)
            sign = sign_of(velocity)
            total = acc[x, t] + upwind_square(left, right, sign)
            left, right = weno_lanes(f(t))
            total = total + upwind_square(left, right, sign)
            emit(x, t, velocity * (root(total) * (-1.0 / 12.0)))
        return _

    lax.fori_loop(0, planes, along_yz, 0, unroll=2)


def reinit_sweep(field, fx, origin, ox, planes, start, step, emit):
    def body(x, _):
        lines = {}

        def f(j):
            if j not in lines:
                lines[j] = strided(field, fx + x, start + j, step)
            return lines[j]

        for t in range(step):
            row = start + t
            centre = f(t)
            base = strided(origin, ox + x, row, step)
            sign_field = base * lax.rsqrt(base * base + 1.0)
            sign = sign_of(sign_field)
            total = upwind_square(
                centre - strided(field, fx + x - 1, row, step),
                centre - strided(field, fx + x + 1, row, step),
                sign,
            )
            total = total + upwind_square(centre - f(t - 1), centre - f(t + 1), sign)
            total = total + upwind_square(
                centre - along_lanes(centre, -1), centre - along_lanes(centre, 1), sign
            )
            emit(x, t, centre - pseudo_step * sign_field * (root(total) - 1.0))
        return _

    lax.fori_loop(0, planes, body, 0, unroll=2)


def weigh(stress, materials):
    weight = jnp.where(materials == 0, 1.0, jnp.where(materials == 1, 0.6, 0.0))
    return weight.astype(jnp.float32) * stress


def pack_source(source, before, after, low, high):
    nx, ny, _ = source.shape
    wide = nx + 2 * SRC
    rest = wide * 8
    planes = [before[k] for k in range(SRC)] + [source[k] for k in range(nx)]
    planes = planes + [after[k] for k in range(SRC)]
    for k, plane in enumerate(planes):
        low[k * 8 : k * 8 + 8] = plane[0:8]
        high[k * 8 : k * 8 + 8] = plane[ny - 8 : ny]
        low[rest + k : rest + k + 1] = plane[8:9]
        high[rest + k : rest + k + 1] = plane[ny - 9 : ny - 8]
    tail = low.shape[0] - rest - wide
    low[rest + wide :] = jnp.zeros((tail, 128), jnp.float32)
    high[rest + wide :] = jnp.zeros((tail, 128), jnp.float32)


def pack_level(level, before, after, order, low, high):
    nx, ny, _ = level.shape
    for k in range(nx + 2 * LEV):
        ref, j = (level, k - LEV)
        if k < LEV:
            ref, j = (before, k)
        elif k >= LEV + nx:
            ref, j = (after, k - LEV - nx)
        low[k] = ref[j, 0:8]
        high[k] = ref[j, ny - 8 : ny]


def velocity(
    source, before, after, below, above, order, speed, own_speed, peaks, src, one, two
):
    nx, ny, _ = source.shape
    wide = nx + 2 * SRC
    top = OWN + ny
    rest = wide * 8
    for k in range(nx):
        src[SRC + k, OWN:top] = source[k]
    for k in range(SRC):
        src[k, OWN:top] = before[k]
        src[SRC + nx + k, OWN:top] = after[k]
    for k in range(wide):
        src[k, OWN - 8 : OWN] = below[k * 8 : k * 8 + 8]
        src[k, top : top + 8] = above[k * 8 : k * 8 + 8]
        src[k, OWN - 9 : OWN - 8] = below[rest + k : rest + k + 1]
        src[k, top + 8 : top + 9] = above[rest + k : rest + k + 1]
    coefficients = velocity_polynomial()
    step = (ny + 2 * (SRC - 1)) // 8
    start = OWN - (SRC - 1)

    def sweep(old, new, shift, lo, hi, last, constant):
        def body(x, _):
            lines = {}

            def f(j):
                if j not in lines:
                    lines[j] = strided(old, x, start + j, step)
                return lines[j]

            for t in range(step):
                centre = f(t)
                beside = strided(old, x - 1, start + t, step) + strided(old, x + 1, start + t, step)
                beside = beside + (f(t - 1) + f(t + 1))
                beside = beside + (along_lanes(centre, 1) + along_lanes(centre, -1))
                if last is not None:
                    beside = last * beside
                own = centre if old is src else strided(src, x, start + t, step)
                new[x - shift, pl.ds(start + t, 8, stride=step), :] = beside + constant * own
            return _

        lax.fori_loop(lo, hi, body, 0, unroll=4)

    sweep(src, one, 0, 1, wide - 1, coefficients[4], coefficients[3])
    sweep(one, two, 0, 2, wide - 2, None, coefficients[2])
    sweep(two, one, 0, 3, wide - 3, None, coefficients[1])
    sweep(one, speed, SRC - SPD, 4, wide - 4, None, coefficients[0])

    def largest(x, carry):
        mine = speed[SPD + x, OWN : OWN + ny]
        own_speed[x] = mine
        return jnp.maximum(carry, jnp.abs(mine))

    top = lax.fori_loop(0, nx, largest, jnp.zeros((ny, 128), jnp.float32))
    peaks[...] = jnp.broadcast_to(jnp.max(top), peaks.shape)


def gather_peaks(mine, other, peaks):
    peaks[...] = jnp.broadcast_to(jnp.maximum(mine[0:1], other[0:1]), peaks.shape)


def first_stage(own_level, before, after, below, above, speed, level, rate, acc):
    nx, ny, _ = own_level.shape
    tall = nx + 2 * LEV
    top = OWN + ny
    for k in range(nx):
        level[LEV + k, OWN:top] = own_level[k]
    for k in range(LEV):
        level[k, OWN:top] = before[k]
        level[LEV + nx + k, OWN:top] = after[k]
    for k in range(tall):
        level[k, OWN - 8 : OWN] = below[k]
        level[k, top : top + 8] = above[k]

    def emit(x, t, value):
        rate[x, pl.ds(OWN - SPD + t, 8, stride=10), :] = value

    weno_rates(level, LEV - SPD, speed, 0, acc, nx + 2 * SPD, OWN - SPD, 10, emit)


def second_stage(level, speed, rate, peaks, new_level, stage, advected, swept, acc):
    nx, ny, _ = new_level.shape
    peak = jnp.max(peaks[...], axis=0, keepdims=True)
    time_step = courant / (peak + 1e-06)
    step_row = jnp.broadcast_to(time_step, (8, 128))
    step_rows = jnp.broadcast_to(time_step, (ROWS - 8, 128))

    def advance(x, _):
        stage[x, 8:ROWS] = level[x + LEV - SPD, 8:ROWS] + step_rows * rate[x, 8:ROWS]
        return _

    lax.fori_loop(0, stage.shape[0], advance, 0)

    start, step = OWN - 2, 9

    def emit(x, t, value):
        row = start + t
        after = strided(stage, x + SPD - 2, row, step) + step_row * value
        before = strided(level, x + LEV - 2, row, step)
        advected[x, pl.ds(row, 8, stride=step), :] = 0.5 * before + 0.5 * after

    weno_rates(stage, SPD - 2, speed, SPD - 2, acc, nx + 4, start, step, emit)

    def emit_one(x, t, value):
        swept[x, pl.ds(OWN - 1 + t, 8, stride=9), :] = value

    reinit_sweep(advected, 1, advected, 1, nx + 2, OWN - 1, 9, emit_one)

    def emit_two(x, t, value):
        new_level[x, pl.ds(t, 8, stride=ny // 8), :] = value

    reinit_sweep(swept, 1, advected, 2, nx, OWN, ny // 8, emit_two)


BIG = 32
VM = pl.BlockSpec(memory_space=pltpu.VMEM)
ANY = pl.BlockSpec(memory_space=pl.ANY)


def call(kernel, outs, scratch, args, megabytes):
    ins = [a if isinstance(a, tuple) else (a, VM) for a in args]
    return pl.pallas_call(
        kernel,
        out_shape=[jax.ShapeDtypeStruct(shape, jnp.float32) for shape in outs],
        in_specs=[place for _, place in ins],
        out_specs=[VM] * len(outs),
        scratch_shapes=[pltpu.VMEM(shape, jnp.float32) for shape in scratch],
        compiler_params=pltpu.CompilerParams(vmem_limit_bytes=megabytes * 1024 * 1024),
    )(*[array for array, _ in ins])


def local(level_set, stress_jump, materials):
    tile = level_set.shape
    nx, ny, nz = tile
    wide, tall, mid = nx + 2 * SRC, nx + 2 * LEV, nx + 2 * SPD
    size_x, size_y = lax.axis_size("gx"), 2 * lax.axis_size("gz")
    devices = size_x * size_y

    def shift(value, axis, size, by):
        return lax.ppermute(value, axis, [(i, (i + by) % size) for i in range(size)])

    low = weigh(stress_jump[:SRC], materials[:SRC])
    high = weigh(stress_jump[nx - SRC :], materials[nx - SRC :])
    source_after = shift(low, "gx", size_x, -1)
    source_before = shift(high, "gx", size_x, 1)
    source = weigh(stress_jump, materials)
    level_low, level_high, _, _ = lax.optimization_barrier(
        (level_set[:LEV], level_set[nx - LEV :], low, high)
    )
    level_after = shift(level_low, "gx", size_x, -1)
    level_before = shift(level_high, "gx", size_x, 1)
    message = (wide * 8 + (wide + 7) // 8 * 8, nz)
    low, high = call(
        pack_source, [message, message], [], (source, source_before, source_after), 8
    )
    source_above = shift(low, ("gz", "core"), size_y, -1)
    source_below = shift(high, ("gz", "core"), size_y, 1)
    message = (tall, 8, nz)
    low, high = call(
        pack_level,
        [message, message],
        [],
        (level_set, level_before, level_after, (low, ANY)),
        8,
    )
    level_above = shift(low, ("gz", "core"), size_y, -1)
    level_below = shift(high, ("gz", "core"), size_y, 1)
    speed, normal_speed, peak = call(
        velocity,
        [(mid, ROWS, nz), tile, (8, nz)],
        [(wide, ROWS, nz)] * 3,
        (source, source_before, source_after, source_below, source_above, (low, ANY)),
        BIG,
    )
    peak, level_above, level_below = lax.optimization_barrier((peak, level_above, level_below))
    other = lax.ppermute(peak, "core", [(0, 1), (1, 0)])
    chips = devices // 2
    (peaks,) = call(gather_peaks, [(chips, nz)], [], (peak, other), 4)
    peaks = lax.all_to_all(peaks.reshape(chips, 1, nz), ("gx", "gz"), 0, 0)
    level, rate = call(
        first_stage,
        [(tall, ROWS, nz), (mid, ROWS, nz)],
        [(mid, 10, 8, nz)],
        (level_set, level_before, level_after, level_below, level_above, speed),
        BIG,
    )
    (new_level,) = call(
        second_stage,
        [tile],
        [(mid, ROWS, nz), (nx + 4, ROWS, nz), (nx + 2, ROWS, nz), (nx + 4, 9, 8, nz)],
        (level, speed, rate, peaks.reshape(chips, nz)),
        BIG,
    )
    return (new_level, normal_speed)


def solution(mesh):
    size_x, size_y = mesh.devices.shape
    chips = Mesh(mesh.devices.reshape(size_x, size_y // 2, 2), ("gx", "gz", "core"))
    spec = P("gx", ("gz", "core"), None)
    return jax.shard_map(
        local, mesh=chips, in_specs=(spec,) * 3, out_specs=(spec,) * 2, check_vma=False
    )
```

```python
import jax
import jax.numpy as jnp
import numpy as np
from jax import lax
from jax.experimental import pallas as pl
from jax.experimental.pallas import tpu as pltpu
from jax.sharding import PartitionSpec as P

SWEEPS = 4
REINIT = 2

screening = 0.1
spectral_mid = screening + 6.0
spectral_half = 6.0
courant = 0.25
pseudo_step = 0.25
weno_floor = 1e-06

OWN = 16
ROWS = 96
SRC = 9
LEV = 8
SPD = 5


def velocity_polynomial():
    times = np.array([0.0, 1.0])
    add = np.polynomial.polynomial.polyadd
    mul = np.polynomial.polynomial.polymul
    operator = add([spectral_mid], -times)
    ratio_now = spectral_half / spectral_mid
    iterate, residue, search = np.array([0.0]), np.array([1.0]), np.array([1.0 / spectral_mid])
    for _ in range(SWEEPS):
        applied = mul(operator, search)
        iterate = add(iterate, search)
        residue = add(residue, -applied)
        ratio_next = 1.0 / (2.0 * spectral_mid / spectral_half - ratio_now)
        search = add(ratio_next * ratio_now * search, 2.0 * ratio_next / spectral_half * residue)
        ratio_now = ratio_next
    return [float(c) for c in add(iterate, search)]


def along_lanes(value, k):
    return pltpu.roll(value, (-k) % value.shape[1], axis=1)


def inverse(x):
    return pl.reciprocal(x, approx=True)


def root(x):
    return x * lax.rsqrt(jnp.maximum(x, 1.2e-38))


def smooth_terms(second, second_next, third, scaled, scaled_next):
    twice = third + third
    middle = (third * twice + (1.5 * weno_floor)) + scaled * second_next
    return middle + scaled_next * twice, middle, middle - scaled * twice


def side_ratios(u1, u2, u3, jump_near, jump_far):
    p12 = jnp.square(u1 * u2)
    p13 = jnp.square(u1 * u3)
    p23 = jnp.square(u2 * u3)
    a = p12 * jump_near
    b = p23 * jump_far
    both = a + b
    both = both + both
    base = 3.0 * p13 + 0.5 * (p12 + p23)
    return (both + a) * inverse(base + p12), (both + b) * inverse(base + p23)


def weno_line(f, count):
    values, first, second, third, scaled, terms, jump, ratios = ({} for _ in range(8))

    def need(table, j, make):
        if j not in table:
            table[j] = make(j)
        return table[j]

    def val(j):
        return need(values, j, f)

    def d1(j):
        return need(first, j, lambda k: val(k + 1) - val(k))

    def d2(j):
        return need(second, j, lambda k: d1(k) - d1(k - 1))

    def d3(j):
        return need(third, j, lambda k: d2(k + 1) - d2(k))

    def sc(j):
        return need(scaled, j, lambda k: 1.5 * d2(k))

    def u(j):
        return need(terms, j, lambda k: smooth_terms(d2(k), d2(k + 1), d3(k), sc(k), sc(k + 1)))

    def g(j):
        return need(jump, j, lambda k: d3(k + 1) - d3(k))

    def r(c):
        return need(
            ratios, c, lambda k: side_ratios(u(k - 2)[0], u(k - 1)[1], u(k)[2], g(k - 1), g(k - 2))
        )

    for i in range(count):
        wide = 6.0 * (d1(i) + d1(i - 1))
        left = (wide - (d3(i - 1) + d3(i - 1))) - r(i)[0]
        right = ((d3(i) + d3(i)) - wide) - r(i + 1)[1]
        yield i, left, right


def weno_lanes(f):
    cells = {k: along_lanes(f, k) if k else f for k in range(-3, 3)}
    first = {k: cells[k + 1] - cells[k] for k in range(-3, 2)}
    second = {k: first[k] - first[k - 1] for k in range(-2, 2)}
    third = {k: second[k + 1] - second[k] for k in range(-2, 1)}

    def terms(k):
        return smooth_terms(
            second[k], second[k + 1], third[k], 1.5 * second[k], 1.5 * second[k + 1]
        )

    ratio_left, ratio_right = side_ratios(
        terms(-2)[0], terms(-1)[1], terms(0)[2], third[0] - third[-1], third[-1] - third[-2]
    )
    wide = 6.0 * (first[0] + first[-1])
    left = (wide - (third[-1] + third[-1])) - ratio_left
    right = ((third[0] + third[0]) - wide) - along_lanes(ratio_right, 1)
    return left, right


def upwind_square(left, right, sign):
    return jnp.square(jnp.maximum(jnp.maximum(sign * left, sign * right), 0.0))


def sign_of(value):
    return jnp.where(value > 0, 1.0, -1.0)


def strided(ref, x, start, step):
    return ref[x, pl.ds(start, 8, stride=step), :]


def weno_rates(field, fx, speed, sx, acc, planes, start, step, emit):
    def along_x(t, _):
        row = start + t

        def f(j):
            return strided(field, fx + j, row, step)

        for i, left, right in weno_line(f, planes):
            sign = sign_of(strided(speed, sx + i, row, step))
            acc[i, t] = upwind_square(left, right, sign)
        return _

    lax.fori_loop(0, step, along_x, 0)

    def along_yz(x, _):
        lines = {}

        def f(j):
            if j not in lines:
                lines[j] = strided(field, fx + x, start + j, step)
            return lines[j]

        for t, left, right in weno_line(f, step):
            velocity = strided(speed, sx + x, start + t, step)
            sign = sign_of(velocity)
            total = acc[x, t] + upwind_square(left, right, sign)
            left, right = weno_lanes(f(t))
            total = total + upwind_square(left, right, sign)
            emit(x, t, velocity * (root(total) * (-1.0 / 12.0)))
        return _

    lax.fori_loop(0, planes, along_yz, 0, unroll=3)


def reinit_sweep(field, fx, origin, ox, planes, start, step, emit):
    def body(x, _):
        lines = {}

        def f(j):
            if j not in lines:
                lines[j] = strided(field, fx + x, start + j, step)
            return lines[j]

        for t in range(step):
            row = start + t
            centre = f(t)
            base = strided(origin, ox + x, row, step)
            sign_field = base * lax.rsqrt(base * base + 1.0)
            sign = sign_of(sign_field)
            total = upwind_square(
                centre - strided(field, fx + x - 1, row, step),
                centre - strided(field, fx + x + 1, row, step),
                sign,
            )
            total = total + upwind_square(centre - f(t - 1), centre - f(t + 1), sign)
            total = total + upwind_square(
                centre - along_lanes(centre, -1), centre - along_lanes(centre, 1), sign
            )
            emit(x, t, centre - pseudo_step * sign_field * (root(total) - 1.0))
        return _

    lax.fori_loop(0, planes, body, 0, unroll=4)


def weigh(stress, materials):
    weight = jnp.where(materials == 0, 1.0, jnp.where(materials == 1, 0.6, 0.0))
    return weight.astype(jnp.float32) * stress


def pack_source(source, before, after, low, high):
    nx, ny, _ = source.shape
    wide = nx + 2 * SRC
    rest = wide * 8
    planes = [before[k] for k in range(SRC)] + [source[k] for k in range(nx)]
    planes = planes + [after[k] for k in range(SRC)]
    for k, plane in enumerate(planes):
        low[k * 8 : k * 8 + 8] = plane[0:8]
        high[k * 8 : k * 8 + 8] = plane[ny - 8 : ny]
        low[rest + k : rest + k + 1] = plane[8:9]
        high[rest + k : rest + k + 1] = plane[ny - 9 : ny - 8]
    tail = low.shape[0] - rest - wide
    low[rest + wide :] = jnp.zeros((tail, 128), jnp.float32)
    high[rest + wide :] = jnp.zeros((tail, 128), jnp.float32)


def pack_level(level, before, after, order, low, high):
    nx, ny, _ = level.shape
    for k in range(nx + 2 * LEV):
        ref, j = (level, k - LEV)
        if k < LEV:
            ref, j = (before, k)
        elif k >= LEV + nx:
            ref, j = (after, k - LEV - nx)
        low[k] = ref[j, 0:8]
        high[k] = ref[j, ny - 8 : ny]


def velocity(
    source, before, after, below, above, order, speed, own_speed, peaks, src, one, two
):
    nx, ny, _ = source.shape
    wide = nx + 2 * SRC
    top = OWN + ny
    rest = wide * 8
    for k in range(nx):
        src[SRC + k, OWN:top] = source[k]
    for k in range(SRC):
        src[k, OWN:top] = before[k]
        src[SRC + nx + k, OWN:top] = after[k]
    for k in range(wide):
        src[k, OWN - 8 : OWN] = below[k * 8 : k * 8 + 8]
        src[k, top : top + 8] = above[k * 8 : k * 8 + 8]
        src[k, OWN - 9 : OWN - 8] = below[rest + k : rest + k + 1]
        src[k, top + 8 : top + 9] = above[rest + k : rest + k + 1]
    coefficients = velocity_polynomial()
    step = (ny + 2 * (SRC - 1)) // 8
    start = OWN - (SRC - 1)

    def sweep(old, new, shift, lo, hi, last, constant):
        def body(x, _):
            lines = {}

            def f(j):
                if j not in lines:
                    lines[j] = strided(old, x, start + j, step)
                return lines[j]

            for t in range(step):
                centre = f(t)
                beside = strided(old, x - 1, start + t, step) + strided(old, x + 1, start + t, step)
                beside = beside + (f(t - 1) + f(t + 1))
                beside = beside + (along_lanes(centre, 1) + along_lanes(centre, -1))
                if last is not None:
                    beside = last * beside
                own = centre if old is src else strided(src, x, start + t, step)
                new[x - shift, pl.ds(start + t, 8, stride=step), :] = beside + constant * own
            return _

        lax.fori_loop(lo, hi, body, 0, unroll=11)

    sweep(src, one, 0, 1, wide - 1, coefficients[4], coefficients[3])
    sweep(one, two, 0, 2, wide - 2, None, coefficients[2])
    sweep(two, one, 0, 3, wide - 3, None, coefficients[1])
    sweep(one, speed, SRC - SPD, 4, wide - 4, None, coefficients[0])

    def largest(x, carry):
        mine = speed[SPD + x, OWN : OWN + ny]
        own_speed[x] = mine
        return jnp.maximum(carry, jnp.abs(mine))

    top = lax.fori_loop(0, nx, largest, jnp.zeros((ny, 128), jnp.float32))
    peaks[...] = jnp.broadcast_to(jnp.max(top), peaks.shape)


def evolve(
    own_level, before, after, below, above, speed, peaks, new_level,
    level, rate, stage, advected, swept, acc,
):
    nx, ny, _ = new_level.shape
    tall = nx + 2 * LEV
    top = OWN + ny
    for k in range(nx):
        level[LEV + k, OWN:top] = own_level[k]
    for k in range(LEV):
        level[k, OWN:top] = before[k]
        level[LEV + nx + k, OWN:top] = after[k]
    for k in range(tall):
        level[k, OWN - 8 : OWN] = below[k]
        level[k, top : top + 8] = above[k]

    def emit_rate(x, t, value):
        rate[x, pl.ds(OWN - SPD + t, 8, stride=10), :] = value

    weno_rates(level, LEV - SPD, speed, 0, acc, nx + 2 * SPD, OWN - SPD, 10, emit_rate)

    peak = jnp.max(peaks[...], axis=0, keepdims=True)
    time_step = courant / (peak + 1e-06)
    step_row = jnp.broadcast_to(time_step, (8, 128))
    step_rows = jnp.broadcast_to(time_step, (ROWS - 8, 128))

    def advance(x, _):
        stage[x, 8:ROWS] = level[x + LEV - SPD, 8:ROWS] + step_rows * rate[x, 8:ROWS]
        return _

    lax.fori_loop(0, stage.shape[0], advance, 0)

    start, step = OWN - 2, 9

    def emit(x, t, value):
        row = start + t
        after = strided(stage, x + SPD - 2, row, step) + step_row * value
        before = strided(level, x + LEV - 2, row, step)
        advected[x, pl.ds(row, 8, stride=step), :] = 0.5 * before + 0.5 * after

    weno_rates(stage, SPD - 2, speed, SPD - 2, acc, nx + 4, start, step, emit)

    def emit_one(x, t, value):
        swept[x, pl.ds(OWN - 1 + t, 8, stride=9), :] = value

    reinit_sweep(advected, 1, advected, 1, nx + 2, OWN - 1, 9, emit_one)

    def emit_two(x, t, value):
        new_level[x, pl.ds(t, 8, stride=ny // 8), :] = value

    reinit_sweep(swept, 1, advected, 2, nx, OWN, ny // 8, emit_two)


BIG = 32
VM = pl.BlockSpec(memory_space=pltpu.VMEM)
ANY = pl.BlockSpec(memory_space=pl.ANY)


def call(kernel, outs, scratch, args, megabytes):
    ins = [a if isinstance(a, tuple) else (a, VM) for a in args]
    return pl.pallas_call(
        kernel,
        out_shape=[jax.ShapeDtypeStruct(shape, jnp.float32) for shape in outs],
        in_specs=[place for _, place in ins],
        out_specs=[VM] * len(outs),
        scratch_shapes=[pltpu.VMEM(shape, jnp.float32) for shape in scratch],
        compiler_params=pltpu.CompilerParams(vmem_limit_bytes=megabytes * 1024 * 1024),
    )(*[array for array, _ in ins])


def local(level_set, stress_jump, materials):
    tile = level_set.shape
    nx, ny, nz = tile
    wide, tall, mid = nx + 2 * SRC, nx + 2 * LEV, nx + 2 * SPD
    size_x, size_y = lax.axis_size("gx"), lax.axis_size("gy")
    devices = size_x * size_y

    def shift(value, axis, size, by):
        return lax.ppermute(value, axis, [(i, (i + by) % size) for i in range(size)])

    low = weigh(stress_jump[:SRC], materials[:SRC])
    high = weigh(stress_jump[nx - SRC :], materials[nx - SRC :])
    source_after = shift(low, "gx", size_x, -1)
    source_before = shift(high, "gx", size_x, 1)
    source = weigh(stress_jump, materials)
    level_low, level_high, _, _ = lax.optimization_barrier(
        (level_set[:LEV], level_set[nx - LEV :], low, high)
    )
    level_after = shift(level_low, "gx", size_x, -1)
    level_before = shift(level_high, "gx", size_x, 1)
    message = (wide * 8 + (wide + 7) // 8 * 8, nz)
    low, high = call(
        pack_source, [message, message], [], (source, source_before, source_after), 8
    )
    source_above = shift(low, "gy", size_y, -1)
    source_below = shift(high, "gy", size_y, 1)
    message = (tall, 8, nz)
    low, high = call(
        pack_level,
        [message, message],
        [],
        (level_set, level_before, level_after, (low, ANY)),
        8,
    )
    level_above = shift(low, "gy", size_y, -1)
    level_below = shift(high, "gy", size_y, 1)
    speed, normal_speed, peaks = call(
        velocity,
        [(mid, ROWS, nz), tile, (devices, nz)],
        [(wide, ROWS, nz)] * 3,
        (source, source_before, source_after, source_below, source_above, (low, ANY)),
        BIG,
    )
    peaks, level_above, level_below = lax.optimization_barrier((peaks, level_above, level_below))
    peaks = lax.all_to_all(peaks.reshape(devices, 1, nz), ("gx", "gy"), 0, 0)
    (new_level,) = call(
        evolve,
        [tile],
        [
            (tall, ROWS, nz),
            (mid, ROWS, nz),
            (mid, ROWS, nz),
            (nx + 4, ROWS, nz),
            (nx + 2, ROWS, nz),
            (mid, 10, 8, nz),
        ],
        (
            level_set,
            level_before,
            level_after,
            level_below,
            level_above,
            speed,
            peaks.reshape(devices, nz),
        ),
        BIG,
    )
    return (new_level, normal_speed)


def solution(mesh):
    in_specs = (P("gx", "gy", None), P("gx", "gy", None), P("gx", "gy", None))
    out_specs = (P("gx", "gy", None), P("gx", "gy", None))
    return jax.shard_map(local, mesh=mesh, in_specs=in_specs, out_specs=out_specs, check_vma=False)
```

```python
import jax
import jax.numpy as jnp
import numpy as np
from jax import lax
from jax.experimental import pallas as pl
from jax.experimental.pallas import tpu as pltpu
from jax.sharding import PartitionSpec as P

SWEEPS = 4
REINIT = 2

screening = 0.1
spectral_mid = screening + 6.0
spectral_half = 6.0
courant = 0.25
pseudo_step = 0.25
weno_floor = 1e-06

OWN = 16
ROWS = 96
SRC = 9
LEV = 8
SPD = 5


def velocity_polynomial():
    times = np.array([0.0, 1.0])
    add = np.polynomial.polynomial.polyadd
    mul = np.polynomial.polynomial.polymul
    operator = add([spectral_mid], -times)
    ratio_now = spectral_half / spectral_mid
    iterate, residue, search = np.array([0.0]), np.array([1.0]), np.array([1.0 / spectral_mid])
    for _ in range(SWEEPS):
        applied = mul(operator, search)
        iterate = add(iterate, search)
        residue = add(residue, -applied)
        ratio_next = 1.0 / (2.0 * spectral_mid / spectral_half - ratio_now)
        search = add(ratio_next * ratio_now * search, 2.0 * ratio_next / spectral_half * residue)
        ratio_now = ratio_next
    return [float(c) for c in add(iterate, search)]


def along_lanes(value, k):
    return pltpu.roll(value, (-k) % value.shape[1], axis=1)


def inverse(x):
    return pl.reciprocal(x, approx=True)


def root(x):
    return x * lax.rsqrt(jnp.maximum(x, 1.2e-38))


def smooth_terms(second, second_next, third, scaled, scaled_next):
    twice = third + third
    middle = (third * twice + (1.5 * weno_floor)) + scaled * second_next
    return middle + scaled_next * twice, middle, middle - scaled * twice


def side_ratios(u1, u2, u3, jump_near, jump_far):
    p12 = jnp.square(u1 * u2)
    p13 = jnp.square(u1 * u3)
    p23 = jnp.square(u2 * u3)
    a = p12 * jump_near
    b = p23 * jump_far
    both = a + b
    both = both + both
    base = 3.0 * p13 + 0.5 * (p12 + p23)
    return (both + a) * inverse(base + p12), (both + b) * inverse(base + p23)


def weno_line(f, count):
    values, first, second, third, scaled, terms, jump, ratios = ({} for _ in range(8))

    def need(table, j, make):
        if j not in table:
            table[j] = make(j)
        return table[j]

    def val(j):
        return need(values, j, f)

    def d1(j):
        return need(first, j, lambda k: val(k + 1) - val(k))

    def d2(j):
        return need(second, j, lambda k: d1(k) - d1(k - 1))

    def d3(j):
        return need(third, j, lambda k: d2(k + 1) - d2(k))

    def sc(j):
        return need(scaled, j, lambda k: 1.5 * d2(k))

    def u(j):
        return need(terms, j, lambda k: smooth_terms(d2(k), d2(k + 1), d3(k), sc(k), sc(k + 1)))

    def g(j):
        return need(jump, j, lambda k: d3(k + 1) - d3(k))

    def r(c):
        return need(
            ratios, c, lambda k: side_ratios(u(k - 2)[0], u(k - 1)[1], u(k)[2], g(k - 1), g(k - 2))
        )

    for i in range(count):
        wide = 6.0 * (d1(i) + d1(i - 1))
        left = (wide - (d3(i - 1) + d3(i - 1))) - r(i)[0]
        right = ((d3(i) + d3(i)) - wide) - r(i + 1)[1]
        yield i, left, right


def weno_lanes(f):
    cells = {k: along_lanes(f, k) if k else f for k in range(-3, 3)}
    first = {k: cells[k + 1] - cells[k] for k in range(-3, 2)}
    second = {k: first[k] - first[k - 1] for k in range(-2, 2)}
    third = {k: second[k + 1] - second[k] for k in range(-2, 1)}

    def terms(k):
        return smooth_terms(
            second[k], second[k + 1], third[k], 1.5 * second[k], 1.5 * second[k + 1]
        )

    ratio_left, ratio_right = side_ratios(
        terms(-2)[0], terms(-1)[1], terms(0)[2], third[0] - third[-1], third[-1] - third[-2]
    )
    wide = 6.0 * (first[0] + first[-1])
    left = (wide - (third[-1] + third[-1])) - ratio_left
    right = ((third[0] + third[0]) - wide) - along_lanes(ratio_right, 1)
    return left, right


def upwind_square(left, right, sign):
    return jnp.square(jnp.maximum(jnp.maximum(sign * left, sign * right), 0.0))


def sign_of(value):
    return jnp.where(value > 0, 1.0, -1.0)


def strided(ref, x, start, step):
    return ref[x, pl.ds(start, 8, stride=step), :]


def weno_rates(field, fx, speed, sx, acc, planes, start, step, emit, lanes=None):
    def along_x(t, _):
        row = start + t

        def f(j):
            return strided(field, fx + j, row, step)

        for i, left, right in weno_line(f, planes):
            sign = sign_of(strided(speed, sx + i, row, step))
            acc[i, t] = upwind_square(left, right, sign)
        return _

    lax.fori_loop(0, step, along_x, 0)

    def along_yz(x, _):
        lines = {}

        def f(j):
            if j not in lines:
                lines[j] = strided(field, fx + x, start + j, step)
            return lines[j]

        for t, left, right in weno_line(f, step):
            velocity = strided(speed, sx + x, start + t, step)
            sign = sign_of(velocity)
            total = acc[x, t] + upwind_square(left, right, sign)
            if lanes is None:
                left, right = weno_lanes(f(t))
                total = total + upwind_square(left, right, sign)
            else:
                total = total + strided(lanes, x, start + t, step)
            emit(x, t, velocity * (root(total) * (-1.0 / 12.0)))
        return _

    lax.fori_loop(0, planes, along_yz, 0, unroll=3)


def reinit_sweep(field, fx, origin, ox, planes, start, step, emit):
    def body(x, _):
        lines = {}

        def f(j):
            if j not in lines:
                lines[j] = strided(field, fx + x, start + j, step)
            return lines[j]

        for t in range(step):
            row = start + t
            centre = f(t)
            base = strided(origin, ox + x, row, step)
            sign_field = base * lax.rsqrt(base * base + 1.0)
            sign = sign_of(sign_field)
            total = upwind_square(
                centre - strided(field, fx + x - 1, row, step),
                centre - strided(field, fx + x + 1, row, step),
                sign,
            )
            total = total + upwind_square(centre - f(t - 1), centre - f(t + 1), sign)
            total = total + upwind_square(
                centre - along_lanes(centre, -1), centre - along_lanes(centre, 1), sign
            )
            emit(x, t, centre - pseudo_step * sign_field * (root(total) - 1.0))
        return _

    lax.fori_loop(0, planes, body, 0, unroll=4)


def weigh(stress, materials):
    weight = jnp.where(materials == 0, 1.0, jnp.where(materials == 1, 0.6, 0.0))
    return weight.astype(jnp.float32) * stress


def pack_source(source, before, after, low, high):
    nx, ny, _ = source.shape
    wide = nx + 2 * SRC
    rest = wide * 8
    planes = [before[k] for k in range(SRC)] + [source[k] for k in range(nx)]
    planes = planes + [after[k] for k in range(SRC)]
    for k, plane in enumerate(planes):
        low[k * 8 : k * 8 + 8] = plane[0:8]
        high[k * 8 : k * 8 + 8] = plane[ny - 8 : ny]
        low[rest + k : rest + k + 1] = plane[8:9]
        high[rest + k : rest + k + 1] = plane[ny - 9 : ny - 8]
    tail = low.shape[0] - rest - wide
    low[rest + wide :] = jnp.zeros((tail, 128), jnp.float32)
    high[rest + wide :] = jnp.zeros((tail, 128), jnp.float32)


def pack_level(level, before, after, order, low, high):
    nx, ny, _ = level.shape
    for k in range(nx + 2 * LEV):
        ref, j = (level, k - LEV)
        if k < LEV:
            ref, j = (before, k)
        elif k >= LEV + nx:
            ref, j = (after, k - LEV - nx)
        low[k] = ref[j, 0:8]
        high[k] = ref[j, ny - 8 : ny]


def own_lanes(level, low, high, upper, lower):
    nx, ny, _ = level.shape

    def body(x, _):
        for t in range(0, ny, 8):
            left, right = weno_lanes(level[x, t : t + 8])
            upper[x, t : t + 8] = jnp.square(jnp.maximum(jnp.maximum(left, right), 0.0))
            lower[x, t : t + 8] = jnp.square(jnp.minimum(jnp.minimum(left, right), 0.0))
        return _

    lax.fori_loop(0, nx, body, 0, unroll=2)


def other_lanes(level, speed, upper, lower, lanes):
    nx, ny, _ = upper.shape
    top = OWN + ny

    def outside(x, row):
        left, right = weno_lanes(level[x + LEV - SPD, row : row + 8])
        lanes[x, row : row + 8] = upwind_square(left, right, sign_of(speed[x, row : row + 8]))

    def rows(x, _):
        outside(x, OWN - 8)
        outside(x, top)
        return _

    def ends(x, _):
        for row in range(OWN, top, 8):
            outside(x, row)
            outside(x + SPD + nx, row)
        return _

    def own(x, _):
        positive = speed[SPD + x, OWN:top] > 0
        lanes[SPD + x, OWN:top] = jnp.where(positive, upper[x], lower[x])
        return _

    lax.fori_loop(0, nx + 2 * SPD, rows, 0, unroll=14)
    lax.fori_loop(0, SPD, ends, 0)
    lax.fori_loop(0, nx, own, 0, unroll=2)


def velocity(
    source, before, after, below, above, order, speed, own_speed, peaks, src, one, two
):
    nx, ny, _ = source.shape
    wide = nx + 2 * SRC
    top = OWN + ny
    rest = wide * 8
    for k in range(nx):
        src[SRC + k, OWN:top] = source[k]
    for k in range(SRC):
        src[k, OWN:top] = before[k]
        src[SRC + nx + k, OWN:top] = after[k]
    for k in range(wide):
        src[k, OWN - 8 : OWN] = below[k * 8 : k * 8 + 8]
        src[k, top : top + 8] = above[k * 8 : k * 8 + 8]
        src[k, OWN - 9 : OWN - 8] = below[rest + k : rest + k + 1]
        src[k, top + 8 : top + 9] = above[rest + k : rest + k + 1]
    coefficients = velocity_polynomial()
    step = (ny + 2 * (SRC - 1)) // 8
    start = OWN - (SRC - 1)

    def sweep(old, new, shift, lo, hi, last, constant):
        def body(x, _):
            lines = {}

            def f(j):
                if j not in lines:
                    lines[j] = strided(old, x, start + j, step)
                return lines[j]

            for t in range(step):
                centre = f(t)
                beside = strided(old, x - 1, start + t, step) + strided(old, x + 1, start + t, step)
                beside = beside + (f(t - 1) + f(t + 1))
                beside = beside + (along_lanes(centre, 1) + along_lanes(centre, -1))
                if last is not None:
                    beside = last * beside
                own = centre if old is src else strided(src, x, start + t, step)
                new[x - shift, pl.ds(start + t, 8, stride=step), :] = beside + constant * own
            return _

        lax.fori_loop(lo, hi, body, 0, unroll=11)

    sweep(src, one, 0, 1, wide - 1, coefficients[4], coefficients[3])
    sweep(one, two, 0, 2, wide - 2, None, coefficients[2])
    sweep(two, one, 0, 3, wide - 3, None, coefficients[1])
    sweep(one, speed, SRC - SPD, 4, wide - 4, None, coefficients[0])

    def largest(x, carry):
        mine = speed[SPD + x, OWN : OWN + ny]
        own_speed[x] = mine
        return jnp.maximum(carry, jnp.abs(mine))

    top = lax.fori_loop(0, nx, largest, jnp.zeros((ny, 128), jnp.float32))
    peaks[...] = jnp.broadcast_to(jnp.max(top), peaks.shape)


def evolve(
    own_level, before, after, below, above, speed, upper, lower, peaks, new_level,
    level, rate, lanes, stage, advected, swept, acc,
):
    nx, ny, _ = new_level.shape
    tall = nx + 2 * LEV
    top = OWN + ny
    for k in range(nx):
        level[LEV + k, OWN:top] = own_level[k]
    for k in range(LEV):
        level[k, OWN:top] = before[k]
        level[LEV + nx + k, OWN:top] = after[k]
    for k in range(tall):
        level[k, OWN - 8 : OWN] = below[k]
        level[k, top : top + 8] = above[k]

    def emit_rate(x, t, value):
        rate[x, pl.ds(OWN - SPD + t, 8, stride=10), :] = value

    other_lanes(level, speed, upper, lower, lanes)
    weno_rates(level, LEV - SPD, speed, 0, acc, nx + 2 * SPD, OWN - SPD, 10, emit_rate, lanes)

    peak = jnp.max(peaks[...], axis=0, keepdims=True)
    time_step = courant / (peak + 1e-06)
    step_row = jnp.broadcast_to(time_step, (8, 128))
    step_rows = jnp.broadcast_to(time_step, (ROWS - 8, 128))

    def advance(x, _):
        stage[x, 8:ROWS] = level[x + LEV - SPD, 8:ROWS] + step_rows * rate[x, 8:ROWS]
        return _

    lax.fori_loop(0, stage.shape[0], advance, 0)

    start, step = OWN - 2, 9

    def emit(x, t, value):
        row = start + t
        after = strided(stage, x + SPD - 2, row, step) + step_row * value
        before = strided(level, x + LEV - 2, row, step)
        advected[x, pl.ds(row, 8, stride=step), :] = 0.5 * before + 0.5 * after

    weno_rates(stage, SPD - 2, speed, SPD - 2, acc, nx + 4, start, step, emit)

    def emit_one(x, t, value):
        swept[x, pl.ds(OWN - 1 + t, 8, stride=9), :] = value

    reinit_sweep(advected, 1, advected, 1, nx + 2, OWN - 1, 9, emit_one)

    def emit_two(x, t, value):
        new_level[x, pl.ds(t, 8, stride=ny // 8), :] = value

    reinit_sweep(swept, 1, advected, 2, nx, OWN, ny // 8, emit_two)


BIG = 32
VM = pl.BlockSpec(memory_space=pltpu.VMEM)
ANY = pl.BlockSpec(memory_space=pl.ANY)


def call(kernel, outs, scratch, args, megabytes):
    ins = [a if isinstance(a, tuple) else (a, VM) for a in args]
    return pl.pallas_call(
        kernel,
        out_shape=[jax.ShapeDtypeStruct(shape, jnp.float32) for shape in outs],
        in_specs=[place for _, place in ins],
        out_specs=[VM] * len(outs),
        scratch_shapes=[pltpu.VMEM(shape, jnp.float32) for shape in scratch],
        compiler_params=pltpu.CompilerParams(vmem_limit_bytes=megabytes * 1024 * 1024),
    )(*[array for array, _ in ins])


def local(level_set, stress_jump, materials):
    tile = level_set.shape
    nx, ny, nz = tile
    wide, tall, mid = nx + 2 * SRC, nx + 2 * LEV, nx + 2 * SPD
    size_x, size_y = lax.axis_size("gx"), lax.axis_size("gy")
    devices = size_x * size_y

    def shift(value, axis, size, by):
        return lax.ppermute(value, axis, [(i, (i + by) % size) for i in range(size)])

    low = weigh(stress_jump[:SRC], materials[:SRC])
    high = weigh(stress_jump[nx - SRC :], materials[nx - SRC :])
    source_after = shift(low, "gx", size_x, -1)
    source_before = shift(high, "gx", size_x, 1)
    source = weigh(stress_jump, materials)
    upper, lower = call(own_lanes, [tile, tile], [], (level_set, (low, ANY), (high, ANY)), 8)
    level_low, level_high, upper, lower, source = lax.optimization_barrier(
        (level_set[:LEV], level_set[nx - LEV :], upper, lower, source)
    )
    level_after = shift(level_low, "gx", size_x, -1)
    level_before = shift(level_high, "gx", size_x, 1)
    message = (wide * 8 + (wide + 7) // 8 * 8, nz)
    low, high = call(
        pack_source, [message, message], [], (source, source_before, source_after), 8
    )
    source_above = shift(low, "gy", size_y, -1)
    source_below = shift(high, "gy", size_y, 1)
    message = (tall, 8, nz)
    low, high = call(
        pack_level,
        [message, message],
        [],
        (level_set, level_before, level_after, (low, ANY)),
        8,
    )
    level_above = shift(low, "gy", size_y, -1)
    level_below = shift(high, "gy", size_y, 1)
    speed, normal_speed, peaks = call(
        velocity,
        [(mid, ROWS, nz), tile, (devices, nz)],
        [(wide, ROWS, nz)] * 3,
        (source, source_before, source_after, source_below, source_above, (low, ANY)),
        BIG,
    )
    peaks, level_above, level_below = lax.optimization_barrier((peaks, level_above, level_below))
    peaks = lax.all_to_all(peaks.reshape(devices, 1, nz), ("gx", "gy"), 0, 0)
    (new_level,) = call(
        evolve,
        [tile],
        [
            (tall, ROWS, nz),
            (mid, ROWS, nz),
            (mid, ROWS, nz),
            (mid, ROWS, nz),
            (nx + 4, ROWS, nz),
            (nx + 2, ROWS, nz),
            (mid, 10, 8, nz),
        ],
        (
            level_set,
            level_before,
            level_after,
            level_below,
            level_above,
            speed,
            upper,
            lower,
            peaks.reshape(devices, nz),
        ),
        BIG,
    )
    return (new_level, normal_speed)


def solution(mesh):
    in_specs = (P("gx", "gy", None), P("gx", "gy", None), P("gx", "gy", None))
    out_specs = (P("gx", "gy", None), P("gx", "gy", None))
    return jax.shard_map(local, mesh=mesh, in_specs=in_specs, out_specs=out_specs, check_vma=False)
```

```python
import jax
import jax.numpy as jnp
import numpy as np
from jax import lax
from jax.experimental import pallas as pl
from jax.experimental.pallas import tpu as pltpu
from jax.sharding import PartitionSpec as P

SWEEPS = 4
REINIT = 2

screening = 0.1
spectral_mid = screening + 6.0
spectral_half = 6.0
courant = 0.25
pseudo_step = 0.25
weno_floor = 1e-06

OWN = 16
ROWS = 96
SRC = 9
LEV = 8
SPD = 5


def velocity_polynomial():
    times = np.array([0.0, 1.0])
    add = np.polynomial.polynomial.polyadd
    mul = np.polynomial.polynomial.polymul
    operator = add([spectral_mid], -times)
    ratio_now = spectral_half / spectral_mid
    iterate, residue, search = np.array([0.0]), np.array([1.0]), np.array([1.0 / spectral_mid])
    for _ in range(SWEEPS):
        applied = mul(operator, search)
        iterate = add(iterate, search)
        residue = add(residue, -applied)
        ratio_next = 1.0 / (2.0 * spectral_mid / spectral_half - ratio_now)
        search = add(ratio_next * ratio_now * search, 2.0 * ratio_next / spectral_half * residue)
        ratio_now = ratio_next
    return [float(c) for c in add(iterate, search)]


def along_lanes(value, k):
    return pltpu.roll(value, (-k) % value.shape[1], axis=1)


def inverse(x):
    return pl.reciprocal(x, approx=True)


def root(x):
    return x * lax.rsqrt(jnp.maximum(x, 1.2e-38))


def smooth_terms(second, second_next, third, scaled, scaled_next):
    twice = third + third
    middle = (third * twice + (1.5 * weno_floor)) + scaled * second_next
    return middle + scaled_next * twice, middle, middle - scaled * twice


def side_ratios(u1, u2, u3, jump_near, jump_far):
    p12 = jnp.square(u1 * u2)
    p13 = jnp.square(u1 * u3)
    p23 = jnp.square(u2 * u3)
    a = p12 * jump_near
    b = p23 * jump_far
    both = a + b
    both = both + both
    base = 3.0 * p13 + 0.5 * (p12 + p23)
    return (both + a) * inverse(base + p12), (both + b) * inverse(base + p23)


def weno_line(f, count):
    values, first, second, third, scaled, terms, jump, ratios = ({} for _ in range(8))

    def need(table, j, make):
        if j not in table:
            table[j] = make(j)
        return table[j]

    def val(j):
        return need(values, j, f)

    def d1(j):
        return need(first, j, lambda k: val(k + 1) - val(k))

    def d2(j):
        return need(second, j, lambda k: d1(k) - d1(k - 1))

    def d3(j):
        return need(third, j, lambda k: d2(k + 1) - d2(k))

    def sc(j):
        return need(scaled, j, lambda k: 1.5 * d2(k))

    def u(j):
        return need(terms, j, lambda k: smooth_terms(d2(k), d2(k + 1), d3(k), sc(k), sc(k + 1)))

    def g(j):
        return need(jump, j, lambda k: d3(k + 1) - d3(k))

    def r(c):
        return need(
            ratios, c, lambda k: side_ratios(u(k - 2)[0], u(k - 1)[1], u(k)[2], g(k - 1), g(k - 2))
        )

    for i in range(count):
        wide = 6.0 * (d1(i) + d1(i - 1))
        left = (wide - (d3(i - 1) + d3(i - 1))) - r(i)[0]
        right = ((d3(i) + d3(i)) - wide) - r(i + 1)[1]
        yield i, left, right


def weno_lanes(f):
    cells = {k: along_lanes(f, k) if k else f for k in range(-3, 3)}
    first = {k: cells[k + 1] - cells[k] for k in range(-3, 2)}
    second = {k: first[k] - first[k - 1] for k in range(-2, 2)}
    third = {k: second[k + 1] - second[k] for k in range(-2, 1)}

    def terms(k):
        return smooth_terms(
            second[k], second[k + 1], third[k], 1.5 * second[k], 1.5 * second[k + 1]
        )

    ratio_left, ratio_right = side_ratios(
        terms(-2)[0], terms(-1)[1], terms(0)[2], third[0] - third[-1], third[-1] - third[-2]
    )
    wide = 6.0 * (first[0] + first[-1])
    left = (wide - (third[-1] + third[-1])) - ratio_left
    right = ((third[0] + third[0]) - wide) - along_lanes(ratio_right, 1)
    return left, right


def upwind_square(left, right, sign):
    return jnp.square(jnp.maximum(jnp.maximum(sign * left, sign * right), 0.0))


def sign_of(value):
    return jnp.where(value > 0, 1.0, -1.0)


def strided(ref, x, start, step):
    return ref[x, pl.ds(start, 8, stride=step), :]


def weno_rates(field, fx, speed, sx, acc, planes, start, step, emit, lanes=None):
    def along_x(t, _):
        row = start + t

        def f(j):
            return strided(field, fx + j, row, step)

        for i, left, right in weno_line(f, planes):
            sign = sign_of(strided(speed, sx + i, row, step))
            acc[i, t] = upwind_square(left, right, sign)
        return _

    lax.fori_loop(0, step, along_x, 0)

    def along_yz(x, _):
        lines = {}

        def f(j):
            if j not in lines:
                lines[j] = strided(field, fx + x, start + j, step)
            return lines[j]

        for t, left, right in weno_line(f, step):
            velocity = strided(speed, sx + x, start + t, step)
            sign = sign_of(velocity)
            total = acc[x, t] + upwind_square(left, right, sign)
            if lanes is None:
                left, right = weno_lanes(f(t))
                total = total + upwind_square(left, right, sign)
            else:
                total = total + strided(lanes, x, start + t, step)
            emit(x, t, velocity * (root(total) * (-1.0 / 12.0)))
        return _

    lax.fori_loop(0, planes, along_yz, 0, unroll=3)


def reinit_sweep(field, fx, origin, ox, planes, start, step, emit):
    def body(x, _):
        lines = {}

        def f(j):
            if j not in lines:
                lines[j] = strided(field, fx + x, start + j, step)
            return lines[j]

        for t in range(step):
            row = start + t
            centre = f(t)
            base = strided(origin, ox + x, row, step)
            sign_field = base * lax.rsqrt(base * base + 1.0)
            sign = sign_of(sign_field)
            total = upwind_square(
                centre - strided(field, fx + x - 1, row, step),
                centre - strided(field, fx + x + 1, row, step),
                sign,
            )
            total = total + upwind_square(centre - f(t - 1), centre - f(t + 1), sign)
            total = total + upwind_square(
                centre - along_lanes(centre, -1), centre - along_lanes(centre, 1), sign
            )
            emit(x, t, centre - pseudo_step * sign_field * (root(total) - 1.0))
        return _

    lax.fori_loop(0, planes, body, 0, unroll=4)


def weigh(stress, materials):
    weight = jnp.where(materials == 0, 1.0, jnp.where(materials == 1, 0.6, 0.0))
    return weight.astype(jnp.float32) * stress


def pack_source(source, before, after, order, low, high):
    nx, ny, _ = source.shape
    wide = nx + 2 * SRC
    rest = wide * 8
    planes = [before[k] for k in range(SRC)] + [source[k] for k in range(nx)]
    planes = planes + [after[k] for k in range(SRC)]
    for k, plane in enumerate(planes):
        low[k * 8 : k * 8 + 8] = plane[0:8]
        high[k * 8 : k * 8 + 8] = plane[ny - 8 : ny]
        low[rest + k : rest + k + 1] = plane[8:9]
        high[rest + k : rest + k + 1] = plane[ny - 9 : ny - 8]
    tail = low.shape[0] - rest - wide
    low[rest + wide :] = jnp.zeros((tail, 128), jnp.float32)
    high[rest + wide :] = jnp.zeros((tail, 128), jnp.float32)


def pack_level(level, below, above, order, low, high):
    nx, ny, _ = level.shape
    for k in range(LEV):
        for ref, j in ((low, k), (high, nx - LEV + k)):
            ref[k, 0:8] = below[j]
            ref[k, 8 : 8 + ny] = level[j]
            ref[k, 8 + ny : 16 + ny] = above[j]


def own_lanes(level, low, high, upper, lower):
    nx, ny, _ = level.shape

    def body(x, _):
        for t in range(0, ny, 8):
            left, right = weno_lanes(level[x, t : t + 8])
            upper[x, t : t + 8] = jnp.square(jnp.maximum(jnp.maximum(left, right), 0.0))
            lower[x, t : t + 8] = jnp.square(jnp.minimum(jnp.minimum(left, right), 0.0))
        return _

    lax.fori_loop(0, nx, body, 0, unroll=2)


def other_lanes(level, speed, upper, lower, lanes):
    nx, ny, _ = upper.shape
    top = OWN + ny

    def outside(x, row):
        left, right = weno_lanes(level[x + LEV - SPD, row : row + 8])
        lanes[x, row : row + 8] = upwind_square(left, right, sign_of(speed[x, row : row + 8]))

    def rows(x, _):
        outside(x, OWN - 8)
        outside(x, top)
        return _

    def ends(x, _):
        for row in range(OWN, top, 8):
            outside(x, row)
            outside(x + SPD + nx, row)
        return _

    def own(x, _):
        positive = speed[SPD + x, OWN:top] > 0
        lanes[SPD + x, OWN:top] = jnp.where(positive, upper[x], lower[x])
        return _

    lax.fori_loop(0, nx + 2 * SPD, rows, 0, unroll=14)
    lax.fori_loop(0, SPD, ends, 0)
    lax.fori_loop(0, nx, own, 0, unroll=2)


def velocity(
    source, before, after, below, above, order, speed, own_speed, peaks, src, one, two
):
    nx, ny, _ = source.shape
    wide = nx + 2 * SRC
    top = OWN + ny
    rest = wide * 8
    for k in range(nx):
        src[SRC + k, OWN:top] = source[k]
    for k in range(SRC):
        src[k, OWN:top] = before[k]
        src[SRC + nx + k, OWN:top] = after[k]
    for k in range(wide):
        src[k, OWN - 8 : OWN] = below[k * 8 : k * 8 + 8]
        src[k, top : top + 8] = above[k * 8 : k * 8 + 8]
        src[k, OWN - 9 : OWN - 8] = below[rest + k : rest + k + 1]
        src[k, top + 8 : top + 9] = above[rest + k : rest + k + 1]
    coefficients = velocity_polynomial()
    step = (ny + 2 * (SRC - 1)) // 8
    start = OWN - (SRC - 1)

    def sweep(old, new, shift, lo, hi, last, constant):
        def body(x, _):
            lines = {}

            def f(j):
                if j not in lines:
                    lines[j] = strided(old, x, start + j, step)
                return lines[j]

            for t in range(step):
                centre = f(t)
                beside = strided(old, x - 1, start + t, step) + strided(old, x + 1, start + t, step)
                beside = beside + (f(t - 1) + f(t + 1))
                beside = beside + (along_lanes(centre, 1) + along_lanes(centre, -1))
                if last is not None:
                    beside = last * beside
                own = centre if old is src else strided(src, x, start + t, step)
                new[x - shift, pl.ds(start + t, 8, stride=step), :] = beside + constant * own
            return _

        lax.fori_loop(lo, hi, body, 0, unroll=11)

    sweep(src, one, 0, 1, wide - 1, coefficients[4], coefficients[3])
    sweep(one, two, 0, 2, wide - 2, None, coefficients[2])
    sweep(two, one, 0, 3, wide - 3, None, coefficients[1])
    sweep(one, speed, SRC - SPD, 4, wide - 4, None, coefficients[0])

    def largest(x, carry):
        mine = speed[SPD + x, OWN : OWN + ny]
        own_speed[x] = mine
        return jnp.maximum(carry, jnp.abs(mine))

    top = lax.fori_loop(0, nx, largest, jnp.zeros((ny, 128), jnp.float32))
    peaks[...] = jnp.broadcast_to(jnp.max(top), peaks.shape)


def evolve(
    own_level, before, after, below, above, speed, upper, lower, peaks, new_level,
    level, rate, lanes, stage, advected, swept, acc,
):
    nx, ny, _ = new_level.shape
    top = OWN + ny
    for k in range(nx):
        level[LEV + k, OWN:top] = own_level[k]
        level[LEV + k, OWN - 8 : OWN] = below[k]
        level[LEV + k, top : top + 8] = above[k]
    for k in range(LEV):
        level[k, OWN - 8 : top + 8] = before[k]
        level[LEV + nx + k, OWN - 8 : top + 8] = after[k]

    def emit_rate(x, t, value):
        rate[x, pl.ds(OWN - SPD + t, 8, stride=10), :] = value

    other_lanes(level, speed, upper, lower, lanes)
    weno_rates(level, LEV - SPD, speed, 0, acc, nx + 2 * SPD, OWN - SPD, 10, emit_rate, lanes)

    peak = jnp.max(peaks[...], axis=0, keepdims=True)
    time_step = courant / (peak + 1e-06)
    step_row = jnp.broadcast_to(time_step, (8, 128))
    step_rows = jnp.broadcast_to(time_step, (ROWS - 8, 128))

    def advance(x, _):
        stage[x, 8:ROWS] = level[x + LEV - SPD, 8:ROWS] + step_rows * rate[x, 8:ROWS]
        return _

    lax.fori_loop(0, stage.shape[0], advance, 0)

    start, step = OWN - 2, 9

    def emit(x, t, value):
        row = start + t
        after = strided(stage, x + SPD - 2, row, step) + step_row * value
        before = strided(level, x + LEV - 2, row, step)
        advected[x, pl.ds(row, 8, stride=step), :] = 0.5 * before + 0.5 * after

    weno_rates(stage, SPD - 2, speed, SPD - 2, acc, nx + 4, start, step, emit)

    def emit_one(x, t, value):
        swept[x, pl.ds(OWN - 1 + t, 8, stride=9), :] = value

    reinit_sweep(advected, 1, advected, 1, nx + 2, OWN - 1, 9, emit_one)

    def emit_two(x, t, value):
        new_level[x, pl.ds(t, 8, stride=ny // 8), :] = value

    reinit_sweep(swept, 1, advected, 2, nx, OWN, ny // 8, emit_two)


BIG = 32
VM = pl.BlockSpec(memory_space=pltpu.VMEM)
ANY = pl.BlockSpec(memory_space=pl.ANY)


def call(kernel, outs, scratch, args, megabytes, weight=None):
    ins = [a if isinstance(a, tuple) else (a, VM) for a in args]
    return pl.pallas_call(
        kernel,
        out_shape=[jax.ShapeDtypeStruct(shape, jnp.float32) for shape in outs],
        in_specs=[place for _, place in ins],
        out_specs=[VM] * len(outs),
        scratch_shapes=[pltpu.VMEM(shape, jnp.float32) for shape in scratch],
        cost_estimate=weight
        and pl.CostEstimate(flops=0, bytes_accessed=weight, transcendentals=0),
        compiler_params=pltpu.CompilerParams(vmem_limit_bytes=megabytes * 1024 * 1024),
    )(*[array for array, _ in ins])


def local(level_set, stress_jump, materials):
    tile = level_set.shape
    nx, ny, nz = tile
    wide, tall, mid = nx + 2 * SRC, nx + 2 * LEV, nx + 2 * SPD
    size_x, size_y = lax.axis_size("gx"), lax.axis_size("gy")
    devices = size_x * size_y

    def shift(value, axis, size, by):
        return lax.ppermute(value, axis, [(i, (i + by) % size) for i in range(size)])

    low = weigh(stress_jump[:SRC], materials[:SRC])
    high = weigh(stress_jump[nx - SRC :], materials[nx - SRC :])
    source_after = shift(low, "gx", size_x, -1)
    source_before = shift(high, "gx", size_x, 1)
    source = weigh(stress_jump, materials)
    level_low, level_high, _, _ = lax.optimization_barrier(
        (level_set[:, :8], level_set[:, ny - 8 :], low, high)
    )
    level_above = shift(level_low, "gy", size_y, -1)
    level_below = shift(level_high, "gy", size_y, 1)
    upper, lower = call(
        own_lanes, [tile, tile], [], (level_set, (level_low, ANY), (level_high, ANY)), 8
    )
    message = (wide * 8 + (wide + 7) // 8 * 8, nz)
    low, high = call(
        pack_source,
        [message, message],
        [],
        (source, source_before, source_after, (upper, ANY)),
        8,
    )
    source_above = shift(low, "gy", size_y, -1)
    source_below = shift(high, "gy", size_y, 1)
    message = (LEV, ny + 16, nz)
    low, high = call(
        pack_level,
        [message, message],
        [],
        (level_set, level_below, level_above, (low, ANY)),
        8,
    )
    level_after = shift(low, "gx", size_x, -1)
    level_before = shift(high, "gx", size_x, 1)
    speed, normal_speed, peaks = call(
        velocity,
        [(mid, ROWS, nz), tile, (devices, nz)],
        [(wide, ROWS, nz)] * 3,
        (source, source_before, source_after, source_below, source_above, (low, ANY)),
        BIG,
        weight=60_000_000,
    )
    peaks, level_before, level_after = lax.optimization_barrier((peaks, level_before, level_after))
    peaks = lax.all_to_all(peaks.reshape(devices, 1, nz), ("gx", "gy"), 0, 0)
    (new_level,) = call(
        evolve,
        [tile],
        [
            (tall, ROWS, nz),
            (mid, ROWS, nz),
            (mid, ROWS, nz),
            (mid, ROWS, nz),
            (nx + 4, ROWS, nz),
            (nx + 2, ROWS, nz),
            (mid, 10, 8, nz),
        ],
        (
            level_set,
            level_before,
            level_after,
            level_below,
            level_above,
            speed,
            upper,
            lower,
            peaks.reshape(devices, nz),
        ),
        BIG,
    )
    return (new_level, normal_speed)


def solution(mesh):
    in_specs = (P("gx", "gy", None), P("gx", "gy", None), P("gx", "gy", None))
    out_specs = (P("gx", "gy", None), P("gx", "gy", None))
    return jax.shard_map(local, mesh=mesh, in_specs=in_specs, out_specs=out_specs, check_vma=False)
```

```python
import jax
import jax.numpy as jnp
import numpy as np
from jax import lax
from jax.experimental import pallas as pl
from jax.experimental.pallas import tpu as pltpu
from jax.sharding import PartitionSpec as P

SWEEPS = 4
REINIT = 2

screening = 0.1
spectral_mid = screening + 6.0
spectral_half = 6.0
courant = 0.25
pseudo_step = 0.25
weno_floor = 1e-06

OWN = 16
ROWS = 96
SRC = 9
LEV = 8
SPD = 5


def velocity_polynomial():
    times = np.array([0.0, 1.0])
    add = np.polynomial.polynomial.polyadd
    mul = np.polynomial.polynomial.polymul
    operator = add([spectral_mid], -times)
    ratio_now = spectral_half / spectral_mid
    iterate, residue, search = np.array([0.0]), np.array([1.0]), np.array([1.0 / spectral_mid])
    for _ in range(SWEEPS):
        applied = mul(operator, search)
        iterate = add(iterate, search)
        residue = add(residue, -applied)
        ratio_next = 1.0 / (2.0 * spectral_mid / spectral_half - ratio_now)
        search = add(ratio_next * ratio_now * search, 2.0 * ratio_next / spectral_half * residue)
        ratio_now = ratio_next
    return [float(c) for c in add(iterate, search)]


def along_lanes(value, k):
    return pltpu.roll(value, (-k) % value.shape[1], axis=1)


def inverse(x):
    return pl.reciprocal(x, approx=True)


def root(x):
    return x * lax.rsqrt(jnp.maximum(x, 1.2e-38))


def smooth_terms(second, second_next, third, scaled, scaled_next):
    twice = third + third
    middle = (third * twice + (1.5 * weno_floor)) + scaled * second_next
    return middle + scaled_next * twice, middle, middle - scaled * twice


def side_ratios(u1, u2, u3, jump_near, jump_far):
    p12 = jnp.square(u1 * u2)
    p13 = jnp.square(u1 * u3)
    p23 = jnp.square(u2 * u3)
    a = p12 * jump_near
    b = p23 * jump_far
    both = a + b
    both = both + both
    base = 3.0 * p13 + 0.5 * (p12 + p23)
    return (both + a) * inverse(base + p12), (both + b) * inverse(base + p23)


def weno_line(f, count):
    values, first, second, third, scaled, terms, jump, ratios = ({} for _ in range(8))

    def need(table, j, make):
        if j not in table:
            table[j] = make(j)
        return table[j]

    def val(j):
        return need(values, j, f)

    def d1(j):
        return need(first, j, lambda k: val(k + 1) - val(k))

    def d2(j):
        return need(second, j, lambda k: d1(k) - d1(k - 1))

    def d3(j):
        return need(third, j, lambda k: d2(k + 1) - d2(k))

    def sc(j):
        return need(scaled, j, lambda k: 1.5 * d2(k))

    def u(j):
        return need(terms, j, lambda k: smooth_terms(d2(k), d2(k + 1), d3(k), sc(k), sc(k + 1)))

    def g(j):
        return need(jump, j, lambda k: d3(k + 1) - d3(k))

    def r(c):
        return need(
            ratios, c, lambda k: side_ratios(u(k - 2)[0], u(k - 1)[1], u(k)[2], g(k - 1), g(k - 2))
        )

    for i in range(count):
        wide = 6.0 * (d1(i) + d1(i - 1))
        left = (wide - (d3(i - 1) + d3(i - 1))) - r(i)[0]
        right = ((d3(i) + d3(i)) - wide) - r(i + 1)[1]
        yield i, left, right


def weno_lanes(f):
    cells = {k: along_lanes(f, k) if k else f for k in range(-3, 3)}
    first = {k: cells[k + 1] - cells[k] for k in range(-3, 2)}
    second = {k: first[k] - first[k - 1] for k in range(-2, 2)}
    third = {k: second[k + 1] - second[k] for k in range(-2, 1)}

    def terms(k):
        return smooth_terms(
            second[k], second[k + 1], third[k], 1.5 * second[k], 1.5 * second[k + 1]
        )

    ratio_left, ratio_right = side_ratios(
        terms(-2)[0], terms(-1)[1], terms(0)[2], third[0] - third[-1], third[-1] - third[-2]
    )
    wide = 6.0 * (first[0] + first[-1])
    left = (wide - (third[-1] + third[-1])) - ratio_left
    right = ((third[0] + third[0]) - wide) - along_lanes(ratio_right, 1)
    return left, right


def upwind_square(left, right, sign):
    return jnp.square(jnp.maximum(jnp.maximum(sign * left, sign * right), 0.0))


def sign_of(value):
    return jnp.where(value > 0, 1.0, -1.0)


def strided(ref, x, start, step):
    return ref[x, pl.ds(start, 8, stride=step), :]


def weno_rates(field, fx, speed, sx, acc, planes, start, step, emit, lanes=None):
    def along_x(t, _):
        row = start + t

        def f(j):
            return strided(field, fx + j, row, step)

        for i, left, right in weno_line(f, planes):
            sign = sign_of(strided(speed, sx + i, row, step))
            acc[i, t] = upwind_square(left, right, sign)
        return _

    lax.fori_loop(0, step, along_x, 0)

    def along_yz(x, _):
        lines = {}

        def f(j):
            if j not in lines:
                lines[j] = strided(field, fx + x, start + j, step)
            return lines[j]

        for t, left, right in weno_line(f, step):
            velocity = strided(speed, sx + x, start + t, step)
            sign = sign_of(velocity)
            total = acc[x, t] + upwind_square(left, right, sign)
            if lanes is None:
                left, right = weno_lanes(f(t))
                total = total + upwind_square(left, right, sign)
            else:
                total = total + strided(lanes, x, start + t, step)
            emit(x, t, velocity * (root(total) * (-1.0 / 12.0)))
        return _

    lax.fori_loop(0, planes, along_yz, 0, unroll=3)


def reinit_sweep(field, fx, origin, ox, planes, start, step, emit):
    def body(x, _):
        lines = {}

        def f(j):
            if j not in lines:
                lines[j] = strided(field, fx + x, start + j, step)
            return lines[j]

        for t in range(step):
            row = start + t
            centre = f(t)
            base = strided(origin, ox + x, row, step)
            sign_field = base * lax.rsqrt(base * base + 1.0)
            sign = sign_of(sign_field)
            total = upwind_square(
                centre - strided(field, fx + x - 1, row, step),
                centre - strided(field, fx + x + 1, row, step),
                sign,
            )
            total = total + upwind_square(centre - f(t - 1), centre - f(t + 1), sign)
            total = total + upwind_square(
                centre - along_lanes(centre, -1), centre - along_lanes(centre, 1), sign
            )
            emit(x, t, centre - pseudo_step * sign_field * (root(total) - 1.0))
        return _

    lax.fori_loop(0, planes, body, 0, unroll=4)


def weigh(stress, materials):
    weight = jnp.where(materials == 0, 1.0, jnp.where(materials == 1, 0.6, 0.0))
    return weight.astype(jnp.float32) * stress


def pack_source(source, before, after, order, low, high):
    nx, ny, _ = source.shape
    wide = nx + 2 * SRC
    rest = wide * 8
    planes = [before[k] for k in range(SRC)] + [source[k] for k in range(nx)]
    planes = planes + [after[k] for k in range(SRC)]
    for k, plane in enumerate(planes):
        low[k * 8 : k * 8 + 8] = plane[0:8]
        high[k * 8 : k * 8 + 8] = plane[ny - 8 : ny]
        low[rest + k : rest + k + 1] = plane[8:9]
        high[rest + k : rest + k + 1] = plane[ny - 9 : ny - 8]
    tail = low.shape[0] - rest - wide
    low[rest + wide :] = jnp.zeros((tail, 128), jnp.float32)
    high[rest + wide :] = jnp.zeros((tail, 128), jnp.float32)


def pack_level(level, before, after, order, low, high):
    nx, ny, _ = level.shape
    for k in range(nx + 2 * LEV):
        ref, j = (level, k - LEV)
        if k < LEV:
            ref, j = (before, k)
        elif k >= LEV + nx:
            ref, j = (after, k - LEV - nx)
        low[k] = ref[j, 0:8]
        high[k] = ref[j, ny - 8 : ny]


def own_lanes(level, low, high, upper, lower):
    nx, ny, _ = level.shape

    def body(x, _):
        for t in range(0, ny, 8):
            left, right = weno_lanes(level[x, t : t + 8])
            upper[x, t : t + 8] = jnp.square(jnp.maximum(jnp.maximum(left, right), 0.0))
            lower[x, t : t + 8] = jnp.square(jnp.minimum(jnp.minimum(left, right), 0.0))
        return _

    lax.fori_loop(0, nx, body, 0, unroll=2)


def other_lanes(level, speed, upper, lower, lanes):
    nx, ny, _ = upper.shape
    top = OWN + ny

    def outside(x, row):
        left, right = weno_lanes(level[x + LEV - SPD, row : row + 8])
        lanes[x, row : row + 8] = upwind_square(left, right, sign_of(speed[x, row : row + 8]))

    def rows(x, _):
        outside(x, OWN - 8)
        outside(x, top)
        return _

    def ends(x, _):
        for row in range(OWN, top, 8):
            outside(x, row)
            outside(x + SPD + nx, row)
        return _

    def own(x, _):
        positive = speed[SPD + x, OWN:top] > 0
        lanes[SPD + x, OWN:top] = jnp.where(positive, upper[x], lower[x])
        return _

    lax.fori_loop(0, nx + 2 * SPD, rows, 0, unroll=14)
    lax.fori_loop(0, SPD, ends, 0)
    lax.fori_loop(0, nx, own, 0, unroll=2)


def velocity(
    source, before, after, below, above, order, speed, own_speed, peaks, src, one, two
):
    nx, ny, _ = source.shape
    wide = nx + 2 * SRC
    top = OWN + ny
    rest = wide * 8
    for k in range(nx):
        src[SRC + k, OWN:top] = source[k]
    for k in range(SRC):
        src[k, OWN:top] = before[k]
        src[SRC + nx + k, OWN:top] = after[k]
    for k in range(wide):
        src[k, OWN - 8 : OWN] = below[k * 8 : k * 8 + 8]
        src[k, top : top + 8] = above[k * 8 : k * 8 + 8]
        src[k, OWN - 9 : OWN - 8] = below[rest + k : rest + k + 1]
        src[k, top + 8 : top + 9] = above[rest + k : rest + k + 1]
    coefficients = velocity_polynomial()
    step = (ny + 2 * (SRC - 1)) // 8
    start = OWN - (SRC - 1)

    def sweep(old, new, shift, lo, hi, last, constant):
        def body(x, _):
            lines = {}

            def f(j):
                if j not in lines:
                    lines[j] = strided(old, x, start + j, step)
                return lines[j]

            for t in range(step):
                centre = f(t)
                beside = strided(old, x - 1, start + t, step) + strided(old, x + 1, start + t, step)
                beside = beside + (f(t - 1) + f(t + 1))
                beside = beside + (along_lanes(centre, 1) + along_lanes(centre, -1))
                if last is not None:
                    beside = last * beside
                own = centre if old is src else strided(src, x, start + t, step)
                new[x - shift, pl.ds(start + t, 8, stride=step), :] = beside + constant * own
            return _

        lax.fori_loop(lo, hi, body, 0, unroll=11)

    sweep(src, one, 0, 1, wide - 1, coefficients[4], coefficients[3])
    sweep(one, two, 0, 2, wide - 2, None, coefficients[2])
    sweep(two, one, 0, 3, wide - 3, None, coefficients[1])
    sweep(one, speed, SRC - SPD, 4, wide - 4, None, coefficients[0])

    def largest(x, carry):
        mine = speed[SPD + x, OWN : OWN + ny]
        own_speed[x] = mine
        return jnp.maximum(carry, jnp.abs(mine))

    top = lax.fori_loop(0, nx, largest, jnp.zeros((ny, 128), jnp.float32))
    peaks[...] = jnp.broadcast_to(jnp.max(top), peaks.shape)


def evolve(
    own_level, before, after, below, above, speed, upper, lower, peaks, new_level,
    level, rate, lanes, stage, advected, swept, acc,
):
    nx, ny, _ = new_level.shape
    tall = nx + 2 * LEV
    top = OWN + ny
    for k in range(nx):
        level[LEV + k, OWN:top] = own_level[k]
    for k in range(LEV):
        level[k, OWN:top] = before[k]
        level[LEV + nx + k, OWN:top] = after[k]
    for k in range(tall):
        level[k, OWN - 8 : OWN] = below[k]
        level[k, top : top + 8] = above[k]

    def emit_rate(x, t, value):
        rate[x, pl.ds(OWN - SPD + t, 8, stride=10), :] = value

    other_lanes(level, speed, upper, lower, lanes)
    weno_rates(level, LEV - SPD, speed, 0, acc, nx + 2 * SPD, OWN - SPD, 10, emit_rate, lanes)

    peak = jnp.max(peaks[...], axis=0, keepdims=True)
    time_step = courant / (peak + 1e-06)
    step_row = jnp.broadcast_to(time_step, (8, 128))
    step_rows = jnp.broadcast_to(time_step, (ROWS - 8, 128))

    def advance(x, _):
        stage[x, 8:ROWS] = level[x + LEV - SPD, 8:ROWS] + step_rows * rate[x, 8:ROWS]
        return _

    lax.fori_loop(0, stage.shape[0], advance, 0)

    start, step = OWN - 2, 9

    def emit(x, t, value):
        row = start + t
        after = strided(stage, x + SPD - 2, row, step) + step_row * value
        before = strided(level, x + LEV - 2, row, step)
        advected[x, pl.ds(row, 8, stride=step), :] = 0.5 * before + 0.5 * after

    weno_rates(stage, SPD - 2, speed, SPD - 2, acc, nx + 4, start, step, emit)

    def emit_one(x, t, value):
        swept[x, pl.ds(OWN - 1 + t, 8, stride=9), :] = value

    reinit_sweep(advected, 1, advected, 1, nx + 2, OWN - 1, 9, emit_one)

    def emit_two(x, t, value):
        new_level[x, pl.ds(t, 8, stride=ny // 8), :] = value

    reinit_sweep(swept, 1, advected, 2, nx, OWN, ny // 8, emit_two)


BIG = 32
VM = pl.BlockSpec(memory_space=pltpu.VMEM)
ANY = pl.BlockSpec(memory_space=pl.ANY)


def call(kernel, outs, scratch, args, megabytes):
    ins = [a if isinstance(a, tuple) else (a, VM) for a in args]
    return pl.pallas_call(
        kernel,
        out_shape=[jax.ShapeDtypeStruct(shape, jnp.float32) for shape in outs],
        in_specs=[place for _, place in ins],
        out_specs=[VM] * len(outs),
        scratch_shapes=[pltpu.VMEM(shape, jnp.float32) for shape in scratch],
        compiler_params=pltpu.CompilerParams(vmem_limit_bytes=megabytes * 1024 * 1024),
    )(*[array for array, _ in ins])


def local(level_set, stress_jump, materials):
    tile = level_set.shape
    nx, ny, nz = tile
    wide, tall, mid = nx + 2 * SRC, nx + 2 * LEV, nx + 2 * SPD
    size_x, size_y = lax.axis_size("gx"), lax.axis_size("gy")
    devices = size_x * size_y

    def shift(value, axis, size, by):
        return lax.ppermute(value, axis, [(i, (i + by) % size) for i in range(size)])

    low = weigh(stress_jump[:SRC], materials[:SRC])
    high = weigh(stress_jump[nx - SRC :], materials[nx - SRC :])
    source_after = shift(low, "gx", size_x, -1)
    source_before = shift(high, "gx", size_x, 1)
    source = weigh(stress_jump, materials)
    level_low, level_high, _, _ = lax.optimization_barrier(
        (level_set[:LEV], level_set[nx - LEV :], low, high)
    )
    level_after = shift(level_low, "gx", size_x, -1)
    level_before = shift(level_high, "gx", size_x, 1)
    upper, lower = call(
        own_lanes, [tile, tile], [], (level_set, (level_low, ANY), (level_high, ANY)), 8
    )
    message = (wide * 8 + (wide + 7) // 8 * 8, nz)
    low, high = call(
        pack_source, [message, message], [], (source, source_before, source_after, (upper, ANY)), 8
    )
    source_above = shift(low, "gy", size_y, -1)
    source_below = shift(high, "gy", size_y, 1)
    message = (tall, 8, nz)
    low, high = call(
        pack_level,
        [message, message],
        [],
        (level_set, level_before, level_after, (low, ANY)),
        8,
    )
    level_above = shift(low, "gy", size_y, -1)
    level_below = shift(high, "gy", size_y, 1)
    speed, normal_speed, peaks = call(
        velocity,
        [(mid, ROWS, nz), tile, (devices, nz)],
        [(wide, ROWS, nz)] * 3,
        (source, source_before, source_after, source_below, source_above, (low, ANY)),
        BIG,
    )
    peaks, level_above, level_below = lax.optimization_barrier((peaks, level_above, level_below))
    peaks = lax.all_to_all(peaks.reshape(devices, 1, nz), ("gx", "gy"), 0, 0)
    (new_level,) = call(
        evolve,
        [tile],
        [
            (tall, ROWS, nz),
            (mid, ROWS, nz),
            (mid, ROWS, nz),
            (mid, ROWS, nz),
            (nx + 4, ROWS, nz),
            (nx + 2, ROWS, nz),
            (mid, 10, 8, nz),
        ],
        (
            level_set,
            level_before,
            level_after,
            level_below,
            level_above,
            speed,
            upper,
            lower,
            peaks.reshape(devices, nz),
        ),
        BIG,
    )
    return (new_level, normal_speed)


def solution(mesh):
    in_specs = (P("gx", "gy", None), P("gx", "gy", None), P("gx", "gy", None))
    out_specs = (P("gx", "gy", None), P("gx", "gy", None))
    return jax.shard_map(local, mesh=mesh, in_specs=in_specs, out_specs=out_specs, check_vma=False)
```

```python
import jax
import jax.numpy as jnp
import numpy as np
from jax import lax
from jax.experimental import pallas as pl
from jax.experimental.pallas import tpu as pltpu
from jax.sharding import PartitionSpec as P

SWEEPS = 4
REINIT = 2

screening = 0.1
spectral_mid = screening + 6.0
spectral_half = 6.0
courant = 0.25
pseudo_step = 0.25
weno_floor = 1e-06

OWN = 16
ROWS = 96
SRC = 9
LEV = 8
SPD = 5
GROUP = 16
ROW_GROUPS = 6


def velocity_polynomial():
    times = np.array([0.0, 1.0])
    add = np.polynomial.polynomial.polyadd
    mul = np.polynomial.polynomial.polymul
    operator = add([spectral_mid], -times)
    ratio_now = spectral_half / spectral_mid
    iterate, residue, search = np.array([0.0]), np.array([1.0]), np.array([1.0 / spectral_mid])
    for _ in range(SWEEPS):
        applied = mul(operator, search)
        iterate = add(iterate, search)
        residue = add(residue, -applied)
        ratio_next = 1.0 / (2.0 * spectral_mid / spectral_half - ratio_now)
        search = add(ratio_next * ratio_now * search, 2.0 * ratio_next / spectral_half * residue)
        ratio_now = ratio_next
    return [float(c) for c in add(iterate, search)]


def along_lanes(value, k):
    return pltpu.roll(value, (-k) % value.shape[1], axis=1)


def inverse(x):
    return pl.reciprocal(x, approx=True)


def root(x):
    return x * lax.rsqrt(jnp.maximum(x, 1.2e-38))


def smooth_terms(second, second_next, third, scaled, scaled_next):
    twice = third + third
    middle = (third * twice + (1.5 * weno_floor)) + scaled * second_next
    return middle + scaled_next * twice, middle, middle - scaled * twice


def side_ratios(u1, u2, u3, jump_near, jump_far):
    p12 = jnp.square(u1 * u2)
    p13 = jnp.square(u1 * u3)
    p23 = jnp.square(u2 * u3)
    a = p12 * jump_near
    b = p23 * jump_far
    both = a + b
    both = both + both
    base = 3.0 * p13 + 0.5 * (p12 + p23)
    return (both + a) * inverse(base + p12), (both + b) * inverse(base + p23)


def weno_line(f, count):
    values, first, second, third, scaled, terms, jump, ratios = ({} for _ in range(8))

    def need(table, j, make):
        if j not in table:
            table[j] = make(j)
        return table[j]

    def val(j):
        return need(values, j, f)

    def d1(j):
        return need(first, j, lambda k: val(k + 1) - val(k))

    def d2(j):
        return need(second, j, lambda k: d1(k) - d1(k - 1))

    def d3(j):
        return need(third, j, lambda k: d2(k + 1) - d2(k))

    def sc(j):
        return need(scaled, j, lambda k: 1.5 * d2(k))

    def u(j):
        return need(terms, j, lambda k: smooth_terms(d2(k), d2(k + 1), d3(k), sc(k), sc(k + 1)))

    def g(j):
        return need(jump, j, lambda k: d3(k + 1) - d3(k))

    def r(c):
        return need(
            ratios, c, lambda k: side_ratios(u(k - 2)[0], u(k - 1)[1], u(k)[2], g(k - 1), g(k - 2))
        )

    for i in range(count):
        wide = 6.0 * (d1(i) + d1(i - 1))
        left = (wide - (d3(i - 1) + d3(i - 1))) - r(i)[0]
        right = ((d3(i) + d3(i)) - wide) - r(i + 1)[1]
        yield i, left, right


SHIFTS = (-3, -2, -1, 1, 2)


def piped(groups, tiles, load, compute, buffers):
    def fill(buffer, g):
        for j in range(tiles):
            f = load(g, j)
            for n, k in enumerate(SHIFTS):
                buffer[n, j] = along_lanes(f, k)

    fill(buffers[0], 0)

    def body(p, _):
        for parity in range(2):
            g = 2 * p + parity
            fill(buffers[1 - parity], jnp.minimum(g + 1, groups - 1))
            for j in range(tiles):
                cells = {k: buffers[parity][n, j] for n, k in enumerate(SHIFTS)}
                cells[0] = load(g, j)
                compute(g, j, cells)
        return _

    lax.fori_loop(0, groups // 2, body, 0)


def weno_lanes(cells):
    first = {k: cells[k + 1] - cells[k] for k in range(-3, 2)}
    second = {k: first[k] - first[k - 1] for k in range(-2, 2)}
    third = {k: second[k + 1] - second[k] for k in range(-2, 1)}

    def terms(k):
        return smooth_terms(
            second[k], second[k + 1], third[k], 1.5 * second[k], 1.5 * second[k + 1]
        )

    ratio_left, ratio_right = side_ratios(
        terms(-2)[0], terms(-1)[1], terms(0)[2], third[0] - third[-1], third[-1] - third[-2]
    )
    wide = 6.0 * (first[0] + first[-1])
    left = (wide - (third[-1] + third[-1])) - ratio_left
    right = ((third[0] + third[0]) - wide) - along_lanes(ratio_right, 1)
    return left, right


def upwind_square(left, right, sign):
    return jnp.square(jnp.maximum(jnp.maximum(sign * left, sign * right), 0.0))


def sign_of(value):
    return jnp.where(value > 0, 1.0, -1.0)


def strided(ref, x, start, step):
    return ref[x, pl.ds(start, 8, stride=step), :]


def weno_rates(field, fx, speed, sx, acc, planes, start, step, emit, lanes=None, buffers=None):
    def along_x(t, _):
        row = start + t

        def f(j):
            return strided(field, fx + j, row, step)

        for i, left, right in weno_line(f, planes):
            sign = sign_of(strided(speed, sx + i, row, step))
            acc[i, t] = upwind_square(left, right, sign)
        return _

    lax.fori_loop(0, step, along_x, 0)

    def finish(x, t, total):
        velocity = strided(speed, sx + x, start + t, step)
        emit(x, t, velocity * (root(total) * (-1.0 / 12.0)))

    def along_y(x, _):
        lines = {}

        def f(j):
            if j not in lines:
                lines[j] = strided(field, fx + x, start + j, step)
            return lines[j]

        for t, left, right in weno_line(f, step):
            sign = sign_of(strided(speed, sx + x, start + t, step))
            total = acc[x, t] + upwind_square(left, right, sign)
            if lanes is None:
                acc[x, t] = total
            else:
                finish(x, t, total + strided(lanes, x, start + t, step))
        return _

    def along_yz(p, _):
        for parity in range(2):
            x = 2 * p + parity
            after = jnp.minimum(x + 1, planes - 1)
            for t in range(step):
                g = strided(field, fx + after, start + t, step)
                for n, k in enumerate(SHIFTS):
                    buffers[1 - parity][n, t] = along_lanes(g, k)
            lines = {}

            def f(j):
                if j not in lines:
                    lines[j] = strided(field, fx + x, start + j, step)
                return lines[j]

            for t, left, right in weno_line(f, step):
                sign = sign_of(strided(speed, sx + x, start + t, step))
                total = acc[x, t] + upwind_square(left, right, sign)
                cells = {k: buffers[parity][n, t] for n, k in enumerate(SHIFTS)}
                cells[0] = f(t)
                left, right = weno_lanes(cells)
                finish(x, t, total + upwind_square(left, right, sign))
        return _

    if lanes is None:
        for t in range(step):
            g = strided(field, fx, start + t, step)
            for n, k in enumerate(SHIFTS):
                buffers[0][n, t] = along_lanes(g, k)
        lax.fori_loop(0, planes // 2, along_yz, 0)
    else:
        lax.fori_loop(0, planes, along_y, 0, unroll=3)


def reinit_sweep(field, fx, origin, ox, planes, start, step, emit):
    def body(x, _):
        lines = {}

        def f(j):
            if j not in lines:
                lines[j] = strided(field, fx + x, start + j, step)
            return lines[j]

        for t in range(step):
            row = start + t
            centre = f(t)
            base = strided(origin, ox + x, row, step)
            sign_field = base * lax.rsqrt(base * base + 1.0)
            sign = sign_of(sign_field)
            total = upwind_square(
                centre - strided(field, fx + x - 1, row, step),
                centre - strided(field, fx + x + 1, row, step),
                sign,
            )
            total = total + upwind_square(centre - f(t - 1), centre - f(t + 1), sign)
            total = total + upwind_square(
                centre - along_lanes(centre, -1), centre - along_lanes(centre, 1), sign
            )
            emit(x, t, centre - pseudo_step * sign_field * (root(total) - 1.0))
        return _

    lax.fori_loop(0, planes, body, 0, unroll=4)


def weigh(stress, materials):
    weight = jnp.where(materials == 0, 1.0, jnp.where(materials == 1, 0.6, 0.0))
    return weight.astype(jnp.float32) * stress


def pack_source(source, before, after, order, low, high):
    nx, ny, _ = source.shape
    wide = nx + 2 * SRC
    rest = wide * 8
    planes = [before[k] for k in range(SRC)] + [source[k] for k in range(nx)]
    planes = planes + [after[k] for k in range(SRC)]
    for k, plane in enumerate(planes):
        low[k * 8 : k * 8 + 8] = plane[0:8]
        high[k * 8 : k * 8 + 8] = plane[ny - 8 : ny]
        low[rest + k : rest + k + 1] = plane[8:9]
        high[rest + k : rest + k + 1] = plane[ny - 9 : ny - 8]
    tail = low.shape[0] - rest - wide
    low[rest + wide :] = jnp.zeros((tail, 128), jnp.float32)
    high[rest + wide :] = jnp.zeros((tail, 128), jnp.float32)


def pack_level(level, before, after, order, low, high):
    nx, ny, _ = level.shape
    for k in range(nx + 2 * LEV):
        ref, j = (level, k - LEV)
        if k < LEV:
            ref, j = (before, k)
        elif k >= LEV + nx:
            ref, j = (after, k - LEV - nx)
        low[k] = ref[j, 0:8]
        high[k] = ref[j, ny - 8 : ny]


def own_lanes(level, low, high, upper, lower, *buffers):
    nx, ny, _ = level.shape
    rows = ny // 8

    def tile(g, j):
        return g * (GROUP // rows) + j // rows, slice(j % rows * 8, j % rows * 8 + 8)

    def compute(g, j, cells):
        left, right = weno_lanes(cells)
        upper[tile(g, j)] = jnp.square(jnp.maximum(jnp.maximum(left, right), 0.0))
        lower[tile(g, j)] = jnp.square(jnp.minimum(jnp.minimum(left, right), 0.0))

    piped(nx * rows // GROUP, GROUP, lambda g, j: level[tile(g, j)], compute, buffers)


def other_lanes(level, speed, upper, lower, lanes, buffers):
    nx, ny, _ = upper.shape
    top = OWN + ny

    def outside(groups, tiles, tile):
        def load(g, j):
            x, row = tile(g, j)
            return level[x + LEV - SPD, row : row + 8]

        def compute(g, j, cells):
            x, row = tile(g, j)
            left, right = weno_lanes(cells)
            sign = sign_of(speed[x, row : row + 8])
            lanes[x, row : row + 8] = upwind_square(left, right, sign)

        piped(groups, tiles, load, compute, buffers)

    planes = nx + 2 * SPD
    outside(ROW_GROUPS, 2 * planes // ROW_GROUPS, lambda g, j: (g * (planes // ROW_GROUPS) + j // 2, (OWN - 8, top)[j % 2]))
    rows = ny // 8
    outside(
        2 * SPD, rows, lambda g, j: (g + jnp.where(g < SPD, 0, nx), OWN + 8 * j)
    )

    def own(x, _):
        positive = speed[SPD + x, OWN:top] > 0
        lanes[SPD + x, OWN:top] = jnp.where(positive, upper[x], lower[x])
        return _

    lax.fori_loop(0, nx, own, 0, unroll=2)


def velocity(
    source, before, after, below, above, order, speed, own_speed, peaks, src, one, two, sem
):
    nx, ny, _ = source.shape
    wide = nx + 2 * SRC
    top = OWN + ny
    rest = wide * 8
    for k in range(nx):
        src[SRC + k, OWN:top] = source[k]
    for k in range(SRC):
        src[k, OWN:top] = before[k]
        src[SRC + nx + k, OWN:top] = after[k]
    for k in range(wide):
        src[k, OWN - 8 : OWN] = below[k * 8 : k * 8 + 8]
        src[k, top : top + 8] = above[k * 8 : k * 8 + 8]
        src[k, OWN - 9 : OWN - 8] = below[rest + k : rest + k + 1]
        src[k, top + 8 : top + 9] = above[rest + k : rest + k + 1]
    coefficients = velocity_polynomial()
    step = (ny + 2 * (SRC - 1)) // 8
    start = OWN - (SRC - 1)

    def sweep(old, new, shift, lo, hi, last, constant):
        def body(x, _):
            lines = {}

            def f(j):
                if j not in lines:
                    lines[j] = strided(old, x, start + j, step)
                return lines[j]

            for t in range(step):
                centre = f(t)
                beside = strided(old, x - 1, start + t, step) + strided(old, x + 1, start + t, step)
                beside = beside + (f(t - 1) + f(t + 1))
                beside = beside + (along_lanes(centre, 1) + along_lanes(centre, -1))
                if last is not None:
                    beside = last * beside
                own = centre if old is src else strided(src, x, start + t, step)
                new[x - shift, pl.ds(start + t, 8, stride=step), :] = beside + constant * own
            return _

        lax.fori_loop(lo, hi, body, 0, unroll=11)

    sweep(src, one, 0, 1, wide - 1, coefficients[4], coefficients[3])
    sweep(one, two, 0, 2, wide - 2, None, coefficients[2])
    sweep(two, one, 0, 3, wide - 3, None, coefficients[1])
    sweep(one, speed, SRC - SPD, 4, wide - 4, None, coefficients[0])

    leaving = pltpu.make_async_copy(
        speed.at[pl.ds(SPD, nx), pl.ds(OWN, ny)], own_speed, sem.at[0]
    )
    leaving.start()

    def largest(x, carry):
        return jnp.maximum(carry, jnp.abs(speed[SPD + x, OWN : OWN + ny]))

    top = lax.fori_loop(0, nx, largest, jnp.zeros((ny, 128), jnp.float32))
    peaks[...] = jnp.broadcast_to(jnp.max(top), peaks.shape)
    leaving.wait()


def evolve(
    own_level, before, after, below, above, speed, upper, lower, peaks, new_level,
    level, rate, lanes, stage, advected, swept, acc, even, odd, result, sems,
):
    nx, ny, _ = new_level.shape
    tall = nx + 2 * LEV
    buffers = (even, odd)
    top = OWN + ny
    for k in range(nx):
        level[LEV + k, OWN:top] = own_level[k]
    for k in range(LEV):
        level[k, OWN:top] = before[k]
        level[LEV + nx + k, OWN:top] = after[k]
    for k in range(tall):
        level[k, OWN - 8 : OWN] = below[k]
        level[k, top : top + 8] = above[k]

    def emit_rate(x, t, value):
        rate[x, pl.ds(OWN - SPD + t, 8, stride=10), :] = value

    other_lanes(level, speed, upper, lower, lanes, buffers)
    weno_rates(level, LEV - SPD, speed, 0, acc, nx + 2 * SPD, OWN - SPD, 10, emit_rate, lanes)

    peak = jnp.max(peaks[...], axis=0, keepdims=True)
    time_step = courant / (peak + 1e-06)
    step_row = jnp.broadcast_to(time_step, (8, 128))
    step_rows = jnp.broadcast_to(time_step, (ROWS - 8, 128))

    def advance(x, _):
        stage[x, 8:ROWS] = level[x + LEV - SPD, 8:ROWS] + step_rows * rate[x, 8:ROWS]
        return _

    lax.fori_loop(0, stage.shape[0], advance, 0)

    start, step = OWN - 2, 9

    def emit(x, t, value):
        row = start + t
        after = strided(stage, x + SPD - 2, row, step) + step_row * value
        before = strided(level, x + LEV - 2, row, step)
        advected[x, pl.ds(row, 8, stride=step), :] = 0.5 * before + 0.5 * after

    weno_rates(stage, SPD - 2, speed, SPD - 2, acc, nx + 4, start, step, emit, None, buffers)

    def emit_one(x, t, value):
        swept[x, pl.ds(OWN - 1 + t, 8, stride=9), :] = value

    reinit_sweep(advected, 1, advected, 1, nx + 2, OWN - 1, 9, emit_one)

    part = nx // PARTS
    leaving = []
    for n in range(PARTS):
        first = n * part

        def emit_two(x, t, value):
            result[first + x, pl.ds(t, 8, stride=ny // 8), :] = value

        reinit_sweep(swept, 1 + first, advected, 2 + first, part, OWN, ny // 8, emit_two)
        planes = pl.ds(first, part)
        leaving.append(
            pltpu.make_async_copy(result.at[planes], new_level.at[planes], sems.at[n])
        )
        leaving[n].start()
    for copy in leaving:
        copy.wait()


PARTS = 4
BIG = 32
VM = pl.BlockSpec(memory_space=pltpu.VMEM)
ANY = pl.BlockSpec(memory_space=pl.ANY)


def call(kernel, outs, scratch, args, megabytes, copies=0):
    ins = [a if isinstance(a, tuple) else (a, VM) for a in args]
    outs = [o if isinstance(o[0], tuple) else (o, VM) for o in outs]
    scratch = [pltpu.VMEM(shape, jnp.float32) for shape in scratch]
    if copies:
        scratch.append(pltpu.SemaphoreType.DMA((copies,)))
    return pl.pallas_call(
        kernel,
        out_shape=[jax.ShapeDtypeStruct(shape, jnp.float32) for shape, _ in outs],
        in_specs=[place for _, place in ins],
        out_specs=[place for _, place in outs],
        scratch_shapes=scratch,
        compiler_params=pltpu.CompilerParams(vmem_limit_bytes=megabytes * 1024 * 1024),
    )(*[array for array, _ in ins])


def local(level_set, stress_jump, materials):
    tile = level_set.shape
    nx, ny, nz = tile
    wide, tall, mid = nx + 2 * SRC, nx + 2 * LEV, nx + 2 * SPD
    size_x, size_y = lax.axis_size("gx"), lax.axis_size("gy")
    devices = size_x * size_y

    def shift(value, axis, size, by):
        return lax.ppermute(value, axis, [(i, (i + by) % size) for i in range(size)])

    low = weigh(stress_jump[:SRC], materials[:SRC])
    high = weigh(stress_jump[nx - SRC :], materials[nx - SRC :])
    source_after = shift(low, "gx", size_x, -1)
    source_before = shift(high, "gx", size_x, 1)
    source = weigh(stress_jump, materials)
    level_low, level_high, _, _ = lax.optimization_barrier(
        (level_set[:LEV], level_set[nx - LEV :], low, high)
    )
    level_after = shift(level_low, "gx", size_x, -1)
    level_before = shift(level_high, "gx", size_x, 1)
    upper, lower = call(
        own_lanes, [tile, tile], [(5, GROUP, 8, nz)] * 2, (level_set, (level_low, ANY), (level_high, ANY)), 8
    )
    message = (wide * 8 + (wide + 7) // 8 * 8, nz)
    low, high = call(
        pack_source, [message, message], [], (source, source_before, source_after, (upper, ANY)), 8
    )
    source_above = shift(low, "gy", size_y, -1)
    source_below = shift(high, "gy", size_y, 1)
    message = (tall, 8, nz)
    low, high = call(
        pack_level,
        [message, message],
        [],
        (level_set, level_before, level_after, (low, ANY)),
        8,
    )
    level_above = shift(low, "gy", size_y, -1)
    level_below = shift(high, "gy", size_y, 1)
    speed, normal_speed, peaks = call(
        velocity,
        [(mid, ROWS, nz), (tile, ANY), (devices, nz)],
        [(wide, ROWS, nz)] * 3,
        (source, source_before, source_after, source_below, source_above, (low, ANY)),
        BIG,
        copies=1,
    )
    peaks, level_above, level_below = lax.optimization_barrier((peaks, level_above, level_below))
    peaks = lax.all_to_all(peaks.reshape(devices, 1, nz), ("gx", "gy"), 0, 0)
    (new_level,) = call(
        evolve,
        [(tile, ANY)],
        [
            (tall, ROWS, nz),
            (mid, ROWS, nz),
            (mid, ROWS, nz),
            (mid, ROWS, nz),
            (nx + 4, ROWS, nz),
            (nx + 2, ROWS, nz),
            (mid, 10, 8, nz),
        ]
        + [(5, GROUP, 8, nz)] * 2
        + [tile],
        (
            level_set,
            level_before,
            level_after,
            level_below,
            level_above,
            speed,
            upper,
            lower,
            peaks.reshape(devices, nz),
        ),
        BIG,
        copies=PARTS,
    )
    return (new_level, normal_speed)


def solution(mesh):
    in_specs = (P("gx", "gy", None), P("gx", "gy", None), P("gx", "gy", None))
    out_specs = (P("gx", "gy", None), P("gx", "gy", None))
    return jax.shard_map(local, mesh=mesh, in_specs=in_specs, out_specs=out_specs, check_vma=False)
```

```python
import jax
import jax.numpy as jnp
import numpy as np
from jax import lax
from jax.experimental import pallas as pl
from jax.experimental.pallas import tpu as pltpu
from jax.sharding import PartitionSpec as P

SWEEPS = 4
REINIT = 2

screening = 0.1
spectral_mid = screening + 6.0
spectral_half = 6.0
courant = 0.25
pseudo_step = 0.25
weno_floor = 1e-06

OWN = 16
ROWS = 96
SRC = 9
LEV = 8
SPD = 5
GROUP = 16
ROW_GROUPS = 6


def velocity_polynomial():
    times = np.array([0.0, 1.0])
    add = np.polynomial.polynomial.polyadd
    mul = np.polynomial.polynomial.polymul
    operator = add([spectral_mid], -times)
    ratio_now = spectral_half / spectral_mid
    iterate, residue, search = np.array([0.0]), np.array([1.0]), np.array([1.0 / spectral_mid])
    for _ in range(SWEEPS):
        applied = mul(operator, search)
        iterate = add(iterate, search)
        residue = add(residue, -applied)
        ratio_next = 1.0 / (2.0 * spectral_mid / spectral_half - ratio_now)
        search = add(ratio_next * ratio_now * search, 2.0 * ratio_next / spectral_half * residue)
        ratio_now = ratio_next
    return [float(c) for c in add(iterate, search)]


def along_lanes(value, k):
    return pltpu.roll(value, (-k) % value.shape[1], axis=1)


def inverse(x):
    return pl.reciprocal(x, approx=True)


def root(x):
    return x * lax.rsqrt(jnp.maximum(x, 1.2e-38))


def smooth_terms(second, second_next, third, scaled, scaled_next):
    twice = third + third
    middle = (third * twice + (1.5 * weno_floor)) + scaled * second_next
    return middle + scaled_next * twice, middle, middle - scaled * twice


def side_ratios(u1, u2, u3, jump_near, jump_far):
    p12 = jnp.square(u1 * u2)
    p13 = jnp.square(u1 * u3)
    p23 = jnp.square(u2 * u3)
    a = p12 * jump_near
    b = p23 * jump_far
    both = a + b
    both = both + both
    base = 3.0 * p13 + 0.5 * (p12 + p23)
    return (both + a) * inverse(base + p12), (both + b) * inverse(base + p23)


def weno_line(f, count):
    values, first, second, third, scaled, terms, jump, ratios = ({} for _ in range(8))

    def need(table, j, make):
        if j not in table:
            table[j] = make(j)
        return table[j]

    def val(j):
        return need(values, j, f)

    def d1(j):
        return need(first, j, lambda k: val(k + 1) - val(k))

    def d2(j):
        return need(second, j, lambda k: d1(k) - d1(k - 1))

    def d3(j):
        return need(third, j, lambda k: d2(k + 1) - d2(k))

    def sc(j):
        return need(scaled, j, lambda k: 1.5 * d2(k))

    def u(j):
        return need(terms, j, lambda k: smooth_terms(d2(k), d2(k + 1), d3(k), sc(k), sc(k + 1)))

    def g(j):
        return need(jump, j, lambda k: d3(k + 1) - d3(k))

    def r(c):
        return need(
            ratios, c, lambda k: side_ratios(u(k - 2)[0], u(k - 1)[1], u(k)[2], g(k - 1), g(k - 2))
        )

    for i in range(count):
        wide = 6.0 * (d1(i) + d1(i - 1))
        left = (wide - (d3(i - 1) + d3(i - 1))) - r(i)[0]
        right = ((d3(i) + d3(i)) - wide) - r(i + 1)[1]
        yield i, left, right


SHIFTS = (-3, -2, -1, 1, 2)


def piped(groups, tiles, load, compute, buffers):
    def fill(buffer, g):
        for j in range(tiles):
            f = load(g, j)
            for n, k in enumerate(SHIFTS):
                buffer[n, j] = along_lanes(f, k)

    fill(buffers[0], 0)

    def body(p, _):
        for parity in range(2):
            g = 2 * p + parity
            fill(buffers[1 - parity], jnp.minimum(g + 1, groups - 1))
            for j in range(tiles):
                cells = {k: buffers[parity][n, j] for n, k in enumerate(SHIFTS)}
                cells[0] = load(g, j)
                compute(g, j, cells)
        return _

    lax.fori_loop(0, groups // 2, body, 0)


def weno_lanes(cells):
    first = {k: cells[k + 1] - cells[k] for k in range(-3, 2)}
    second = {k: first[k] - first[k - 1] for k in range(-2, 2)}
    third = {k: second[k + 1] - second[k] for k in range(-2, 1)}

    def terms(k):
        return smooth_terms(
            second[k], second[k + 1], third[k], 1.5 * second[k], 1.5 * second[k + 1]
        )

    ratio_left, ratio_right = side_ratios(
        terms(-2)[0], terms(-1)[1], terms(0)[2], third[0] - third[-1], third[-1] - third[-2]
    )
    wide = 6.0 * (first[0] + first[-1])
    left = (wide - (third[-1] + third[-1])) - ratio_left
    right = ((third[0] + third[0]) - wide) - along_lanes(ratio_right, 1)
    return left, right


def upwind_square(left, right, sign):
    return jnp.square(jnp.maximum(jnp.maximum(sign * left, sign * right), 0.0))


def sign_of(value):
    return jnp.where(value > 0, 1.0, -1.0)


def strided(ref, x, start, step):
    return ref[x, pl.ds(start, 8, stride=step), :]


def weno_rates(field, fx, speed, sx, acc, planes, start, step, emit, lanes=None, buffers=None):
    def along_x(t, _):
        row = start + t

        def f(j):
            return strided(field, fx + j, row, step)

        for i, left, right in weno_line(f, planes):
            sign = sign_of(strided(speed, sx + i, row, step))
            acc[i, t] = upwind_square(left, right, sign)
        return _

    if lanes is None:
        lax.fori_loop(0, step, along_x, 0)

    def finish(x, t, total):
        velocity = strided(speed, sx + x, start + t, step)
        emit(x, t, velocity * (root(total) * (-1.0 / 12.0)))

    def along_y(x, _):
        lines = {}

        def f(j):
            if j not in lines:
                lines[j] = strided(field, fx + x, start + j, step)
            return lines[j]

        for t, left, right in weno_line(f, step):
            sign = sign_of(strided(speed, sx + x, start + t, step))
            total = upwind_square(left, right, sign)
            finish(x, t, total + strided(lanes, x, start + t, step))
        return _

    def along_yz(p, _):
        for parity in range(2):
            x = 2 * p + parity
            after = jnp.minimum(x + 1, planes - 1)
            for t in range(step):
                g = strided(field, fx + after, start + t, step)
                for n, k in enumerate(SHIFTS):
                    buffers[1 - parity][n, t] = along_lanes(g, k)
            lines = {}

            def f(j):
                if j not in lines:
                    lines[j] = strided(field, fx + x, start + j, step)
                return lines[j]

            for t, left, right in weno_line(f, step):
                sign = sign_of(strided(speed, sx + x, start + t, step))
                total = acc[x, t] + upwind_square(left, right, sign)
                cells = {k: buffers[parity][n, t] for n, k in enumerate(SHIFTS)}
                cells[0] = f(t)
                left, right = weno_lanes(cells)
                finish(x, t, total + upwind_square(left, right, sign))
        return _

    if lanes is None:
        for t in range(step):
            g = strided(field, fx, start + t, step)
            for n, k in enumerate(SHIFTS):
                buffers[0][n, t] = along_lanes(g, k)
        lax.fori_loop(0, planes // 2, along_yz, 0)
    else:
        lax.fori_loop(0, planes, along_y, 0, unroll=3)


def reinit_sweep(field, fx, origin, ox, planes, start, step, emit):
    def body(x, _):
        lines = {}

        def f(j):
            if j not in lines:
                lines[j] = strided(field, fx + x, start + j, step)
            return lines[j]

        for t in range(step):
            row = start + t
            centre = f(t)
            base = strided(origin, ox + x, row, step)
            sign_field = base * lax.rsqrt(base * base + 1.0)
            sign = sign_of(base)
            signed = sign * centre

            def climb(low, high):
                lowest = jnp.minimum(sign * low, sign * high)
                return jnp.square(jnp.maximum(signed - lowest, 0.0))

            total = climb(
                strided(field, fx + x - 1, row, step), strided(field, fx + x + 1, row, step)
            )
            total = total + climb(f(t - 1), f(t + 1))
            total = total + climb(along_lanes(centre, -1), along_lanes(centre, 1))
            emit(x, t, centre - pseudo_step * sign_field * (root(total) - 1.0))
        return _

    lax.fori_loop(0, planes, body, 0, unroll=4)


def weigh(stress, materials):
    weight = jnp.where(materials == 0, 1.0, jnp.where(materials == 1, 0.6, 0.0))
    return weight.astype(jnp.float32) * stress


def pack_source(source, before, after, order, low, high):
    nx, ny, _ = source.shape
    wide = nx + 2 * SRC
    rest = wide * 8
    planes = [before[k] for k in range(SRC)] + [source[k] for k in range(nx)]
    planes = planes + [after[k] for k in range(SRC)]
    for k, plane in enumerate(planes):
        low[k * 8 : k * 8 + 8] = plane[0:8]
        high[k * 8 : k * 8 + 8] = plane[ny - 8 : ny]
        low[rest + k : rest + k + 1] = plane[8:9]
        high[rest + k : rest + k + 1] = plane[ny - 9 : ny - 8]
    tail = low.shape[0] - rest - wide
    low[rest + wide :] = jnp.zeros((tail, 128), jnp.float32)
    high[rest + wide :] = jnp.zeros((tail, 128), jnp.float32)


def pack_level(level, before, after, order, low, high):
    nx, ny, _ = level.shape
    for k in range(nx + 2 * LEV):
        ref, j = (level, k - LEV)
        if k < LEV:
            ref, j = (before, k)
        elif k >= LEV + nx:
            ref, j = (after, k - LEV - nx)
        low[k] = ref[j, 0:8]
        high[k] = ref[j, ny - 8 : ny]


def own_lanes(level, low, high, upper, lower, *buffers):
    nx, ny, _ = level.shape
    rows = ny // 8

    def tile(g, j):
        return g * (GROUP // rows) + j // rows, slice(j % rows * 8, j % rows * 8 + 8)

    def compute(g, j, cells):
        left, right = weno_lanes(cells)
        upper[tile(g, j)] = jnp.square(jnp.maximum(jnp.maximum(left, right), 0.0))
        lower[tile(g, j)] = jnp.square(jnp.minimum(jnp.minimum(left, right), 0.0))

    piped(nx * rows // GROUP, GROUP, lambda g, j: level[tile(g, j)], compute, buffers)

    def inner(n, _):
        at = pl.ds(pl.multiple_of(n * 8, 8), 8)
        for i, left, right in weno_line(lambda j: level[3 + j, at], nx - 6):
            high = jnp.square(jnp.maximum(jnp.maximum(left, right), 0.0))
            low_square = jnp.square(jnp.minimum(jnp.minimum(left, right), 0.0))
            upper[3 + i, at] = upper[3 + i, at] + high
            lower[3 + i, at] = lower[3 + i, at] + low_square
        return _

    lax.fori_loop(0, rows, inner, 0)


def other_lanes(level, speed, upper, lower, lanes, buffers):
    nx, ny, _ = upper.shape
    top = OWN + ny

    def outside(groups, tiles, tile):
        def load(g, j):
            x, row = tile(g, j)
            return level[x + LEV - SPD, row : row + 8]

        def compute(g, j, cells):
            x, row = tile(g, j)
            left, right = weno_lanes(cells)
            sign = sign_of(speed[x, row : row + 8])
            lanes[x, row : row + 8] = upwind_square(left, right, sign)

        piped(groups, tiles, load, compute, buffers)

    planes = nx + 2 * SPD
    outside(ROW_GROUPS, 2 * planes // ROW_GROUPS, lambda g, j: (g * (planes // ROW_GROUPS) + j // 2, (OWN - 8, top)[j % 2]))
    rows = ny // 8
    outside(
        2 * SPD, rows, lambda g, j: (g + jnp.where(g < SPD, 0, nx), OWN + 8 * j)
    )

    def own(x, _):
        positive = speed[SPD + x, OWN:top] > 0
        lanes[SPD + x, OWN:top] = jnp.where(positive, upper[x], lower[x])
        return _

    lax.fori_loop(0, nx, own, 0, unroll=2)

    def add_x(first, count, at):
        for i, left, right in weno_line(lambda j: level[LEV - SPD + first + j, at], count):
            x = first + i
            lanes[x, at] = lanes[x, at] + upwind_square(left, right, sign_of(speed[x, at]))

    def edges(n, _):
        at = pl.ds(pl.multiple_of(OWN - 8 + n * (ny + 8), 8), 8)
        add_x(0, planes, at)
        return _

    def sides(n, _):
        at = pl.ds(pl.multiple_of(OWN + n * 8, 8), 8)
        add_x(0, SPD + 3, at)
        add_x(SPD + nx - 3, SPD + 3, at)
        return _

    lax.fori_loop(0, 2, edges, 0)
    lax.fori_loop(0, rows, sides, 0)


def velocity(
    source, before, after, below, above, order, speed, own_speed, peaks, src, one, two, sem
):
    nx, ny, _ = source.shape
    wide = nx + 2 * SRC
    top = OWN + ny
    rest = wide * 8
    for k in range(nx):
        src[SRC + k, OWN:top] = source[k]
    for k in range(SRC):
        src[k, OWN:top] = before[k]
        src[SRC + nx + k, OWN:top] = after[k]
    for k in range(wide):
        src[k, OWN - 8 : OWN] = below[k * 8 : k * 8 + 8]
        src[k, top : top + 8] = above[k * 8 : k * 8 + 8]
        src[k, OWN - 9 : OWN - 8] = below[rest + k : rest + k + 1]
        src[k, top + 8 : top + 9] = above[rest + k : rest + k + 1]
    coefficients = velocity_polynomial()
    step = (ny + 2 * (SRC - 1)) // 8
    start = OWN - (SRC - 1)

    def sweep(old, new, shift, lo, hi, last, constant):
        def body(x, _):
            lines = {}

            def f(j):
                if j not in lines:
                    lines[j] = strided(old, x, start + j, step)
                return lines[j]

            for t in range(step):
                centre = f(t)
                beside = strided(old, x - 1, start + t, step) + strided(old, x + 1, start + t, step)
                beside = beside + (f(t - 1) + f(t + 1))
                beside = beside + (along_lanes(centre, 1) + along_lanes(centre, -1))
                if last is not None:
                    beside = last * beside
                own = centre if old is src else strided(src, x, start + t, step)
                new[x - shift, pl.ds(start + t, 8, stride=step), :] = beside + constant * own
            return _

        lax.fori_loop(lo, hi, body, 0, unroll=11)

    sweep(src, one, 0, 1, wide - 1, coefficients[4], coefficients[3])
    sweep(one, two, 0, 2, wide - 2, None, coefficients[2])
    sweep(two, one, 0, 3, wide - 3, None, coefficients[1])
    sweep(one, speed, SRC - SPD, 4, wide - 4, None, coefficients[0])

    leaving = pltpu.make_async_copy(
        speed.at[pl.ds(SPD, nx), pl.ds(OWN, ny)], own_speed, sem.at[0]
    )
    leaving.start()

    def largest(x, carry):
        return jnp.maximum(carry, jnp.abs(speed[SPD + x, OWN : OWN + ny]))

    top = lax.fori_loop(0, nx, largest, jnp.zeros((ny, 128), jnp.float32))
    peaks[...] = jnp.broadcast_to(jnp.max(top), peaks.shape)
    leaving.wait()


def evolve(
    own_level, before, after, below, above, speed, upper, lower, peaks, new_level,
    level, rate, lanes, stage, advected, swept, acc, even, odd, result, sems,
):
    nx, ny, _ = new_level.shape
    tall = nx + 2 * LEV
    buffers = (even, odd)
    top = OWN + ny
    for k in range(nx):
        level[LEV + k, OWN:top] = own_level[k]
    for k in range(LEV):
        level[k, OWN:top] = before[k]
        level[LEV + nx + k, OWN:top] = after[k]
    for k in range(tall):
        level[k, OWN - 8 : OWN] = below[k]
        level[k, top : top + 8] = above[k]

    def emit_rate(x, t, value):
        rate[x, pl.ds(OWN - SPD + t, 8, stride=10), :] = value

    other_lanes(level, speed, upper, lower, lanes, buffers)
    weno_rates(level, LEV - SPD, speed, 0, acc, nx + 2 * SPD, OWN - SPD, 10, emit_rate, lanes)

    peak = jnp.max(peaks[...], axis=0, keepdims=True)
    time_step = courant / (peak + 1e-06)
    step_row = jnp.broadcast_to(time_step, (8, 128))
    step_rows = jnp.broadcast_to(time_step, (ROWS - 8, 128))

    def advance(x, _):
        stage[x, 8:ROWS] = level[x + LEV - SPD, 8:ROWS] + step_rows * rate[x, 8:ROWS]
        return _

    lax.fori_loop(0, stage.shape[0], advance, 0)

    start, step = OWN - 2, 9

    def emit(x, t, value):
        row = start + t
        after = strided(stage, x + SPD - 2, row, step) + step_row * value
        before = strided(level, x + LEV - 2, row, step)
        advected[x, pl.ds(row, 8, stride=step), :] = 0.5 * before + 0.5 * after

    weno_rates(stage, SPD - 2, speed, SPD - 2, acc, nx + 4, start, step, emit, None, buffers)

    def emit_one(x, t, value):
        swept[x, pl.ds(OWN - 1 + t, 8, stride=9), :] = value

    reinit_sweep(advected, 1, advected, 1, nx + 2, OWN - 1, 9, emit_one)

    part = nx // PARTS
    leaving = []
    for n in range(PARTS):
        first = n * part

        def emit_two(x, t, value):
            result[first + x, pl.ds(t, 8, stride=ny // 8), :] = value

        reinit_sweep(swept, 1 + first, advected, 2 + first, part, OWN, ny // 8, emit_two)
        planes = pl.ds(first, part)
        leaving.append(
            pltpu.make_async_copy(result.at[planes], new_level.at[planes], sems.at[n])
        )
        leaving[n].start()
    for copy in leaving:
        copy.wait()


PARTS = 4
BIG = 32
VM = pl.BlockSpec(memory_space=pltpu.VMEM)
ANY = pl.BlockSpec(memory_space=pl.ANY)


def call(kernel, outs, scratch, args, megabytes, copies=0):
    ins = [a if isinstance(a, tuple) else (a, VM) for a in args]
    outs = [o if isinstance(o[0], tuple) else (o, VM) for o in outs]
    scratch = [pltpu.VMEM(shape, jnp.float32) for shape in scratch]
    if copies:
        scratch.append(pltpu.SemaphoreType.DMA((copies,)))
    return pl.pallas_call(
        kernel,
        out_shape=[jax.ShapeDtypeStruct(shape, jnp.float32) for shape, _ in outs],
        in_specs=[place for _, place in ins],
        out_specs=[place for _, place in outs],
        scratch_shapes=scratch,
        compiler_params=pltpu.CompilerParams(vmem_limit_bytes=megabytes * 1024 * 1024),
    )(*[array for array, _ in ins])


def local(level_set, stress_jump, materials):
    tile = level_set.shape
    nx, ny, nz = tile
    wide, tall, mid = nx + 2 * SRC, nx + 2 * LEV, nx + 2 * SPD
    size_x, size_y = lax.axis_size("gx"), lax.axis_size("gy")
    devices = size_x * size_y

    def shift(value, axis, size, by):
        return lax.ppermute(value, axis, [(i, (i + by) % size) for i in range(size)])

    low = weigh(stress_jump[:SRC], materials[:SRC])
    high = weigh(stress_jump[nx - SRC :], materials[nx - SRC :])
    source_after = shift(low, "gx", size_x, -1)
    source_before = shift(high, "gx", size_x, 1)
    source = weigh(stress_jump, materials)
    level_low, level_high, _, _ = lax.optimization_barrier(
        (level_set[:LEV], level_set[nx - LEV :], low, high)
    )
    level_after = shift(level_low, "gx", size_x, -1)
    level_before = shift(level_high, "gx", size_x, 1)
    upper, lower = call(
        own_lanes, [tile, tile], [(5, GROUP, 8, nz)] * 2, (level_set, (level_low, ANY), (level_high, ANY)), 8
    )
    message = (wide * 8 + (wide + 7) // 8 * 8, nz)
    low, high = call(
        pack_source, [message, message], [], (source, source_before, source_after, (upper, ANY)), 8
    )
    source_above = shift(low, "gy", size_y, -1)
    source_below = shift(high, "gy", size_y, 1)
    message = (tall, 8, nz)
    low, high = call(
        pack_level,
        [message, message],
        [],
        (level_set, level_before, level_after, (low, ANY)),
        8,
    )
    level_above = shift(low, "gy", size_y, -1)
    level_below = shift(high, "gy", size_y, 1)
    speed, normal_speed, peaks = call(
        velocity,
        [(mid, ROWS, nz), (tile, ANY), (devices, nz)],
        [(wide, ROWS, nz)] * 3,
        (source, source_before, source_after, source_below, source_above, (low, ANY)),
        BIG,
        copies=1,
    )
    peaks, level_above, level_below = lax.optimization_barrier((peaks, level_above, level_below))
    peaks = lax.all_to_all(peaks.reshape(devices, 1, nz), ("gx", "gy"), 0, 0)
    (new_level,) = call(
        evolve,
        [(tile, ANY)],
        [
            (tall, ROWS, nz),
            (mid, ROWS, nz),
            (mid, ROWS, nz),
            (mid, ROWS, nz),
            (nx + 4, ROWS, nz),
            (nx + 2, ROWS, nz),
            (mid, 10, 8, nz),
        ]
        + [(5, GROUP, 8, nz)] * 2
        + [tile],
        (
            level_set,
            level_before,
            level_after,
            level_below,
            level_above,
            speed,
            upper,
            lower,
            peaks.reshape(devices, nz),
        ),
        BIG,
        copies=PARTS,
    )
    return (new_level, normal_speed)


def solution(mesh):
    in_specs = (P("gx", "gy", None), P("gx", "gy", None), P("gx", "gy", None))
    out_specs = (P("gx", "gy", None), P("gx", "gy", None))
    return jax.shard_map(local, mesh=mesh, in_specs=in_specs, out_specs=out_specs, check_vma=False)
```

```python
import jax
import jax.numpy as jnp
import numpy as np
from jax import lax
from jax.experimental import pallas as pl
from jax.experimental.pallas import tpu as pltpu
from jax.sharding import PartitionSpec as P

SWEEPS = 4
REINIT = 2

screening = 0.1
spectral_mid = screening + 6.0
spectral_half = 6.0
courant = 0.25
pseudo_step = 0.25
weno_floor = 1e-06

OWN = 16
ROWS = 96
SRC = 9
LEV = 8
SPD = 5
GROUP = 16
ROW_GROUPS = 6


def velocity_polynomial():
    times = np.array([0.0, 1.0])
    add = np.polynomial.polynomial.polyadd
    mul = np.polynomial.polynomial.polymul
    operator = add([spectral_mid], -times)
    ratio_now = spectral_half / spectral_mid
    iterate, residue, search = np.array([0.0]), np.array([1.0]), np.array([1.0 / spectral_mid])
    for _ in range(SWEEPS):
        applied = mul(operator, search)
        iterate = add(iterate, search)
        residue = add(residue, -applied)
        ratio_next = 1.0 / (2.0 * spectral_mid / spectral_half - ratio_now)
        search = add(ratio_next * ratio_now * search, 2.0 * ratio_next / spectral_half * residue)
        ratio_now = ratio_next
    return [float(c) for c in add(iterate, search)]


def along_lanes(value, k):
    return pltpu.roll(value, (-k) % value.shape[1], axis=1)


def inverse(x):
    return pl.reciprocal(x, approx=True)


def root(x):
    return x * lax.rsqrt(jnp.maximum(x, 1.2e-38))


def smooth_terms(second, second_next, third, scaled, scaled_next):
    twice = third + third
    middle = (third * twice + (1.5 * weno_floor)) + scaled * second_next
    return middle + scaled_next * twice, middle, middle - scaled * twice


def side_ratios(u1, u2, u3, jump_near, jump_far):
    p12 = jnp.square(u1 * u2)
    p13 = jnp.square(u1 * u3)
    p23 = jnp.square(u2 * u3)
    a = p12 * jump_near
    b = p23 * jump_far
    both = a + b
    both = both + both
    base = 3.0 * p13 + 0.5 * (p12 + p23)
    return (both + a) * inverse(base + p12), (both + b) * inverse(base + p23)


def weno_line(f, count):
    values, first, second, third, scaled, terms, jump, ratios = ({} for _ in range(8))

    def need(table, j, make):
        if j not in table:
            table[j] = make(j)
        return table[j]

    def val(j):
        return need(values, j, f)

    def d1(j):
        return need(first, j, lambda k: val(k + 1) - val(k))

    def d2(j):
        return need(second, j, lambda k: d1(k) - d1(k - 1))

    def d3(j):
        return need(third, j, lambda k: d2(k + 1) - d2(k))

    def sc(j):
        return need(scaled, j, lambda k: 1.5 * d2(k))

    def u(j):
        return need(terms, j, lambda k: smooth_terms(d2(k), d2(k + 1), d3(k), sc(k), sc(k + 1)))

    def g(j):
        return need(jump, j, lambda k: d3(k + 1) - d3(k))

    def r(c):
        return need(
            ratios, c, lambda k: side_ratios(u(k - 2)[0], u(k - 1)[1], u(k)[2], g(k - 1), g(k - 2))
        )

    for i in range(count):
        wide = 6.0 * (d1(i) + d1(i - 1))
        left = (wide - (d3(i - 1) + d3(i - 1))) - r(i)[0]
        right = ((d3(i) + d3(i)) - wide) - r(i + 1)[1]
        yield i, left, right


SHIFTS = (-3, -2, -1, 1, 2)


def piped(groups, tiles, load, compute, buffers):
    def fill(buffer, g):
        for j in range(tiles):
            f = load(g, j)
            for n, k in enumerate(SHIFTS):
                buffer[n, j] = along_lanes(f, k)

    fill(buffers[0], 0)

    def body(p, _):
        for parity in range(2):
            g = 2 * p + parity
            fill(buffers[1 - parity], jnp.minimum(g + 1, groups - 1))
            for j in range(tiles):
                cells = {k: buffers[parity][n, j] for n, k in enumerate(SHIFTS)}
                cells[0] = load(g, j)
                compute(g, j, cells)
        return _

    lax.fori_loop(0, groups // 2, body, 0)


def weno_lanes(cells):
    first = {k: cells[k + 1] - cells[k] for k in range(-3, 2)}
    second = {k: first[k] - first[k - 1] for k in range(-2, 2)}
    third = {k: second[k + 1] - second[k] for k in range(-2, 1)}

    def terms(k):
        return smooth_terms(
            second[k], second[k + 1], third[k], 1.5 * second[k], 1.5 * second[k + 1]
        )

    ratio_left, ratio_right = side_ratios(
        terms(-2)[0], terms(-1)[1], terms(0)[2], third[0] - third[-1], third[-1] - third[-2]
    )
    wide = 6.0 * (first[0] + first[-1])
    left = (wide - (third[-1] + third[-1])) - ratio_left
    right = ((third[0] + third[0]) - wide) - along_lanes(ratio_right, 1)
    return left, right


def upwind_square(left, right, sign):
    return jnp.square(jnp.maximum(jnp.maximum(sign * left, sign * right), 0.0))


def sign_of(value):
    return jnp.where(value > 0, 1.0, -1.0)


def strided(ref, x, start, step):
    return ref[x, pl.ds(start, 8, stride=step), :]


def weno_rates(field, fx, speed, sx, acc, planes, start, step, emit, lanes=None, buffers=None):
    def along_x(t, _):
        row = start + t

        def f(j):
            return strided(field, fx + j, row, step)

        for i, left, right in weno_line(f, planes):
            sign = sign_of(strided(speed, sx + i, row, step))
            acc[i, t] = upwind_square(left, right, sign)
        return _

    if lanes is None:
        lax.fori_loop(0, step, along_x, 0)

    def finish(x, t, total):
        velocity = strided(speed, sx + x, start + t, step)
        emit(x, t, velocity * (root(total) * (-1.0 / 12.0)))

    def along_y(x, _):
        lines = {}

        def f(j):
            if j not in lines:
                lines[j] = strided(field, fx + x, start + j, step)
            return lines[j]

        for t, left, right in weno_line(f, step):
            sign = sign_of(strided(speed, sx + x, start + t, step))
            total = upwind_square(left, right, sign)
            finish(x, t, total + strided(lanes, x, start + t, step))
        return _

    def along_yz(p, _):
        for parity in range(2):
            x = 2 * p + parity
            after = jnp.minimum(x + 1, planes - 1)
            for t in range(step):
                g = strided(field, fx + after, start + t, step)
                for n, k in enumerate(SHIFTS):
                    buffers[1 - parity][n, t] = along_lanes(g, k)
            lines = {}

            def f(j):
                if j not in lines:
                    lines[j] = strided(field, fx + x, start + j, step)
                return lines[j]

            for t, left, right in weno_line(f, step):
                sign = sign_of(strided(speed, sx + x, start + t, step))
                total = acc[x, t] + upwind_square(left, right, sign)
                cells = {k: buffers[parity][n, t] for n, k in enumerate(SHIFTS)}
                cells[0] = f(t)
                left, right = weno_lanes(cells)
                finish(x, t, total + upwind_square(left, right, sign))
        return _

    if lanes is None:
        for t in range(step):
            g = strided(field, fx, start + t, step)
            for n, k in enumerate(SHIFTS):
                buffers[0][n, t] = along_lanes(g, k)
        lax.fori_loop(0, planes // 2, along_yz, 0)
    else:
        lax.fori_loop(0, planes, along_y, 0, unroll=3)


def reinit_sweep(field, fx, origin, ox, planes, start, step, emit):
    def body(x, _):
        lines = {}

        def f(j):
            if j not in lines:
                lines[j] = strided(field, fx + x, start + j, step)
            return lines[j]

        for t in range(step):
            row = start + t
            centre = f(t)
            base = strided(origin, ox + x, row, step)
            sign_field = base * lax.rsqrt(base * base + 1.0)
            sign = sign_of(base)
            signed = sign * centre

            def climb(low, high):
                lowest = jnp.minimum(sign * low, sign * high)
                return jnp.square(jnp.maximum(signed - lowest, 0.0))

            total = climb(
                strided(field, fx + x - 1, row, step), strided(field, fx + x + 1, row, step)
            )
            total = total + climb(f(t - 1), f(t + 1))
            total = total + climb(along_lanes(centre, -1), along_lanes(centre, 1))
            emit(x, t, centre - pseudo_step * sign_field * (root(total) - 1.0))
        return _

    lax.fori_loop(0, planes, body, 0, unroll=4)


def weigh(stress, materials):
    weight = jnp.where(materials == 0, 1.0, jnp.where(materials == 1, 0.6, 0.0))
    return weight.astype(jnp.float32) * stress


def pack_source(source, before, after, order, low, high):
    nx, ny, _ = source.shape
    wide = nx + 2 * SRC
    rest = wide * 8
    planes = [before[k] for k in range(SRC)] + [source[k] for k in range(nx)]
    planes = planes + [after[k] for k in range(SRC)]
    for k, plane in enumerate(planes):
        low[k * 8 : k * 8 + 8] = plane[0:8]
        high[k * 8 : k * 8 + 8] = plane[ny - 8 : ny]
        low[rest + k : rest + k + 1] = plane[8:9]
        high[rest + k : rest + k + 1] = plane[ny - 9 : ny - 8]
    tail = low.shape[0] - rest - wide
    low[rest + wide :] = jnp.zeros((tail, 128), jnp.float32)
    high[rest + wide :] = jnp.zeros((tail, 128), jnp.float32)


def pack_level(level, before, after, order, low, high):
    nx, ny, _ = level.shape
    for k in range(nx + 2 * LEV):
        ref, j = (level, k - LEV)
        if k < LEV:
            ref, j = (before, k)
        elif k >= LEV + nx:
            ref, j = (after, k - LEV - nx)
        low[k] = ref[j, 0:8]
        high[k] = ref[j, ny - 8 : ny]


def own_lanes(level, low, high, upper, lower, *buffers):
    nx, ny, _ = level.shape
    rows = ny // 8

    def tile(g, j):
        return g * (GROUP // rows) + j // rows, slice(j % rows * 8, j % rows * 8 + 8)

    def compute(g, j, cells):
        left, right = weno_lanes(cells)
        upper[tile(g, j)] = jnp.square(jnp.maximum(jnp.maximum(left, right), 0.0))
        lower[tile(g, j)] = jnp.square(jnp.minimum(jnp.minimum(left, right), 0.0))

    piped(nx * rows // GROUP, GROUP, lambda g, j: level[tile(g, j)], compute, buffers)

    def inner(n, _):
        at = pl.ds(pl.multiple_of(n * 8, 8), 8)
        for i, left, right in weno_line(lambda j: level[3 + j, at], nx - 6):
            high = jnp.square(jnp.maximum(jnp.maximum(left, right), 0.0))
            low_square = jnp.square(jnp.minimum(jnp.minimum(left, right), 0.0))
            upper[3 + i, at] = upper[3 + i, at] + high
            lower[3 + i, at] = lower[3 + i, at] + low_square
        return _

    lax.fori_loop(0, rows, inner, 0)


def other_lanes(level, speed, upper, lower, lanes, buffers):
    nx, ny, _ = upper.shape
    top = OWN + ny

    def outside(groups, tiles, tile):
        def load(g, j):
            x, row = tile(g, j)
            return level[x + LEV - SPD, row : row + 8]

        def compute(g, j, cells):
            x, row = tile(g, j)
            left, right = weno_lanes(cells)
            sign = sign_of(speed[x, row : row + 8])
            lanes[x, row : row + 8] = upwind_square(left, right, sign)

        piped(groups, tiles, load, compute, buffers)

    planes = nx + 2 * SPD
    outside(ROW_GROUPS, 2 * planes // ROW_GROUPS, lambda g, j: (g * (planes // ROW_GROUPS) + j // 2, (OWN - 8, top)[j % 2]))
    rows = ny // 8
    outside(
        2 * SPD, rows, lambda g, j: (g + jnp.where(g < SPD, 0, nx), OWN + 8 * j)
    )

    def own(x, _):
        positive = speed[SPD + x, OWN:top] > 0
        lanes[SPD + x, OWN:top] = jnp.where(positive, upper[x], lower[x])
        return _

    lax.fori_loop(0, nx, own, 0, unroll=2)

    def add_x(first, count, at):
        for i, left, right in weno_line(lambda j: level[LEV - SPD + first + j, at], count):
            x = first + i
            lanes[x, at] = lanes[x, at] + upwind_square(left, right, sign_of(speed[x, at]))

    def edges(n, _):
        at = pl.ds(pl.multiple_of(OWN - 8 + n * (ny + 8), 8), 8)
        add_x(0, planes, at)
        return _

    def sides(n, _):
        at = pl.ds(pl.multiple_of(OWN + n * 8, 8), 8)
        add_x(0, SPD + 3, at)
        add_x(SPD + nx - 3, SPD + 3, at)
        return _

    lax.fori_loop(0, 2, edges, 0)
    lax.fori_loop(0, rows, sides, 0)


def velocity(
    source, before, after, below, above, order, speed, own_speed, peaks, src, one, two, sem
):
    nx, ny, _ = source.shape
    wide = nx + 2 * SRC
    top = OWN + ny
    rest = wide * 8
    for k in range(nx):
        src[SRC + k, OWN:top] = source[k]
    for k in range(SRC):
        src[k, OWN:top] = before[k]
        src[SRC + nx + k, OWN:top] = after[k]
    for k in range(wide):
        src[k, OWN - 8 : OWN] = below[k * 8 : k * 8 + 8]
        src[k, top : top + 8] = above[k * 8 : k * 8 + 8]
        src[k, OWN - 9 : OWN - 8] = below[rest + k : rest + k + 1]
        src[k, top + 8 : top + 9] = above[rest + k : rest + k + 1]
    coefficients = velocity_polynomial()
    step = (ny + 2 * (SRC - 1)) // 8
    start = OWN - (SRC - 1)

    def sweep(old, new, shift, lo, hi, last, constant):
        def body(x, _):
            lines = {}

            def f(j):
                if j not in lines:
                    lines[j] = strided(old, x, start + j, step)
                return lines[j]

            for t in range(step):
                centre = f(t)
                beside = strided(old, x - 1, start + t, step) + strided(old, x + 1, start + t, step)
                beside = beside + (f(t - 1) + f(t + 1))
                beside = beside + (along_lanes(centre, 1) + along_lanes(centre, -1))
                if last is not None:
                    beside = last * beside
                own = centre if old is src else strided(src, x, start + t, step)
                new[x - shift, pl.ds(start + t, 8, stride=step), :] = beside + constant * own
            return _

        unroll = min(range(14, 8, -1), key=lambda u: (hi - lo) % u)
        lax.fori_loop(lo, hi, body, 0, unroll=unroll)

    sweep(src, one, 0, 1, wide - 1, coefficients[4], coefficients[3])
    sweep(one, two, 0, 2, wide - 2, None, coefficients[2])
    sweep(two, one, 0, 3, wide - 3, None, coefficients[1])
    sweep(one, speed, SRC - SPD, 4, wide - 4, None, coefficients[0])

    leaving = pltpu.make_async_copy(
        speed.at[pl.ds(SPD, nx), pl.ds(OWN, ny)], own_speed, sem.at[0]
    )
    leaving.start()

    def largest(x, carry):
        return jnp.maximum(carry, jnp.abs(speed[SPD + x, OWN : OWN + ny]))

    top = lax.fori_loop(0, nx, largest, jnp.zeros((ny, 128), jnp.float32))
    peaks[...] = jnp.broadcast_to(jnp.max(top), peaks.shape)
    leaving.wait()


def evolve(
    own_level, before, after, below, above, speed, upper, lower, peaks, new_level,
    level, rate, lanes, stage, advected, swept, acc, even, odd, result, sems,
):
    nx, ny, _ = new_level.shape
    tall = nx + 2 * LEV
    buffers = (even, odd)
    top = OWN + ny
    for k in range(nx):
        level[LEV + k, OWN:top] = own_level[k]
    for k in range(LEV):
        level[k, OWN:top] = before[k]
        level[LEV + nx + k, OWN:top] = after[k]
    for k in range(tall):
        level[k, OWN - 8 : OWN] = below[k]
        level[k, top : top + 8] = above[k]

    def emit_rate(x, t, value):
        rate[x, pl.ds(OWN - SPD + t, 8, stride=10), :] = value

    other_lanes(level, speed, upper, lower, lanes, buffers)
    weno_rates(level, LEV - SPD, speed, 0, acc, nx + 2 * SPD, OWN - SPD, 10, emit_rate, lanes)

    peak = jnp.max(peaks[...], axis=0, keepdims=True)
    time_step = courant / (peak + 1e-06)
    step_row = jnp.broadcast_to(time_step, (8, 128))
    step_rows = jnp.broadcast_to(time_step, (ROWS - 8, 128))

    def advance(x, _):
        stage[x, 8:ROWS] = level[x + LEV - SPD, 8:ROWS] + step_rows * rate[x, 8:ROWS]
        return _

    lax.fori_loop(0, stage.shape[0], advance, 0)

    start, step = OWN - 2, 9

    def emit(x, t, value):
        row = start + t
        after = strided(stage, x + SPD - 2, row, step) + step_row * value
        before = strided(level, x + LEV - 2, row, step)
        advected[x, pl.ds(row, 8, stride=step), :] = 0.5 * before + 0.5 * after

    weno_rates(stage, SPD - 2, speed, SPD - 2, acc, nx + 4, start, step, emit, None, buffers)

    def emit_one(x, t, value):
        swept[x, pl.ds(OWN - 1 + t, 8, stride=9), :] = value

    reinit_sweep(advected, 1, advected, 1, nx + 2, OWN - 1, 9, emit_one)

    part = nx // PARTS
    leaving = []
    for n in range(PARTS):
        first = n * part

        def emit_two(x, t, value):
            result[first + x, pl.ds(t, 8, stride=ny // 8), :] = value

        reinit_sweep(swept, 1 + first, advected, 2 + first, part, OWN, ny // 8, emit_two)
        planes = pl.ds(first, part)
        leaving.append(
            pltpu.make_async_copy(result.at[planes], new_level.at[planes], sems.at[n])
        )
        leaving[n].start()
    for copy in leaving:
        copy.wait()


PARTS = 4
BIG = 32
VM = pl.BlockSpec(memory_space=pltpu.VMEM)
ANY = pl.BlockSpec(memory_space=pl.ANY)


def call(kernel, outs, scratch, args, megabytes, copies=0):
    ins = [a if isinstance(a, tuple) else (a, VM) for a in args]
    outs = [o if isinstance(o[0], tuple) else (o, VM) for o in outs]
    scratch = [pltpu.VMEM(shape, jnp.float32) for shape in scratch]
    if copies:
        scratch.append(pltpu.SemaphoreType.DMA((copies,)))
    return pl.pallas_call(
        kernel,
        out_shape=[jax.ShapeDtypeStruct(shape, jnp.float32) for shape, _ in outs],
        in_specs=[place for _, place in ins],
        out_specs=[place for _, place in outs],
        scratch_shapes=scratch,
        compiler_params=pltpu.CompilerParams(vmem_limit_bytes=megabytes * 1024 * 1024),
    )(*[array for array, _ in ins])


def local(level_set, stress_jump, materials):
    tile = level_set.shape
    nx, ny, nz = tile
    wide, tall, mid = nx + 2 * SRC, nx + 2 * LEV, nx + 2 * SPD
    size_x, size_y = lax.axis_size("gx"), lax.axis_size("gy")
    devices = size_x * size_y

    def shift(value, axis, size, by):
        return lax.ppermute(value, axis, [(i, (i + by) % size) for i in range(size)])

    low = weigh(stress_jump[:SRC], materials[:SRC])
    high = weigh(stress_jump[nx - SRC :], materials[nx - SRC :])
    source_after = shift(low, "gx", size_x, -1)
    source_before = shift(high, "gx", size_x, 1)
    source = weigh(stress_jump, materials)
    level_low, level_high, _, _ = lax.optimization_barrier(
        (level_set[:LEV], level_set[nx - LEV :], low, high)
    )
    level_after = shift(level_low, "gx", size_x, -1)
    level_before = shift(level_high, "gx", size_x, 1)
    upper, lower = call(
        own_lanes, [tile, tile], [(5, GROUP, 8, nz)] * 2, (level_set, (level_low, ANY), (level_high, ANY)), 8
    )
    message = (wide * 8 + (wide + 7) // 8 * 8, nz)
    low, high = call(
        pack_source, [message, message], [], (source, source_before, source_after, (upper, ANY)), 8
    )
    source_above = shift(low, "gy", size_y, -1)
    source_below = shift(high, "gy", size_y, 1)
    message = (tall, 8, nz)
    low, high = call(
        pack_level,
        [message, message],
        [],
        (level_set, level_before, level_after, (low, ANY)),
        8,
    )
    level_above = shift(low, "gy", size_y, -1)
    level_below = shift(high, "gy", size_y, 1)
    speed, normal_speed, peaks = call(
        velocity,
        [(mid, ROWS, nz), (tile, ANY), (devices, nz)],
        [(wide, ROWS, nz)] * 3,
        (source, source_before, source_after, source_below, source_above, (low, ANY)),
        BIG,
        copies=1,
    )
    peaks, level_above, level_below = lax.optimization_barrier((peaks, level_above, level_below))
    peaks = lax.all_to_all(peaks.reshape(devices, 1, nz), ("gx", "gy"), 0, 0)
    (new_level,) = call(
        evolve,
        [(tile, ANY)],
        [
            (tall, ROWS, nz),
            (mid, ROWS, nz),
            (mid, ROWS, nz),
            (mid, ROWS, nz),
            (nx + 4, ROWS, nz),
            (nx + 2, ROWS, nz),
            (mid, 10, 8, nz),
        ]
        + [(5, GROUP, 8, nz)] * 2
        + [tile],
        (
            level_set,
            level_before,
            level_after,
            level_below,
            level_above,
            speed,
            upper,
            lower,
            peaks.reshape(devices, nz),
        ),
        BIG,
        copies=PARTS,
    )
    return (new_level, normal_speed)


def solution(mesh):
    in_specs = (P("gx", "gy", None), P("gx", "gy", None), P("gx", "gy", None))
    out_specs = (P("gx", "gy", None), P("gx", "gy", None))
    return jax.shard_map(local, mesh=mesh, in_specs=in_specs, out_specs=out_specs, check_vma=False)
```
